128 devices in a mesh: gx: 8 (over x, core), gy: 4 (over y), gz: 4 (over z).
Axes of the slice: x: 4, y: 4, z: 4, core: 2. Of those that a mesh axis runs over, the one named last changes fastest.
Arguments:
- source: float32 [128, 128, 512], P('gx', 'gy', 'gz'), may hold values from -24 to 24
- conductivity: float32 [128, 128, 512], P('gx', 'gy', 'gz'), may hold values from 0.5 to 8
Outputs:
- correction: float32 [128, 128, 512], P('gx', 'gy', 'gz')
The draws below stay inside these ranges and needn't reach their ends.
All inputs are finite; a program needn't handle non-finite values.
Results may differ from the reference program's by a relative error of at most 0.0001.
Values sent between devices are 32-bit elements; how exact they have to be, the bound alone decides.
A program may use at most 128 MiB of HBM per device.

```python
import math
import jax
import jax.numpy as jnp
from jax import lax

SWEEPS = 6
COARSE_SWEEPS = 16
NX = 128
NY = 128
NZ = 512


def steps_of(stream_key, extent, shards, least, top_value):
    loudness = 1.0
    for axis_at, blocks in shards:
        draws = jax.random.uniform(jax.random.fold_in(jax.random.fold_in(stream_key, 6), axis_at), (blocks,), jnp.float32, least / len(shards), top_value / len(shards))
        loudness = loudness * jnp.repeat(jnp.exp(draws), extent[axis_at] // blocks).reshape((-1,) + (1,) * (len(extent) - 1 - axis_at))
    return loudness


def normal_values(stream_key, dims, deviation, limit, pieces=(), held_as=jnp.bfloat16):
    gain = steps_of(stream_key, dims, pieces, -0.22, 0.18) if pieces else 1.0
    values = jax.random.normal(stream_key, dims, jnp.float32) * deviation * gain
    return jnp.minimum(jnp.maximum(values, -limit), limit).astype(held_as)


def setup_inputs(seed: int = 0) -> dict:
    seeds = jax.random.split(jax.random.key(seed), 3)
    return {
        "source": normal_values(seeds[0], (NX, NY, NZ), 4.0, 24.0, ((0, 8), (1, 4), (2, 4)), jnp.float32),
        "conductivity": jnp.clip(jnp.exp(math.log(8.0) - 2.7725887 * jax.random.uniform(seeds[1], (NX, NY, NZ), jnp.float32) ** steps_of(seeds[1], (NX, NY, NZ), ((0, 8), (1, 4), (2, 4)), -0.2, 0.2)), 0.5, 8.0),
    }


DAMPING = 0.8


def centre(padded):
    return padded[1:-1, 1:-1, 1:-1]


def neighbours(padded):
    return [padded[2:, 1:-1, 1:-1], padded[:-2, 1:-1, 1:-1], padded[1:-1, 2:, 1:-1],
            padded[1:-1, :-2, 1:-1], padded[1:-1, 1:-1, 2:], padded[1:-1, 1:-1, :-2]]


def zero_pad(field):
    return jnp.pad(field, 1)


def stencil(field_pad, coef_pad, weight):
    middle = centre(field_pad)
    coef_mid = centre(coef_pad)
    total = jnp.zeros_like(middle)
    for field_near, coef_near in zip(neighbours(field_pad), neighbours(coef_pad)):
        total = total + 0.5 * (coef_mid + coef_near) * (middle - field_near)
    return weight * total


def diagonal(coef_pad, weight):
    coef_mid = centre(coef_pad)
    total = jnp.zeros_like(coef_mid)
    for coef_near in neighbours(coef_pad):
        total = total + 0.5 * (coef_mid + coef_near)
    return weight * total


def restrict(field):
    shape = field.shape
    blocks = field.reshape(shape[0] // 2, 2, shape[1] // 2, 2, shape[2] // 2, 2)
    return blocks.mean(axis=(1, 3, 5))


def prolong(field):
    return jnp.repeat(jnp.repeat(jnp.repeat(field, 2, 0), 2, 1), 2, 2)


def jacobi(field, rhs_level, coef_pad, diag_terms, weight, padder):
    return field + DAMPING * (rhs_level - stencil(padder(field), coef_pad, weight)) / diag_terms


def reference(source, conductivity):
    rhs_level = source
    coef_level = conductivity
    saved = []
    for level_index in range(4):
        weight = 0.25 ** level_index
        coef_pad = zero_pad(coef_level)
        diag_terms = diagonal(coef_pad, weight)
        field = jnp.zeros_like(rhs_level)
        for sweep_index in range(SWEEPS):
            field = jacobi(field, rhs_level, coef_pad, diag_terms, weight, zero_pad)
        residual = rhs_level - stencil(zero_pad(field), coef_pad, weight)
        saved.append((field, rhs_level, coef_pad, diag_terms, weight))
        rhs_level = restrict(residual)
        coef_level = restrict(coef_level)
    weight = 0.25 ** 4
    coef_pad = zero_pad(coef_level)
    diag_terms = diagonal(coef_pad, weight)

    def coarse_step(count, field):
        return jacobi(field, rhs_level, coef_pad, diag_terms, weight, zero_pad)

    result = lax.fori_loop(0, COARSE_SWEEPS, coarse_step, jnp.zeros_like(rhs_level))
    for level_index in (3, 2, 1, 0):
        field, rhs_here, coef_pad, diag_terms, weight = saved[level_index]
        field = field + prolong(result)
        for sweep_index in range(SWEEPS):
            field = jacobi(field, rhs_here, coef_pad, diag_terms, weight, zero_pad)
        result = field
    return result
```

```python
import jax
import jax.numpy as jnp
from jax import lax
from jax.experimental import pallas as pl
from jax.experimental.pallas import tpu as pltpu
from jax.sharding import PartitionSpec as P

MESH = pl.DeviceIdType.MESH
F32 = jnp.float32
HI = lax.Precision.HIGHEST
DAMPING = 0.8

KF, BF, VF = 0, 1, 2
NEAR = [(a, b, c) for a in (-1, 0, 1) for b in (-1, 0, 1) for c in (-1, 0, 1) if (a, b, c) != (0, 0, 0)]
PLANE = [(0, b, c) for b in range(4) for c in range(4) if (b, c) != (0, 0)]
LINE = [(a, 0, 0) for a in range(1, 8)]
PEERS = sorted({(a % 8, b % 4, c % 4) for a, b, c in NEAR + PLANE + LINE})


def iota(shape, dim):
    return lax.broadcasted_iota(jnp.int32, shape, dim)


def roll(v, amount, axis):
    shape = v.shape
    if axis == -1:
        return pltpu.roll(v.reshape(-1, 128), amount % 128, 1).reshape(shape)
    return pltpu.roll(v.reshape(-1, 8, 128), amount % 8, 1).reshape(shape)


def shifted(v, axis, step, edge):
    n = v.shape[axis]
    if n == 1:
        return edge
    if step > 0:
        return jnp.concatenate([lax.slice_in_dim(v, 1, n, axis=axis), edge], axis=axis)
    return jnp.concatenate([edge, lax.slice_in_dim(v, 0, n - 1, axis=axis)], axis=axis)


def up(v):
    return jnp.concatenate([v[1:], roll(v[:1], -1, -2)], axis=0)


def down(v):
    return jnp.concatenate([roll(v[-1:], 1, -2), v[:-1]], axis=0)


def dot(a, b):
    return jnp.dot(a, b, precision=HI, preferred_element_type=F32)


def kernel(
    src_hbm, cond_hbm, out_ref,
    raw, D0, Z0s, Z0r, K0, CX0, CY0, CZ0, S0, B0, V0, W0, T0,
    D1, Z1s, Z1r, K1, CX1, CY1, CZ1, S1, B1, V1, W1, T1, T2, F0, F1,
    P2s, R2, G2, H2, K2, V2, A2, S2, I2, Q2, K3, V3, A3, S3, I3, Q3, K4, A4, S4, Q4,
    raw_sem, s0s, s0r, s1s, s1r, xs, xr, g1s, g1r, g2s, g2r,
):
    ix, iy, iz = lax.axis_index("gx"), lax.axis_index("gy"), lax.axis_index("gz")
    lane = iota((8, 128), 1)
    row = iota((8, 128), 0)

    def at(offset):
        a, b, c = offset
        return (lax.rem(ix + (a + 8), 8), lax.rem(iy + (b + 4), 4), lax.rem(iz + (c + 4), 4))

    def remote(src, dst, send, recv, offset):
        return pltpu.make_async_remote_copy(
            src_ref=src, dst_ref=dst, send_sem=send, recv_sem=recv, device_id=at(offset), device_id_type=MESH)

    loads = [pltpu.make_async_copy(cond_hbm, raw.at[0], raw_sem.at[0]),
             pltpu.make_async_copy(src_hbm, raw.at[1], raw_sem.at[1])]
    for c in loads:
        c.start()
    barrier = pltpu.get_barrier_semaphore()
    for offset in PEERS:
        pl.semaphore_signal(barrier, inc=1, device_id=at(offset), device_id_type=MESH)

    def copies0(f):
        count = 7 if f == KF else 6
        made = []
        for n, (dx, dy, dz) in enumerate(NEAR):
            sx, tx, cx = {0: (8, 8, 16), -1: (8, 24, count), 1: (24 - count, 8 - count, count)}[dx]
            sr, tr, cr = {0: (8, 8, 32), -1: (8, 40, 8), 1: (32, 0, 8)}[dy]
            if dz == 0:
                src = D0.at[f, pl.ds(sx, cx), pl.ds(sr, cr)]
                dst = D0.at[f, pl.ds(tx, cx), pl.ds(tr, cr)]
            else:
                side = 0 if dz == -1 else 1
                sh, th, ch = {0: (0, 1, 2), -1: (0, 3, 1), 1: (1, 0, 1)}[dx]
                src = Z0s.at[f, pl.ds(sh, ch), pl.ds(sr - 8, cr)]
                dst = Z0r.at[f, side, pl.ds(th, ch), pl.ds(tr, cr)]
            made.append(remote(src, dst, s0s.at[f * 26 + n], s0r.at[f * 26 + n], (dx, dy, dz)))
        return made

    def copies1(f):
        made = []
        for n, (dx, dy, dz) in enumerate(NEAR):
            if f == BF:
                sr, tr, cr = {0: (16, 16, 16), -1: (16, 32, 8), 1: (24, 8, 8)}[dy]
            else:
                sr, tr, cr = {0: (16, 16, 16), -1: (16, 32, 16), 1: (16, 0, 16)}[dy]
            if dz == 0:
                src = D1.at[f, 1, :, pl.ds(sr, cr)]
                dst = D1.at[f, 1 - dx, :, pl.ds(tr, cr)]
            else:
                side = 0 if dz == -1 else 1
                src = Z1s.at[f, :, pl.ds(sr - 16, cr)]
                dst = Z1r.at[f, side, 1 - dx, :, pl.ds(tr, cr)]
            made.append(remote(src, dst, s1s.at[f * 26 + n], s1r.at[f * 26 + n], (dx, dy, dz)))
        return made

    def copies_far(ref, f):
        return [remote(ref.at[8], ref.at[0], xs.at[2 * f], xr.at[2 * f], (1, 0, 0)),
                remote(ref.at[17], ref.at[25], xs.at[2 * f + 1], xr.at[2 * f + 1], (-1, 0, 0))]

    here = iy * 4 + iz

    def copies_plane(f):
        return [remote(P2s.at[f], R2.at[f, here], g1s.at[f * 15 + n], g1r.at[f * 15 + n], o)
                for n, o in enumerate(PLANE)]

    slab = pl.ds(pl.multiple_of(ix * 128, 128), 128)

    def copies_line(f):
        return [remote(G2.at[f, slab], G2.at[f, slab], g2s.at[f * 7 + n], g2r.at[f * 7 + n], o)
                for n, o in enumerate(LINE)]

    def start(made):
        for c in made:
            c.start()

    def wait_recv(made):
        for c in made:
            c.wait_recv()

    def wait_send(made):
        for c in made:
            c.wait_send()

    cc, ll = iota((128, 128), 0), iota((128, 128), 1)
    split = (cc == jnp.where(ll < 64, 2 * ll, 2 * (ll - 64) + 1)).astype(F32)
    lane32 = iota((32, 128), 1)
    lane16 = iota((16, 128), 1)

    def permute_in(f):
        def body(i, _):
            x = raw[f, pl.ds(i * 4, 4)].reshape(128, 128)
            D0[f, pl.ds(8 + i * 4, 4), 8:40, :] = dot(x, split).reshape(4, 32, 128)
            return 0
        lax.fori_loop(0, 4, body, 0)

    even_strip = (lane32 < 4) | ((lane32 >= 60) & (lane32 < 64))
    odd_strip = ((lane32 >= 64) & (lane32 < 68)) | (lane32 >= 124)

    def pack0(f):
        for h in range(2):
            total = None
            for xi in range(8):
                d = D0[f, 8 + 8 * h + xi, 8:40, :]
                part = (pltpu.roll(jnp.where(even_strip, d, 0.0), (16 * xi) % 128, 1)
                        + pltpu.roll(jnp.where(odd_strip, d, 0.0), (16 * xi + 72) % 128, 1))
                total = part if total is None else total + part
            Z0s[f, h] = total

    ring0 = (lane < 64) | ((lane < 68) & (iz < 3)) | ((lane >= 124) & (iz > 0))
    even4 = lax.rem(lax.div(lane, 4), 2) == 0

    def assemble0(f, dst):
        def body(t, _):
            xh, j = lax.div(t, 6), lax.rem(t, 6)
            rows = pl.ds(j, 8, stride=6)
            c = jnp.where(even4, Z0r[f, 0, xh, rows, :], Z0r[f, 1, xh, rows, :])
            mask = ring0
            if f == KF:
                y = row * 6 + j + (iy * 32 - 8)
                xb = ix * 2 + xh - 1
                mask = mask & (y >= 0) & (y < 128) & (xb >= 0) & (xb < 16)
            for xi in range(8):
                x = xh * 8 + xi
                d = D0[f, x, rows, :]
                full = mask
                if f == KF and xi in (0, 7):
                    full = mask & (x > 0) & (x < 31)
                for p in range(2):
                    main = d if p == 0 else pltpu.roll(d, 64, 1)
                    halo = pltpu.roll(c, (64 - 16 * xi - 8 * p) % 128, 1)
                    dst[x, p, j] = jnp.where(full, jnp.where(lane < 64, main, halo), 0.0)
            return 0
        lax.fori_loop(0, 24, body, 0)

    def coefs0():
        def body(x, lower):
            ke, ko, ne, no = K0[x, 0], K0[x, 1], K0[x + 1, 0], K0[x + 1, 1]
            xe, xo = 0.5 * (ke + ne), 0.5 * (ko + no)
            ye, yo = 0.5 * (ke + up(ke)), 0.5 * (ko + up(ko))
            ze, zo = 0.5 * (ke + ko), 0.5 * (ko + roll(ke, -1, -1))
            de = xe + lower[0] + ye + down(ye) + ze + roll(zo, 1, -1)
            do = xo + lower[1] + yo + down(yo) + zo + ze
            CX0[x, 0], CX0[x, 1] = xe, xo
            CY0[x, 0], CY0[x, 1] = ye, yo
            CZ0[x, 0], CZ0[x, 1] = ze, zo
            S0[x, 0] = jnp.where(ke > 0, DAMPING / de, 0.0)
            S0[x, 1] = jnp.where(ko > 0, DAMPING / do, 0.0)
            return xe, xo
        lax.fori_loop(1, 30, body, (0.5 * K0[1, 0], 0.5 * K0[1, 1]))

    def flow0(x, c, n, low):
        ce, co = c
        fe, fo = CX0[x, 0] * (n[0] - ce), CX0[x, 1] * (n[1] - co)
        ye, yo = CY0[x, 0] * (up(ce) - ce), CY0[x, 1] * (up(co) - co)
        ze, zo = CZ0[x, 0] * (co - ce), CZ0[x, 1] * (roll(ce, -1, -1) - co)
        re = B0[x, 0] + ((fe - low[0]) + (ye - down(ye)) + (ze - roll(zo, 1, -1)))
        ro = B0[x, 1] + ((fo - low[1]) + (yo - down(yo)) + (zo - ze))
        return (re, ro), (fe, fo)

    def pair0(x):
        return V0[x, 0], V0[x, 1]

    def first0(x):
        c, n = pair0(x - 1), pair0(x)
        return CX0[x - 1, 0] * (n[0] - c[0]), CX0[x - 1, 1] * (n[1] - c[1])

    def sweeps0(count):
        def sweep(i, _):
            lo = 3 + i
            def body(q, carry):
                c, low = carry
                for u in range(2):
                    x = lo + 2 * q + u
                    n = pair0(x + 1)
                    r, low = flow0(x, c, n, low)
                    V0[x, 0] = c[0] + S0[x, 0] * r[0]
                    V0[x, 1] = c[1] + S0[x, 1] * r[1]
                    c = n
                return c, low
            lax.fori_loop(0, 13 - i, body, (pair0(lo), first0(lo)))
            return 0
        lax.fori_loop(0, count, sweep, 0)

    def restrict_k1():
        def body(i, _):
            for t in range(2):
                parts = []
                for base in (8, 16):
                    x = base + 2 * i
                    a = None
                    for u in range(2):
                        for o in range(2):
                            d = D0[KF, x + u, pl.ds(8 + 16 * t + o, 8, stride=2), :]
                            a = d if a is None else a + d
                    parts.append((a + pltpu.roll(a, 64, 1)) * 0.125)
                D1[KF, 1, i, 16 + 8 * t:24 + 8 * t, :] = jnp.where(lane < 64, parts[0], parts[1])
            return 0
        lax.fori_loop(0, 4, body, 0)

    def restrict_b1():
        def coarse(x):
            total = None
            low = first0(x)
            c = pair0(x)
            for u in range(2):
                n = pair0(x + u + 1)
                r, low = flow0(x + u, c, n, low)
                c = n
                part = r[0] + r[1]
                total = part if total is None else total + part
            return [(total[2 * m] + total[2 * m + 1]) * 0.125 for m in range(3)]
        def body(i, _):
            a, b = coarse(8 + 2 * i), coarse(16 + 2 * i)
            for m in range(3):
                T1[i, pl.ds(4 + m, 8, stride=3), :] = jnp.where(lane < 64, a[m], pltpu.roll(b[m], 64, 1))
            return 0
        lax.fori_loop(0, 4, body, 0)
        D1[BF, 1, :, 16:32, :] = T1[:, 8:24, :]

    low_strip = (lane16 < 16) | ((lane16 >= 48) & (lane16 < 64))
    high_strip = ((lane16 >= 64) & (lane16 < 80)) | (lane16 >= 112)

    def pack1(f):
        for h, strip in ((0, low_strip), (1, high_strip)):
            total = None
            for u in range(4):
                d = D1[f, 1, u, 16:32, :]
                part = pltpu.roll(jnp.where(strip, d, 0.0), (64 * h + 32 * u) % 128, 1)
                total = part if total is None else total + part
            Z1s[f, h] = total

    ring1 = (lane < 64) | ((lane < 80) & (iz < 3)) | ((lane >= 112) & (iz > 0))
    even16 = lax.rem(lax.div(lane, 16), 2) == 0

    def assemble1(f, dst):
        def body(t, _):
            g, j = lax.div(t, 5), lax.rem(t, 5)
            rows = pl.ds(4 + j, 8, stride=5)
            c = [jnp.where(even16, Z1r[f, 0, g, h, rows, :], Z1r[f, 1, g, h, rows, :]) for h in range(2)]
            mask = ring1
            if f == KF:
                y = row * 5 + j + (iy * 16 - 12)
                xb = ix + g - 1
                mask = mask & (y >= 0) & (y < 64) & (xb >= 0) & (xb < 8)
            for xl in range(8):
                d = D1[f, g, xl % 4, rows, :]
                main = d if xl < 4 else pltpu.roll(d, 64, 1)
                halo = pltpu.roll(c[xl // 4], (64 - 32 * (xl % 4)) % 128, 1)
                dst[1 + g * 8 + xl, j] = jnp.where(mask, jnp.where(lane < 64, main, halo), 0.0)
            return 0
        lax.fori_loop(0, 15, body, 0)

    HW1 = 0.5 * 0.25

    def coefs1():
        def body(q, lower):
            for u in range(2):
                x = 1 + 2 * q + u
                k, n = K1[x], K1[x + 1]
                cx, cy, cz = HW1 * (k + n), HW1 * (k + up(k)), HW1 * (k + roll(k, -1, -1))
                d = cx + lower + cy + down(cy) + cz + roll(cz, 1, -1)
                CX1[x], CY1[x], CZ1[x] = cx, cy, cz
                S1[x] = jnp.where(k > 0, DAMPING / d, 0.0)
                lower = cx
            return lower
        c0 = HW1 * (K1[0] + K1[1])
        CX1[0] = c0
        lax.fori_loop(0, 12, body, c0)

    def flow1(x, c, n, low):
        f = CX1[x] * (n - c)
        y = CY1[x] * (up(c) - c)
        z = CZ1[x] * (roll(c, -1, -1) - c)
        return B1[x] + ((f - low) + (y - down(y)) + (z - roll(z, 1, -1))), f

    def sweeps1(lo0, pairs0, count):
        def sweep(i, _):
            lo = lo0 + i
            def body(q, carry):
                c, low = carry
                for u in range(2):
                    x = lo + 2 * q + u
                    n = V1[x + 1]
                    r, low = flow1(x, c, n, low)
                    V1[x] = c + S1[x] * r
                    c = n
                return c, low
            c = V1[lo]
            lax.fori_loop(0, pairs0 - i, body, (c, CX1[lo - 1] * (c - V1[lo - 1])))
            return 0
        lax.fori_loop(0, count, sweep, 0)

    def pick(xl):
        q = lax.rem(ll, 32)
        z = lax.rem(q, 8) * 4 + lax.div(q, 8)
        return ((lax.div(ll, 32) == xl) & (lax.div(cc, 2) == z)).astype(F32)

    picks = [pick(xl) for xl in range(4)]

    def pack_k2():
        total = None
        for h in range(2):
            a = None
            for u in range(2):
                for o in range(2):
                    d = D1[KF, 1, 2 * h + u, pl.ds(16 + o, 8, stride=2), :]
                    a = d if a is None else a + d
            a = a * 0.125
            part = dot(a, picks[h]) + dot(pltpu.roll(a, 64, 1), picks[2 + h])
            total = part if total is None else total + part
        P2s[KF] = total
        R2[KF, here] = total

    def pack_b2():
        for xl in range(4):
            x = 9 + 2 * xl
            total = None
            c = V1[x]
            low = CX1[x - 1] * (c - V1[x - 1])
            for u in range(2):
                n = V1[x + u + 1]
                r, low = flow1(x + u, c, n, low)
                c = n
                total = r if total is None else total + r
            for j in range(5):
                T2[xl, pl.ds(j, 8, stride=5), :] = total[j]
        total = None
        for xl in range(4):
            a = (T2[xl, pl.ds(12, 8, stride=2), :] + T2[xl, pl.ds(13, 8, stride=2), :]) * 0.125
            part = dot(a, picks[xl])
            total = part if total is None else total + part
        P2s[BF] = total
        R2[BF, here] = total

    def spread(f):
        v = [R2[f, g] for g in range(16)]
        for bit in (1, 2, 4, 8):
            clear = lax.rem(lax.div(lane, 8 * bit), 2) == 0
            for r in range(16):
                if r & bit:
                    continue
                a, d = v[r], v[r | bit]
                v[r] = jnp.where(clear, a, pltpu.roll(d, 8 * bit, 1))
                v[r | bit] = jnp.where(clear, pltpu.roll(a, 128 - 8 * bit, 1), d)
        for q in range(16):
            G2[f, pl.ds(pl.multiple_of(ix * 128 + q * 8, 8), 8), :] = v[q]

    def gathered(f, yl):
        rows = []
        for xl in range(4):
            rows.append(jnp.stack([G2[f, pl.ds((xl * 4 + zl) * 8 + yl, 8, stride=128), :] for zl in range(4)], 0))
        return jnp.stack(rows, 0)

    def edges(ref, ny):
        ref[0] = jnp.where(lane >= 32, roll(ref[ny], 32, -1), 0.0)
        ref[ny + 1] = jnp.where(lane < 96, roll(ref[1], -32, -1), 0.0)

    def around(v):
        xp = shifted(v, 0, 1, roll(v[:1], -1, -2))
        xm = shifted(v, 0, -1, roll(v[-1:], 1, -2))
        zp = shifted(v, 1, 1, roll(v[:, :1], -1, -1))
        zm = shifted(v, 1, -1, roll(v[:, -1:], 1, -1))
        return xp, xm, zp, zm

    z_top, z_end = lax.rem(lane, 32) == 31, lax.rem(lane, 32) == 0

    def inside(k):
        xp = shifted(k, 0, 1, jnp.where(row == 7, 0.0, roll(k[:1], -1, -2)))
        xm = shifted(k, 0, -1, jnp.where(row == 0, 0.0, roll(k[-1:], 1, -2)))
        zp = shifted(k, 1, 1, jnp.where(z_top, 0.0, roll(k[:, :1], -1, -1)))
        zm = shifted(k, 1, -1, jnp.where(z_end, 0.0, roll(k[:, -1:], 1, -1)))
        return xp, xm, zp, zm

    def coefs_low(level, K, A, S, I, ny):
        hw = 0.5 * 0.25 ** level
        edges(K, ny)
        def body(y, _):
            k = K[y + 1]
            near = inside(k) + (K[y + 2], K[y])
            c = [hw * (k + n) for n in near]
            d = ((c[0] + c[1]) + (c[2] + c[3])) + (c[4] + c[5])
            s = DAMPING / d
            S[y] = s
            if I is not None:
                I[y] = d * (1.0 / DAMPING)
            for m in range(6):
                A[m, y] = jnp.where(near[m] > 0, s * c[m], 0.0)
            return 0
        lax.fori_loop(0, ny, body, 0)

    def fold(blocks):
        t = blocks[0] + blocks[1]
        t = t.reshape((t.shape[0] // 2, 2) + t.shape[1:])
        t = t[:, 0] + t[:, 1]
        t = t.reshape((t.shape[0], t.shape[1] // 2, 2) + t.shape[2:])
        return (t[:, :, 0] + t[:, :, 1]) * 0.125

    def load_k2():
        def body(y, _):
            K2[y + 1] = gathered(KF, y)
            return 0
        lax.fori_loop(0, 8, body, 0)
        coefs_low(2, K2, A2, S2, I2, 8)
        def body3(y, _):
            K3[y + 1] = fold([K2[2 * y + 1], K2[2 * y + 2]])
            return 0
        lax.fori_loop(0, 4, body3, 0)
        coefs_low(3, K3, A3, S3, I3, 4)
        for y in range(2):
            K4[y + 1] = fold([K3[2 * y + 1], K3[2 * y + 2]])
        coefs_low(4, K4, A4, S4, None, 2)

    def next2(y, cur, before, after):
        xp, xm, zp, zm = around(cur)
        t = 0.2 * cur + Q2[y]
        t = t + A2[0, y] * xp + A2[1, y] * xm
        t = t + A2[2, y] * zp + A2[3, y] * zm
        return t + (A2[4, y] * after + A2[5, y] * before)

    def sweeps2(count):
        def sweep(i, _):
            edges(V2, 8)
            def body(y, before):
                cur = V2[y + 1]
                V2[y + 1] = next2(y, cur, before, V2[y + 2])
                return cur
            lax.fori_loop(0, 8, body, V2[0])
            return 0
        lax.fori_loop(0, count, sweep, 0)

    def next_whole(v, a, g, ny):
        first = roll(v[ny - 1], 32, -1)
        last = roll(v[0], -32, -1)
        out = []
        for y in range(ny):
            xp, xm, zp, zm = around(v[y])
            yp = v[y + 1] if y + 1 < ny else last
            ym = v[y - 1] if y else first
            t = (0.2 * v[y] + g(y)) + (a(0, y) * xp + a(1, y) * xm)
            out.append(t + ((a(2, y) * zp + a(3, y) * zm) + (a(4, y) * yp + a(5, y) * ym)))
        return out

    def a3(m, y):
        return A3[m, y]

    def g3(y):
        return Q3[y]

    def sweeps3(v, count):
        return lax.fori_loop(0, count, lambda i, w: tuple(next_whole(list(w), a3, g3, 4)), tuple(v))

    def lower_levels():
        v = sweeps3([Q3[y] for y in range(4)], 5)
        w = next_whole(list(v), a3, g3, 4)
        r = [(w[y] - v[y]) * I3[y] for y in range(4)]
        g4 = [fold(r[2 * y:2 * y + 2]) * S4[y] for y in range(2)]
        a4 = [[A4[m, y] for y in range(2)] for m in range(6)]
        c = lax.fori_loop(
            0, 15, lambda i, w: tuple(next_whole(list(w), lambda m, y: a4[m][y], lambda y: g4[y], 2)), tuple(g4))
        v = [v[y] + c[y // 2] for y in range(4)]
        return sweeps3(v, 6)

    pl.semaphore_wait(barrier, len(PEERS))
    loads[0].wait()
    permute_in(KF)
    pack0(KF)
    k0 = copies0(KF)
    start(k0)
    loads[1].wait()
    permute_in(BF)
    pack0(BF)
    b0 = copies0(BF)
    start(b0)

    restrict_k1()
    pack1(KF)
    k1 = copies1(KF)
    start(k1)
    pack_k2()
    k2 = copies_plane(KF)
    start(k2)

    wait_recv(k0)
    assemble0(KF, K0)
    coefs0()
    wait_recv(b0)
    assemble0(BF, B0)

    def first_sweep0(x, _):
        V0[x] = S0[x] * B0[x]
        return 0
    lax.fori_loop(2, 30, first_sweep0, 0)
    wait_recv(k2)
    spread(KF)
    k2l = copies_line(KF)
    start(k2l)
    sweeps0(5)
    restrict_b1()
    pack1(BF)
    b1 = copies1(BF)
    start(b1)

    def stage0(x, _):
        for j in range(6):
            T0[x, pl.ds(j, 8, stride=6), :] = jnp.where(
                lane < 64, V0[8 + x, 0, j], pltpu.roll(V0[8 + x, 1, j], 64, 1))
        D0[VF, 8 + x, 8:40, :] = T0[x, 8:40, :]
        return 0
    lax.fori_loop(0, 16, stage0, 0)
    pack0(VF)
    v0 = copies0(VF)
    start(v0)

    wait_recv(k1)
    assemble1(KF, K1)
    k1f = copies_far(K1, 0)
    start(k1f)
    wait_recv(k2l)
    load_k2()
    wait_recv(k1f)
    coefs1()

    wait_recv(b1)
    assemble1(BF, B1)

    def first_sweep1(x, _):
        V1[x] = S1[x] * B1[x]
        return 0
    lax.fori_loop(3, 23, first_sweep1, 0)
    sweeps1(4, 9, 5)
    pack_b2()
    b2 = copies_plane(BF)
    start(b2)

    def stage1(i, _):
        for j in range(5):
            T2[i, pl.ds(j, 8, stride=5), :] = jnp.where(
                lane < 64, V1[9 + i, j], pltpu.roll(V1[13 + i, j], 64, 1))
        for t in range(2):
            D1[VF, 1, i, 16 + 8 * t:24 + 8 * t, :] = T2[i, pl.ds(12 + 8 * t, 8, stride=1), :]
        return 0
    lax.fori_loop(0, 4, stage1, 0)
    pack1(VF)
    v1 = copies1(VF)
    start(v1)

    wait_recv(b2)
    spread(BF)
    b2l = copies_line(BF)
    start(b2l)

    wait_recv(v1)
    assemble1(VF, W1)
    v1f = copies_far(W1, 1)
    start(v1f)
    wait_recv(v0)
    assemble0(VF, W0)

    wait_recv(b2l)

    def load_b2(y, _):
        q = S2[y] * gathered(BF, y)
        Q2[y] = q
        V2[y + 1] = q
        return 0
    lax.fori_loop(0, 8, load_b2, 0)
    sweeps2(5)

    edges(V2, 8)

    def restrict2(y, _):
        r = []
        for u in range(2):
            z = 2 * y + u
            cur = V2[z + 1]
            r.append((next2(z, cur, V2[z], V2[z + 2]) - cur) * I2[z])
        Q3[y] = fold(r) * S3[y]
        return 0
    lax.fori_loop(0, 4, restrict2, 0)
    v3 = lower_levels()
    for y in range(4):
        V3[y] = v3[y]

    def prolong2(y, _):
        for xl in range(4):
            for zl in range(4):
                V2[y + 1, xl, zl] = V2[y + 1, xl, zl] + V3[lax.div(y, 2), xl // 2, zl // 2]
        return 0
    lax.fori_loop(0, 8, prolong2, 0)
    sweeps2(6)

    def lay2(y, _):
        for xl in range(4):
            for zl in range(4):
                H2[pl.ds((xl * 4 + zl) * 8 + y, 8, stride=128), :] = V2[y + 1, xl, zl]
        return 0
    lax.fori_loop(0, 8, lay2, 0)
    planes = [(-2, 3)] + [(o, xl) for o in (-1, 0, 1) for xl in range(4)] + [(2, 0)]
    acc = None
    zf = jnp.where(ll < 96, ll, ll - 128)
    zc = lax.div(zf + 128, 2) - 64 + iz * 32
    for zl in range(4):
        left = []
        for o, xl in planes:
            at_x = jnp.clip(ix + o, 0, 7)
            left.append(H2[pl.ds(pl.multiple_of(at_x * 128 + (xl * 4 + zl) * 8, 8), 8), :])
        left = jnp.concatenate(left, axis=0)
        ok = (zc >= 0) & (zc < 128) & (lax.rem(zc + 128, 4) == zl)
        right = jnp.concatenate(
            [(ok & (cc == (iy + dy) * 32 + lax.div(zc, 4))).astype(F32) for dy in (-1, 0, 1)], axis=1)
        part = dot(left, right)
        acc = part if acc is None else acc + part
    for m in range(14):
        for d in range(3):
            v = acc[8 * m:8 * m + 8, 128 * d:128 * d + 128]
            F1[m, pl.ds(16 * d, 8, stride=2), :] = v
            F1[m, pl.ds(16 * d + 1, 8, stride=2), :] = v
    wait_recv(v1f)

    def start1(x, _):
        m = lax.div(x + 1, 2)
        for j in range(5):
            V1[x, j] = jnp.where(K1[x, j] > 0, W1[x, j] + F1[m, pl.ds(4 + j, 8, stride=5), :], 0.0)
        return 0
    lax.fori_loop(0, 26, start1, 0)
    sweeps1(1, 12, 6)

    def lay1(i, _):
        for j in range(5):
            F0[i, pl.ds(j, 8, stride=5), :] = V1[6 + i, j]
        return 0
    lax.fori_loop(0, 14, lay1, 0)

    def start0(i, _):
        for m in range(3):
            add = F0[i, pl.ds(8 + m, 8, stride=3), :]
            for u in range(2):
                x = 2 + 2 * i + u
                for p in range(2):
                    for o in range(2):
                        j = 2 * m + o
                        V0[x, p, j] = jnp.where(S0[x, p, j] > 0, W0[x, p, j] + add, 0.0)
        return 0
    lax.fori_loop(0, 14, start0, 0)
    sweeps0(6)

    join = (ll == jnp.where(cc < 64, 2 * cc, 2 * (cc - 64) + 1)).astype(F32)

    def finish(x, _):
        for j in range(6):
            T0[x, pl.ds(j, 8, stride=6), :] = jnp.where(
                lane < 64, V0[8 + x, 0, j], pltpu.roll(V0[8 + x, 1, j], 64, 1))
        return 0
    lax.fori_loop(0, 16, finish, 0)

    def permute_out(i, _):
        d = T0[pl.ds(i * 4, 4), 8:40, :].reshape(128, 128)
        out_ref[pl.ds(i * 4, 4)] = dot(d, join).reshape(4, 32, 128)
        return 0
    lax.fori_loop(0, 4, permute_out, 0)
    for made in (k0, b0, v0, k1, b1, v1, k1f, v1f, k2, b2, k2l, b2l):
        wait_send(made)


def shards(source, conductivity):
    def vm(*shape):
        return pltpu.VMEM(shape, F32)

    def dma(n):
        return pltpu.SemaphoreType.DMA((n,))

    fine = (32, 2, 6, 8, 128)
    mid = (26, 5, 8, 128)
    low2, low3, low4 = (4, 4, 8, 128), (2, 2, 8, 128), (1, 1, 8, 128)
    scratch = [
        vm(2, 16, 32, 128), vm(3, 32, 48, 128), vm(3, 2, 32, 128), vm(3, 2, 4, 48, 128),
        vm(*fine), vm(*fine), vm(*fine), vm(*fine), vm(*fine), vm(*fine), vm(*fine), vm(*fine), vm(16, 48, 128),
        vm(3, 3, 4, 48, 128), vm(3, 2, 16, 128), vm(3, 2, 3, 2, 48, 128),
        vm(*mid), vm(*mid), vm(*mid), vm(*mid), vm(*mid), vm(*mid), vm(*mid), vm(*mid),
        vm(4, 32, 128), vm(4, 40, 128), vm(14, 40, 128), vm(14, 48, 128),
        vm(2, 8, 128), vm(2, 16, 8, 128), vm(2, 1024, 128), vm(1024, 128),
        vm(10, *low2), vm(10, *low2), vm(6, 8, *low2), vm(8, *low2), vm(8, *low2), vm(8, *low2),
        vm(6, *low3), vm(4, *low3), vm(6, 4, *low3), vm(4, *low3), vm(4, *low3), vm(4, *low3),
        vm(4, *low4), vm(6, 2, *low4), vm(2, *low4), vm(2, *low4),
        dma(2), dma(78), dma(78), dma(78), dma(78), dma(4), dma(4), dma(30), dma(30), dma(14), dma(14),
    ]
    return pl.pallas_call(
        kernel,
        out_shape=jax.ShapeDtypeStruct((16, 32, 128), F32),
        in_specs=[pl.BlockSpec(memory_space=pl.ANY)] * 2,
        out_specs=pl.BlockSpec(memory_space=pltpu.VMEM),
        scratch_shapes=scratch,
        compiler_params=pltpu.CompilerParams(
            collective_id=0, has_side_effects=True, vmem_limit_bytes=52 * 1024 * 1024),
    )(source, conductivity)


def solution(mesh):
    spec = P("gx", "gy", "gz")
    return jax.shard_map(shards, mesh=mesh, in_specs=(spec, spec), out_specs=spec, check_vma=False)
```

```python
import jax
import jax.numpy as jnp
from jax import lax
from jax.experimental import pallas as pl
from jax.experimental.pallas import tpu as pltpu
from jax.sharding import PartitionSpec as P

MESH = pl.DeviceIdType.MESH
F32 = jnp.float32
HI = lax.Precision.HIGHEST
DAMPING = 0.8

U0 = 4
UC0 = 3
UC1 = 6

KF, BF, VF = 0, 1, 2
NEAR = [(a, b, c) for a in (-1, 0, 1) for b in (-1, 0, 1) for c in (-1, 0, 1) if (a, b, c) != (0, 0, 0)]
PLANE = [(0, b, c) for b in range(4) for c in range(4) if (b, c) != (0, 0)]
LINE = [(a, 0, 0) for a in range(1, 8)]
PEERS = sorted({(a % 8, b % 4, c % 4) for a, b, c in NEAR + PLANE + LINE})


def iota(shape, dim):
    return lax.broadcasted_iota(jnp.int32, shape, dim)


def roll(v, amount, axis):
    shape = v.shape
    if axis == -1:
        return pltpu.roll(v.reshape(-1, 128), amount % 128, 1).reshape(shape)
    return pltpu.roll(v.reshape(-1, 8, 128), amount % 8, 1).reshape(shape)


def shifted(v, axis, step, edge):
    n = v.shape[axis]
    if n == 1:
        return edge
    if step > 0:
        return jnp.concatenate([lax.slice_in_dim(v, 1, n, axis=axis), edge], axis=axis)
    return jnp.concatenate([edge, lax.slice_in_dim(v, 0, n - 1, axis=axis)], axis=axis)


def up(v):
    return jnp.concatenate([v[1:], roll(v[:1], -1, -2)], axis=0)


def down(v):
    return jnp.concatenate([roll(v[-1:], 1, -2), v[:-1]], axis=0)


def times(count, step):
    def body(i, carry):
        for u in range(count):
            step(i * count + u, 0)
        return carry
    return body


def dot(a, b):
    return jnp.dot(a, b, precision=HI, preferred_element_type=F32)


def kernel(
    src_hbm, cond_hbm, out_ref,
    raw, D0, Z0s, Z0r, K0, CX0, CY0, CYM0, CZ0, CZM0, S0, B0, V0, W0, T0,
    D1, Z1s, Z1r, K1, CX1, CY1, CYM1, CZ1, CZM1, S1, B1, V1, W1, T1, T2, F0, F1,
    P2s, R2, G2, H2, K2, V2, A2, S2, I2, Q2, K3, V3, A3, S3, I3, Q3, K4, A4, S4, Q4,
    raw_sem, s0s, s0r, s1s, s1r, xs, xr, g1s, g1r, g2s, g2r,
):
    ix, iy, iz = lax.axis_index("gx"), lax.axis_index("gy"), lax.axis_index("gz")
    lane = iota((8, 128), 1)
    row = iota((8, 128), 0)

    def at(offset):
        a, b, c = offset
        return (lax.rem(ix + (a + 8), 8), lax.rem(iy + (b + 4), 4), lax.rem(iz + (c + 4), 4))

    def remote(src, dst, send, recv, offset):
        return pltpu.make_async_remote_copy(
            src_ref=src, dst_ref=dst, send_sem=send, recv_sem=recv, device_id=at(offset), device_id_type=MESH)

    loads = [pltpu.make_async_copy(cond_hbm, raw.at[0], raw_sem.at[0]),
             pltpu.make_async_copy(src_hbm, raw.at[1], raw_sem.at[1])]
    for c in loads:
        c.start()
    barrier = pltpu.get_barrier_semaphore()
    for offset in PEERS:
        pl.semaphore_signal(barrier, inc=1, device_id=at(offset), device_id_type=MESH)

    def copies0(f):
        count = 7 if f == KF else 6
        made = []
        for n, (dx, dy, dz) in enumerate(NEAR):
            sx, tx, cx = {0: (8, 8, 16), -1: (8, 24, count), 1: (24 - count, 8 - count, count)}[dx]
            sr, tr, cr = {0: (8, 8, 32), -1: (8, 40, 8), 1: (32, 0, 8)}[dy]
            if dz == 0:
                src = D0.at[f, pl.ds(sx, cx), pl.ds(sr, cr)]
                dst = D0.at[f, pl.ds(tx, cx), pl.ds(tr, cr)]
            else:
                side = 0 if dz == -1 else 1
                sh, th, ch = {0: (0, 1, 2), -1: (0, 3, 1), 1: (1, 0, 1)}[dx]
                src = Z0s.at[f, pl.ds(sh, ch), pl.ds(sr - 8, cr)]
                dst = Z0r.at[f, side, pl.ds(th, ch), pl.ds(tr, cr)]
            made.append(remote(src, dst, s0s.at[f * 26 + n], s0r.at[f * 26 + n], (dx, dy, dz)))
        return made

    def copies1(f):
        made = []
        for n, (dx, dy, dz) in enumerate(NEAR):
            if f == BF:
                sr, tr, cr = {0: (16, 16, 16), -1: (16, 32, 8), 1: (24, 8, 8)}[dy]
            else:
                sr, tr, cr = {0: (16, 16, 16), -1: (16, 32, 16), 1: (16, 0, 16)}[dy]
            if dz == 0:
                src = D1.at[f, 1, :, pl.ds(sr, cr)]
                dst = D1.at[f, 1 - dx, :, pl.ds(tr, cr)]
            else:
                side = 0 if dz == -1 else 1
                src = Z1s.at[f, :, pl.ds(sr - 16, cr)]
                dst = Z1r.at[f, side, 1 - dx, :, pl.ds(tr, cr)]
            made.append(remote(src, dst, s1s.at[f * 26 + n], s1r.at[f * 26 + n], (dx, dy, dz)))
        return made

    def copies_far(ref, f):
        return [remote(ref.at[8], ref.at[0], xs.at[2 * f], xr.at[2 * f], (1, 0, 0)),
                remote(ref.at[17], ref.at[25], xs.at[2 * f + 1], xr.at[2 * f + 1], (-1, 0, 0))]

    here = iy * 4 + iz

    def copies_plane(f):
        return [remote(P2s.at[f], R2.at[f, here], g1s.at[f * 15 + n], g1r.at[f * 15 + n], o)
                for n, o in enumerate(PLANE)]

    slab = pl.ds(pl.multiple_of(ix * 128, 128), 128)

    def copies_line(f):
        return [remote(G2.at[f, slab], G2.at[f, slab], g2s.at[f * 7 + n], g2r.at[f * 7 + n], o)
                for n, o in enumerate(LINE)]

    def start(made):
        for c in made:
            c.start()

    def wait_recv(made):
        for c in made:
            c.wait_recv()

    def wait_send(made):
        for c in made:
            c.wait_send()

    cc, ll = iota((128, 128), 0), iota((128, 128), 1)
    split = (cc == jnp.where(ll < 64, 2 * ll, 2 * (ll - 64) + 1)).astype(F32)
    lane32 = iota((32, 128), 1)
    lane16 = iota((16, 128), 1)

    def permute_in(f):
        def body(i, _):
            x = raw[f, pl.ds(i * 4, 4)].reshape(128, 128)
            D0[f, pl.ds(8 + i * 4, 4), 8:40, :] = dot(x, split).reshape(4, 32, 128)
            return 0
        lax.fori_loop(0, 4, body, 0)

    even_strip = (lane32 < 4) | ((lane32 >= 60) & (lane32 < 64))
    odd_strip = ((lane32 >= 64) & (lane32 < 68)) | (lane32 >= 124)

    def pack0(f):
        for h in range(2):
            total = None
            for xi in range(8):
                d = D0[f, 8 + 8 * h + xi, 8:40, :]
                part = (pltpu.roll(jnp.where(even_strip, d, 0.0), (16 * xi) % 128, 1)
                        + pltpu.roll(jnp.where(odd_strip, d, 0.0), (16 * xi + 72) % 128, 1))
                total = part if total is None else total + part
            Z0s[f, h] = total

    ring0 = (lane < 64) | ((lane < 68) & (iz < 3)) | ((lane >= 124) & (iz > 0))
    even4 = lax.rem(lax.div(lane, 4), 2) == 0

    def assemble0(f, dst):
        def body(xh, _):
            for j in range(6):
                rows = pl.ds(j, 8, stride=6)
                c = jnp.where(even4, Z0r[f, 0, xh, rows, :], Z0r[f, 1, xh, rows, :])
                mask = ring0
                if f == KF:
                    y = row * 6 + j + (iy * 32 - 8)
                    xb = ix * 2 + xh - 1
                    mask = mask & (y >= 0) & (y < 128) & (xb >= 0) & (xb < 16)
                for xi in range(8):
                    x = xh * 8 + xi
                    d = D0[f, x, rows, :]
                    full = mask
                    if f == KF and xi in (0, 7):
                        full = mask & (x > 0) & (x < 31)
                    for p in range(2):
                        main = d if p == 0 else pltpu.roll(d, 64, 1)
                        halo = pltpu.roll(c, (64 - 16 * xi - 8 * p) % 128, 1)
                        dst[x, p, j] = jnp.where(full, jnp.where(lane < 64, main, halo), 0.0)
            return 0
        lax.fori_loop(0, 4, body, 0)

    def coefs0():
        def body(q, carry):
            (ke, ko), lower = carry
            for u in range(UC0):
                x = 1 + UC0 * q + u
                ne, no = K0[x + 1, 0], K0[x + 1, 1]
                xe, xo = 0.5 * (ke + ne), 0.5 * (ko + no)
                ye, yo = 0.5 * (ke + up(ke)), 0.5 * (ko + up(ko))
                me, mo = 0.5 * (ke[:1] + roll(ke[-1:], 1, -2)), 0.5 * (ko[:1] + roll(ko[-1:], 1, -2))
                ze, zo = 0.5 * (ke + ko), 0.5 * (ko + roll(ke, -1, -1))
                zm = 0.5 * (ke + roll(ko, 1, -1))
                de = xe + lower[0] + ye + jnp.concatenate([me, ye[:-1]], axis=0) + ze + zm
                do = xo + lower[1] + yo + jnp.concatenate([mo, yo[:-1]], axis=0) + zo + ze
                CX0[x, 0], CX0[x, 1] = xe, xo
                CY0[x, 0], CY0[x, 1] = ye, yo
                CYM0[x, 0], CYM0[x, 1] = me[0], mo[0]
                CZ0[x, 0], CZ0[x, 1] = ze, zo
                CZM0[x] = zm
                S0[x, 0] = jnp.where(ke > 0, DAMPING / de, 0.0)
                S0[x, 1] = jnp.where(ko > 0, DAMPING / do, 0.0)
                ke, ko, lower = ne, no, (xe, xo)
            return (ke, ko), lower
        first = (K0[1, 0], K0[1, 1])
        lax.fori_loop(0, 30 // UC0, body, (first, (0.5 * first[0], 0.5 * first[1])))

    def flow0(x, c, n, low):
        ce, co = c
        fe, fo = CX0[x, 0] * (n[0] - ce), CX0[x, 1] * (n[1] - co)
        ye, yo = CY0[x, 0] * (up(ce) - ce), CY0[x, 1] * (up(co) - co)
        me = CYM0[x, 0][None] * (ce[:1] - roll(ce[-1:], 1, -2))
        mo = CYM0[x, 1][None] * (co[:1] - roll(co[-1:], 1, -2))
        ze = CZ0[x, 0] * (co - ce)
        zo, zm = CZ0[x, 1] * (roll(ce, -1, -1) - co), CZM0[x] * (ce - roll(co, 1, -1))
        re = B0[x, 0] + ((fe - low[0]) + (ye - jnp.concatenate([me, ye[:-1]], axis=0)) + (ze - zm))
        ro = B0[x, 1] + ((fo - low[1]) + (yo - jnp.concatenate([mo, yo[:-1]], axis=0)) + (zo - ze))
        return (re, ro), (fe, fo)

    def pair0(x):
        return V0[x, 0], V0[x, 1]

    def first0(x):
        c, n = pair0(x - 1), pair0(x)
        return CX0[x - 1, 0] * (n[0] - c[0]), CX0[x - 1, 1] * (n[1] - c[1])

    def sweeps0(count):
        def sweep(i, _):
            lo = 3 + i
            def body(q, carry):
                c, low = carry
                for u in range(U0):
                    x = lo + U0 * q + u
                    n = pair0(x + 1)
                    r, low = flow0(x, c, n, low)
                    V0[x, 0] = c[0] + S0[x, 0] * r[0]
                    V0[x, 1] = c[1] + S0[x, 1] * r[1]
                    c = n
                return c, low
            lax.fori_loop(0, lax.div(26 - 2 * i + (U0 - 1), U0), body, (pair0(lo), first0(lo)))
            return 0
        lax.fori_loop(0, count, sweep, 0)

    def restrict_k1():
        def body(i, _):
            for t in range(2):
                parts = []
                for base in (8, 16):
                    x = base + 2 * i
                    a = None
                    for u in range(2):
                        for o in range(2):
                            d = D0[KF, x + u, pl.ds(8 + 16 * t + o, 8, stride=2), :]
                            a = d if a is None else a + d
                    parts.append((a + pltpu.roll(a, 64, 1)) * 0.125)
                D1[KF, 1, i, 16 + 8 * t:24 + 8 * t, :] = jnp.where(lane < 64, parts[0], parts[1])
            return 0
        lax.fori_loop(0, 4, body, 0)

    def restrict_b1():
        def coarse(x):
            total = None
            low = first0(x)
            c = pair0(x)
            for u in range(2):
                n = pair0(x + u + 1)
                r, low = flow0(x + u, c, n, low)
                c = n
                part = r[0] + r[1]
                total = part if total is None else total + part
            return [(total[2 * m] + total[2 * m + 1]) * 0.125 for m in range(3)]
        def body(i, _):
            a, b = coarse(8 + 2 * i), coarse(16 + 2 * i)
            for m in range(3):
                T1[i, pl.ds(4 + m, 8, stride=3), :] = jnp.where(lane < 64, a[m], pltpu.roll(b[m], 64, 1))
            return 0
        lax.fori_loop(0, 4, body, 0)
        D1[BF, 1, :, 16:32, :] = T1[:, 8:24, :]

    low_strip = (lane16 < 16) | ((lane16 >= 48) & (lane16 < 64))
    high_strip = ((lane16 >= 64) & (lane16 < 80)) | (lane16 >= 112)

    def pack1(f):
        for h, strip in ((0, low_strip), (1, high_strip)):
            total = None
            for u in range(4):
                d = D1[f, 1, u, 16:32, :]
                part = pltpu.roll(jnp.where(strip, d, 0.0), (64 * h + 32 * u) % 128, 1)
                total = part if total is None else total + part
            Z1s[f, h] = total

    ring1 = (lane < 64) | ((lane < 80) & (iz < 3)) | ((lane >= 112) & (iz > 0))
    even16 = lax.rem(lax.div(lane, 16), 2) == 0

    def assemble1(f, dst):
        def body(g, _):
            for j in range(5):
                rows = pl.ds(4 + j, 8, stride=5)
                c = [jnp.where(even16, Z1r[f, 0, g, h, rows, :], Z1r[f, 1, g, h, rows, :]) for h in range(2)]
                mask = ring1
                if f == KF:
                    y = row * 5 + j + (iy * 16 - 12)
                    xb = ix + g - 1
                    mask = mask & (y >= 0) & (y < 64) & (xb >= 0) & (xb < 8)
                for xl in range(8):
                    d = D1[f, g, xl % 4, rows, :]
                    main = d if xl < 4 else pltpu.roll(d, 64, 1)
                    halo = pltpu.roll(c[xl // 4], (64 - 32 * (xl % 4)) % 128, 1)
                    dst[1 + g * 8 + xl, j] = jnp.where(mask, jnp.where(lane < 64, main, halo), 0.0)
            return 0
        lax.fori_loop(0, 3, body, 0)

    HW1 = 0.5 * 0.25

    def coefs1():
        def body(q, lower):
            for u in range(UC1):
                x = 1 + UC1 * q + u
                k, n = K1[x], K1[x + 1]
                cx, cy, cz = HW1 * (k + n), HW1 * (k + up(k)), HW1 * (k + roll(k, -1, -1))
                ym, zm = HW1 * (k[:1] + roll(k[-1:], 1, -2)), HW1 * (k + roll(k, 1, -1))
                d = cx + lower + cy + jnp.concatenate([ym, cy[:-1]], axis=0) + cz + zm
                CX1[x], CY1[x], CYM1[x], CZ1[x], CZM1[x] = cx, cy, ym[0], cz, zm
                S1[x] = jnp.where(k > 0, DAMPING / d, 0.0)
                lower = cx
            return lower
        c0 = HW1 * (K1[0] + K1[1])
        CX1[0] = c0
        lax.fori_loop(0, 24 // UC1, body, c0)

    def flow1(x, c, n, low):
        f = CX1[x] * (n - c)
        y = CY1[x] * (up(c) - c)
        ym = CYM1[x][None] * (c[:1] - roll(c[-1:], 1, -2))
        z, zm = CZ1[x] * (roll(c, -1, -1) - c), CZM1[x] * (c - roll(c, 1, -1))
        return B1[x] + ((f - low) + (y - jnp.concatenate([ym, y[:-1]], axis=0)) + (z - zm)), f

    def sweeps1(lo, planes, count):
        def sweep(i, _):
            c = V1[lo]
            low = CX1[lo - 1] * (c - V1[lo - 1])
            for x in range(lo, lo + planes):
                n = V1[x + 1]
                r, low = flow1(x, c, n, low)
                V1[x] = c + S1[x] * r
                c = n
            return 0
        lax.fori_loop(0, count, sweep, 0)

    def pick(xl):
        q = lax.rem(ll, 32)
        z = lax.rem(q, 8) * 4 + lax.div(q, 8)
        return ((lax.div(ll, 32) == xl) & (lax.div(cc, 2) == z)).astype(F32)

    picks = [pick(xl) for xl in range(4)]

    def pack_k2():
        total = None
        for h in range(2):
            a = None
            for u in range(2):
                for o in range(2):
                    d = D1[KF, 1, 2 * h + u, pl.ds(16 + o, 8, stride=2), :]
                    a = d if a is None else a + d
            a = a * 0.125
            part = dot(a, picks[h]) + dot(pltpu.roll(a, 64, 1), picks[2 + h])
            total = part if total is None else total + part
        P2s[KF] = total
        R2[KF, here] = total

    def pack_b2():
        for xl in range(4):
            x = 9 + 2 * xl
            total = None
            c = V1[x]
            low = CX1[x - 1] * (c - V1[x - 1])
            for u in range(2):
                n = V1[x + u + 1]
                r, low = flow1(x + u, c, n, low)
                c = n
                total = r if total is None else total + r
            for j in range(5):
                T2[xl, pl.ds(j, 8, stride=5), :] = total[j]
        total = None
        for xl in range(4):
            a = (T2[xl, pl.ds(12, 8, stride=2), :] + T2[xl, pl.ds(13, 8, stride=2), :]) * 0.125
            part = dot(a, picks[xl])
            total = part if total is None else total + part
        P2s[BF] = total
        R2[BF, here] = total

    def spread(f):
        v = [R2[f, g] for g in range(16)]
        for bit in (1, 2, 4, 8):
            clear = lax.rem(lax.div(lane, 8 * bit), 2) == 0
            for r in range(16):
                if r & bit:
                    continue
                a, d = v[r], v[r | bit]
                v[r] = jnp.where(clear, a, pltpu.roll(d, 8 * bit, 1))
                v[r | bit] = jnp.where(clear, pltpu.roll(a, 128 - 8 * bit, 1), d)
        for q in range(16):
            G2[f, pl.ds(pl.multiple_of(ix * 128 + q * 8, 8), 8), :] = v[q]

    def gathered(f, yl):
        rows = []
        for xl in range(4):
            rows.append(jnp.stack([G2[f, pl.ds((xl * 4 + zl) * 8 + yl, 8, stride=128), :] for zl in range(4)], 0))
        return jnp.stack(rows, 0)

    def edges(ref, ny):
        ref[0] = jnp.where(lane >= 32, roll(ref[ny], 32, -1), 0.0)
        ref[ny + 1] = jnp.where(lane < 96, roll(ref[1], -32, -1), 0.0)

    def around(v):
        xp = shifted(v, 0, 1, roll(v[:1], -1, -2))
        xm = shifted(v, 0, -1, roll(v[-1:], 1, -2))
        zp = shifted(v, 1, 1, roll(v[:, :1], -1, -1))
        zm = shifted(v, 1, -1, roll(v[:, -1:], 1, -1))
        return xp, xm, zp, zm

    z_top, z_end = lax.rem(lane, 32) == 31, lax.rem(lane, 32) == 0

    def inside(k):
        xp = shifted(k, 0, 1, jnp.where(row == 7, 0.0, roll(k[:1], -1, -2)))
        xm = shifted(k, 0, -1, jnp.where(row == 0, 0.0, roll(k[-1:], 1, -2)))
        zp = shifted(k, 1, 1, jnp.where(z_top, 0.0, roll(k[:, :1], -1, -1)))
        zm = shifted(k, 1, -1, jnp.where(z_end, 0.0, roll(k[:, -1:], 1, -1)))
        return xp, xm, zp, zm

    def coefs_low(level, K, A, S, I, ny):
        hw = 0.5 * 0.25 ** level
        edges(K, ny)
        def body(y, _):
            k = K[y + 1]
            near = inside(k) + (K[y + 2], K[y])
            c = [hw * (k + n) for n in near]
            d = ((c[0] + c[1]) + (c[2] + c[3])) + (c[4] + c[5])
            s = DAMPING / d
            S[y] = s
            if I is not None:
                I[y] = d * (1.0 / DAMPING)
            for m in range(6):
                A[m, y] = jnp.where(near[m] > 0, s * c[m], 0.0)
            return 0
        lax.fori_loop(0, ny // 2, times(2, body), 0)

    def fold(blocks):
        t = blocks[0] + blocks[1]
        t = t.reshape((t.shape[0] // 2, 2) + t.shape[1:])
        t = t[:, 0] + t[:, 1]
        t = t.reshape((t.shape[0], t.shape[1] // 2, 2) + t.shape[2:])
        return (t[:, :, 0] + t[:, :, 1]) * 0.125

    def load_k2():
        def body(y, _):
            K2[y + 1] = gathered(KF, y)
            return 0
        lax.fori_loop(0, 2, times(4, body), 0)
        coefs_low(2, K2, A2, S2, I2, 8)
        def body3(y, _):
            K3[y + 1] = fold([K2[2 * y + 1], K2[2 * y + 2]])
            return 0
        lax.fori_loop(0, 1, times(4, body3), 0)
        coefs_low(3, K3, A3, S3, I3, 4)
        for y in range(2):
            K4[y + 1] = fold([K3[2 * y + 1], K3[2 * y + 2]])
        coefs_low(4, K4, A4, S4, None, 2)

    def next2(y, cur, before, after):
        xp, xm, zp, zm = around(cur)
        t = 0.2 * cur + Q2[y]
        t = t + A2[0, y] * xp + A2[1, y] * xm
        t = t + A2[2, y] * zp + A2[3, y] * zm
        return t + (A2[4, y] * after + A2[5, y] * before)

    def sweeps2(count):
        def sweep(i, _):
            edges(V2, 8)
            before = V2[0]
            for y in range(8):
                cur = V2[y + 1]
                V2[y + 1] = next2(y, cur, before, V2[y + 2])
                before = cur
            return 0
        lax.fori_loop(0, count, sweep, 0)

    def next_whole(v, a, g, ny):
        first = roll(v[ny - 1], 32, -1)
        last = roll(v[0], -32, -1)
        out = []
        for y in range(ny):
            xp, xm, zp, zm = around(v[y])
            yp = v[y + 1] if y + 1 < ny else last
            ym = v[y - 1] if y else first
            t = (0.2 * v[y] + g(y)) + (a(0, y) * xp + a(1, y) * xm)
            out.append(t + ((a(2, y) * zp + a(3, y) * zm) + (a(4, y) * yp + a(5, y) * ym)))
        return out

    def a3(m, y):
        return A3[m, y]

    def g3(y):
        return Q3[y]

    def sweeps3(v, count):
        return lax.fori_loop(0, count, lambda i, w: tuple(next_whole(list(w), a3, g3, 4)), tuple(v))

    def lower_levels():
        v = sweeps3([Q3[y] for y in range(4)], 5)
        w = next_whole(list(v), a3, g3, 4)
        r = [(w[y] - v[y]) * I3[y] for y in range(4)]
        g4 = [fold(r[2 * y:2 * y + 2]) * S4[y] for y in range(2)]
        a4 = [[A4[m, y] for y in range(2)] for m in range(6)]
        c = lax.fori_loop(
            0, 15, lambda i, w: tuple(next_whole(list(w), lambda m, y: a4[m][y], lambda y: g4[y], 2)), tuple(g4))
        v = [v[y] + c[y // 2] for y in range(4)]
        return sweeps3(v, 6)

    pl.semaphore_wait(barrier, len(PEERS))
    loads[0].wait()
    permute_in(KF)
    pack0(KF)
    k0 = copies0(KF)
    start(k0)
    loads[1].wait()
    permute_in(BF)
    pack0(BF)
    b0 = copies0(BF)
    start(b0)

    restrict_k1()
    pack1(KF)
    k1 = copies1(KF)
    start(k1)
    pack_k2()
    k2 = copies_plane(KF)
    start(k2)

    wait_recv(k0)
    assemble0(KF, K0)
    coefs0()
    wait_recv(b0)
    assemble0(BF, B0)

    def first_sweep0(x, _):
        V0[2 + x] = S0[2 + x] * B0[2 + x]
        return 0
    lax.fori_loop(0, 7, times(4, first_sweep0), 0)
    wait_recv(k2)
    spread(KF)
    k2l = copies_line(KF)
    start(k2l)
    sweeps0(5)
    restrict_b1()
    pack1(BF)
    b1 = copies1(BF)
    start(b1)

    def stage0(x, _):
        for j in range(6):
            T0[x, pl.ds(j, 8, stride=6), :] = jnp.where(
                lane < 64, V0[8 + x, 0, j], pltpu.roll(V0[8 + x, 1, j], 64, 1))
        D0[VF, 8 + x, 8:40, :] = T0[x, 8:40, :]
        return 0
    lax.fori_loop(0, 4, times(4, stage0), 0)
    pack0(VF)
    v0 = copies0(VF)
    start(v0)

    wait_recv(k1)
    assemble1(KF, K1)
    k1f = copies_far(K1, 0)
    start(k1f)
    wait_recv(k2l)
    load_k2()
    wait_recv(k1f)
    coefs1()

    wait_recv(b1)
    assemble1(BF, B1)

    def first_sweep1(x, _):
        V1[3 + x] = S1[3 + x] * B1[3 + x]
        return 0
    lax.fori_loop(0, 2, times(10, first_sweep1), 0)
    sweeps1(4, 18, 2)
    sweeps1(6, 14, 3)
    pack_b2()
    b2 = copies_plane(BF)
    start(b2)

    def stage1(i, _):
        for j in range(5):
            T2[i, pl.ds(j, 8, stride=5), :] = jnp.where(
                lane < 64, V1[9 + i, j], pltpu.roll(V1[13 + i, j], 64, 1))
        for t in range(2):
            D1[VF, 1, i, 16 + 8 * t:24 + 8 * t, :] = T2[i, pl.ds(12 + 8 * t, 8, stride=1), :]
        return 0
    lax.fori_loop(0, 1, times(4, stage1), 0)
    pack1(VF)
    v1 = copies1(VF)
    start(v1)

    wait_recv(b2)
    spread(BF)
    b2l = copies_line(BF)
    start(b2l)

    wait_recv(v1)
    assemble1(VF, W1)
    v1f = copies_far(W1, 1)
    start(v1f)
    wait_recv(v0)
    assemble0(VF, W0)

    wait_recv(b2l)

    def load_b2(y, _):
        q = S2[y] * gathered(BF, y)
        Q2[y] = q
        V2[y + 1] = q
        return 0
    lax.fori_loop(0, 2, times(4, load_b2), 0)
    sweeps2(5)

    edges(V2, 8)

    def restrict2(y, _):
        r = []
        for u in range(2):
            z = 2 * y + u
            cur = V2[z + 1]
            r.append((next2(z, cur, V2[z], V2[z + 2]) - cur) * I2[z])
        Q3[y] = fold(r) * S3[y]
        return 0
    lax.fori_loop(0, 2, times(2, restrict2), 0)
    v3 = lower_levels()
    for y in range(4):
        V3[y] = v3[y]

    def prolong2(y, _):
        for xl in range(4):
            for zl in range(4):
                V2[y + 1, xl, zl] = V2[y + 1, xl, zl] + V3[lax.div(y, 2), xl // 2, zl // 2]
        return 0
    lax.fori_loop(0, 2, times(4, prolong2), 0)
    sweeps2(6)

    def lay2(y, _):
        for xl in range(4):
            for zl in range(4):
                H2[pl.ds((xl * 4 + zl) * 8 + y, 8, stride=128), :] = V2[y + 1, xl, zl]
        return 0
    lax.fori_loop(0, 2, times(4, lay2), 0)
    planes = [(-2, 3)] + [(o, xl) for o in (-1, 0, 1) for xl in range(4)] + [(2, 0)]
    acc = None
    zf = jnp.where(ll < 96, ll, ll - 128)
    zc = lax.div(zf + 128, 2) - 64 + iz * 32
    for zl in range(4):
        left = []
        for o, xl in planes:
            at_x = jnp.clip(ix + o, 0, 7)
            left.append(H2[pl.ds(pl.multiple_of(at_x * 128 + (xl * 4 + zl) * 8, 8), 8), :])
        left = jnp.concatenate(left, axis=0)
        ok = (zc >= 0) & (zc < 128) & (lax.rem(zc + 128, 4) == zl)
        right = jnp.concatenate(
            [(ok & (cc == (iy + dy) * 32 + lax.div(zc, 4))).astype(F32) for dy in (-1, 0, 1)], axis=1)
        part = dot(left, right)
        acc = part if acc is None else acc + part
    for m in range(14):
        for d in range(3):
            v = acc[8 * m:8 * m + 8, 128 * d:128 * d + 128]
            F1[m, pl.ds(16 * d, 8, stride=2), :] = v
            F1[m, pl.ds(16 * d + 1, 8, stride=2), :] = v
    wait_recv(v1f)

    def start1(x, _):
        m = lax.div(x + 1, 2)
        for j in range(5):
            V1[x, j] = jnp.where(K1[x, j] > 0, W1[x, j] + F1[m, pl.ds(4 + j, 8, stride=5), :], 0.0)
        return 0
    lax.fori_loop(0, 2, times(13, start1), 0)
    sweeps1(1, 24, 3)
    sweeps1(4, 18, 3)

    def lay1(i, _):
        for j in range(5):
            F0[i, pl.ds(j, 8, stride=5), :] = V1[6 + i, j]
        return 0
    lax.fori_loop(0, 2, times(7, lay1), 0)

    def start0(i, _):
        for m in range(3):
            add = F0[i, pl.ds(8 + m, 8, stride=3), :]
            for u in range(2):
                x = 2 + 2 * i + u
                for p in range(2):
                    for o in range(2):
                        j = 2 * m + o
                        V0[x, p, j] = jnp.where(S0[x, p, j] > 0, W0[x, p, j] + add, 0.0)
        return 0
    lax.fori_loop(0, 7, times(2, start0), 0)
    sweeps0(6)

    join = (ll == jnp.where(cc < 64, 2 * cc, 2 * (cc - 64) + 1)).astype(F32)

    def finish(x, _):
        for j in range(6):
            T0[x, pl.ds(j, 8, stride=6), :] = jnp.where(
                lane < 64, V0[8 + x, 0, j], pltpu.roll(V0[8 + x, 1, j], 64, 1))
        return 0
    lax.fori_loop(0, 4, times(4, finish), 0)

    def permute_out(i, _):
        d = T0[pl.ds(i * 4, 4), 8:40, :].reshape(128, 128)
        out_ref[pl.ds(i * 4, 4)] = dot(d, join).reshape(4, 32, 128)
        return 0
    lax.fori_loop(0, 4, permute_out, 0)
    for made in (k0, b0, v0, k1, b1, v1, k1f, v1f, k2, b2, k2l, b2l):
        wait_send(made)


def shards(source, conductivity):
    def vm(*shape):
        return pltpu.VMEM(shape, F32)

    def dma(n):
        return pltpu.SemaphoreType.DMA((n,))

    fine = (32, 2, 6, 8, 128)
    mid = (26, 5, 8, 128)
    low2, low3, low4 = (4, 4, 8, 128), (2, 2, 8, 128), (1, 1, 8, 128)
    scratch = [
        vm(2, 16, 32, 128), vm(3, 32, 48, 128), vm(3, 2, 32, 128), vm(3, 2, 4, 48, 128),
        vm(*fine), vm(*fine), vm(*fine), vm(32, 2, 8, 128), vm(*fine), vm(32, 6, 8, 128),
        vm(*fine), vm(*fine), vm(*fine), vm(*fine), vm(16, 48, 128),
        vm(3, 3, 4, 48, 128), vm(3, 2, 16, 128), vm(3, 2, 3, 2, 48, 128),
        vm(*mid), vm(*mid), vm(*mid), vm(26, 8, 128), vm(*mid), vm(*mid), vm(*mid), vm(*mid), vm(*mid), vm(*mid),
        vm(4, 32, 128), vm(4, 40, 128), vm(14, 40, 128), vm(14, 48, 128),
        vm(2, 8, 128), vm(2, 16, 8, 128), vm(2, 1024, 128), vm(1024, 128),
        vm(10, *low2), vm(10, *low2), vm(6, 8, *low2), vm(8, *low2), vm(8, *low2), vm(8, *low2),
        vm(6, *low3), vm(4, *low3), vm(6, 4, *low3), vm(4, *low3), vm(4, *low3), vm(4, *low3),
        vm(4, *low4), vm(6, 2, *low4), vm(2, *low4), vm(2, *low4),
        dma(2), dma(78), dma(78), dma(78), dma(78), dma(4), dma(4), dma(30), dma(30), dma(14), dma(14),
    ]
    return pl.pallas_call(
        kernel,
        out_shape=jax.ShapeDtypeStruct((16, 32, 128), F32),
        in_specs=[pl.BlockSpec(memory_space=pl.ANY)] * 2,
        out_specs=pl.BlockSpec(memory_space=pltpu.VMEM),
        scratch_shapes=scratch,
        compiler_params=pltpu.CompilerParams(
            collective_id=0, has_side_effects=True, vmem_limit_bytes=52 * 1024 * 1024),
    )(source, conductivity)


def solution(mesh):
    spec = P("gx", "gy", "gz")
    return jax.shard_map(shards, mesh=mesh, in_specs=(spec, spec), out_specs=spec, check_vma=False)
```

```python
import jax
import jax.numpy as jnp
from jax import lax
from jax.experimental import pallas as pl
from jax.experimental.pallas import tpu as pltpu
from jax.sharding import PartitionSpec as P

MESH = pl.DeviceIdType.MESH
F32 = jnp.float32
HI = lax.Precision.HIGHEST
DAMPING = 0.8

U0 = 4
UC0 = 3
UC1 = 6

KF, BF, VF = 0, 1, 2
NEAR = [(a, b, c) for a in (-1, 0, 1) for b in (-1, 0, 1) for c in (-1, 0, 1) if (a, b, c) != (0, 0, 0)]
PLANE = [(0, b, c) for b in range(4) for c in range(4) if (b, c) != (0, 0)]
LINE = [(a, 0, 0) for a in range(1, 8)]
PEERS = sorted({(a % 8, b % 4, c % 4) for a, b, c in NEAR + PLANE + LINE})


def iota(shape, dim):
    return lax.broadcasted_iota(jnp.int32, shape, dim)


def roll(v, amount, axis):
    shape = v.shape
    if axis == -1:
        return pltpu.roll(v.reshape(-1, 128), amount % 128, 1).reshape(shape)
    return pltpu.roll(v.reshape(-1, 8, 128), amount % 8, 1).reshape(shape)


def shifted(v, axis, step, edge):
    n = v.shape[axis]
    if n == 1:
        return edge
    if step > 0:
        return jnp.concatenate([lax.slice_in_dim(v, 1, n, axis=axis), edge], axis=axis)
    return jnp.concatenate([edge, lax.slice_in_dim(v, 0, n - 1, axis=axis)], axis=axis)


def up(v):
    return jnp.concatenate([v[1:], roll(v[:1], -1, -2)], axis=0)


def down(v):
    return jnp.concatenate([roll(v[-1:], 1, -2), v[:-1]], axis=0)


def times(count, step):
    def body(i, carry):
        for u in range(count):
            step(i * count + u, 0)
        return carry
    return body


def dot(a, b):
    return jnp.dot(a, b, precision=HI, preferred_element_type=F32)


def kernel(
    src_hbm, cond_hbm, out_ref,
    raw, D0, Z0s, Z0r, K0, CX0, CY0, CYM0, CZ0, CZM0, S0, B0, V0, W0, T0,
    D1, Z1s, Z1r, K1, CX1, CY1, CYM1, CZ1, CZM1, S1, B1, V1, W1, T1, T2, F0, F1,
    P2s, R2, G2, H2, K2, V2, A2, S2, I2, Q2, K3, V3, A3, S3, I3, Q3, K4, A4, S4, Q4,
    raw_sem, s0s, s0r, s1s, s1r, xs, xr, g1s, g1r, g2s, g2r,
):
    ix, iy, iz = lax.axis_index("gx"), lax.axis_index("gy"), lax.axis_index("gz")
    lane = iota((8, 128), 1)
    row = iota((8, 128), 0)

    def at(offset):
        a, b, c = offset
        return (lax.rem(ix + (a + 8), 8), lax.rem(iy + (b + 4), 4), lax.rem(iz + (c + 4), 4))

    def remote(src, dst, send, recv, offset):
        return pltpu.make_async_remote_copy(
            src_ref=src, dst_ref=dst, send_sem=send, recv_sem=recv, device_id=at(offset), device_id_type=MESH)

    loads = [pltpu.make_async_copy(cond_hbm, raw.at[0], raw_sem.at[0]),
             pltpu.make_async_copy(src_hbm, raw.at[1], raw_sem.at[1])]
    for c in loads:
        c.start()
    barrier = pltpu.get_barrier_semaphore()
    for offset in PEERS:
        pl.semaphore_signal(barrier, inc=1, device_id=at(offset), device_id_type=MESH)

    def copies0(f):
        reach = 7 if f == KF else 6
        made = []
        for n, (dx, dy, dz) in enumerate(NEAR):
            n_x = reach - (dy != 0) - (dz != 0)
            n_y = reach - (dx != 0) - (dz != 0)
            sx, tx, cx = {0: (8, 8, 16), -1: (8, 24, n_x), 1: (24 - n_x, 8 - n_x, n_x)}[dx]
            sr, tr, cr = {0: (8, 8, 32), -1: (8, 40, n_y), 1: (40 - n_y, 8 - n_y, n_y)}[dy]
            if dz == 0:
                src = D0.at[f, pl.ds(sx, cx), pl.ds(sr, cr)]
                dst = D0.at[f, pl.ds(tx, cx), pl.ds(tr, cr)]
            else:
                side = 0 if dz == -1 else 1
                sh, th, ch = {0: (0, 1, 2), -1: (0, 3, 1), 1: (1, 0, 1)}[dx]
                src = Z0s.at[f, pl.ds(sh, ch), pl.ds(sr - 8, cr)]
                dst = Z0r.at[f, side, pl.ds(th, ch), pl.ds(tr, cr)]
            made.append(remote(src, dst, s0s.at[f * 26 + n], s0r.at[f * 26 + n], (dx, dy, dz)))
        return made

    def copies1(f):
        made = []
        for n, (dx, dy, dz) in enumerate(NEAR):
            n_y = 8 if f == BF else 9
            sr, tr, cr = {0: (16, 16, 16), -1: (16, 32, n_y), 1: (32 - n_y, 16 - n_y, n_y)}[dy]
            if dz == 0:
                src = D1.at[f, 1, :, pl.ds(sr, cr)]
                dst = D1.at[f, 1 - dx, :, pl.ds(tr, cr)]
            else:
                side = 0 if dz == -1 else 1
                src = Z1s.at[f, :, pl.ds(sr - 16, cr)]
                dst = Z1r.at[f, side, 1 - dx, :, pl.ds(tr, cr)]
            made.append(remote(src, dst, s1s.at[f * 26 + n], s1r.at[f * 26 + n], (dx, dy, dz)))
        return made

    def copies_far(ref, f):
        return [remote(ref.at[8], ref.at[0], xs.at[2 * f], xr.at[2 * f], (1, 0, 0)),
                remote(ref.at[17], ref.at[25], xs.at[2 * f + 1], xr.at[2 * f + 1], (-1, 0, 0))]

    here = iy * 4 + iz

    def copies_plane(f):
        return [remote(P2s.at[f], R2.at[f, here], g1s.at[f * 15 + n], g1r.at[f * 15 + n], o)
                for n, o in enumerate(PLANE)]

    slab = pl.ds(pl.multiple_of(ix * 128, 128), 128)

    other = 1 - 2 * lax.rem(ix, 2)

    def copies_line(f):
        return [remote(G2.at[f, slab], G2.at[f, slab], g2s.at[f * 7 + n], g2r.at[f * 7 + n], (o, 0, 0))
                for n, o in enumerate((2, 6, 4, other))]

    def copies_on(f):
        made = []
        for n, o in enumerate((2, 6, 4)):
            rows = pl.ds(pl.multiple_of(lax.rem(ix + 8 - o, 8) * 128, 128), 128)
            made.append(remote(G2.at[f, rows], G2.at[f, rows], g2s.at[f * 7 + 4 + n], g2r.at[f * 7 + 4 + n], (other, 0, 0)))
        return made

    def pass_on(made, onward):
        for c, d in zip(made, onward):
            c.wait_recv()
            d.start()

    def start(made):
        for c in made:
            c.start()

    def wait_recv(made):
        for c in made:
            c.wait_recv()

    def wait_send(made):
        for c in made:
            c.wait_send()

    cc, ll = iota((128, 128), 0), iota((128, 128), 1)
    split = (cc == jnp.where(ll < 64, 2 * ll, 2 * (ll - 64) + 1)).astype(F32)
    lane32 = iota((32, 128), 1)
    lane16 = iota((16, 128), 1)

    def permute_in(f):
        for i in range(4):
            x = raw[f, 4 * i:4 * i + 4].reshape(128, 128)
            D0[f, 8 + 4 * i:12 + 4 * i, 8:40, :] = dot(x, split).reshape(4, 32, 128)

    even_strip = (lane32 < 4) | ((lane32 >= 60) & (lane32 < 64))
    odd_strip = ((lane32 >= 64) & (lane32 < 68)) | (lane32 >= 124)

    def pack0(f):
        for h in range(2):
            total = None
            for xi in range(8):
                d = D0[f, 8 + 8 * h + xi, 8:40, :]
                part = (pltpu.roll(jnp.where(even_strip, d, 0.0), (16 * xi) % 128, 1)
                        + pltpu.roll(jnp.where(odd_strip, d, 0.0), (16 * xi + 72) % 128, 1))
                total = part if total is None else total + part
            Z0s[f, h] = total

    ring0 = (lane < 64) | ((lane < 68) & (iz < 3)) | ((lane >= 124) & (iz > 0))
    even4 = lax.rem(lax.div(lane, 4), 2) == 0

    def assemble0(f, dst):
        def body(xh, _):
            for j in range(6):
                rows = pl.ds(j, 8, stride=6)
                c = jnp.where(even4, Z0r[f, 0, xh, rows, :], Z0r[f, 1, xh, rows, :])
                mask = ring0
                if f == KF:
                    y = row * 6 + j + (iy * 32 - 8)
                    xb = ix * 2 + xh - 1
                    mask = mask & (y >= 0) & (y < 128) & (xb >= 0) & (xb < 16)
                for xi in range(8):
                    x = xh * 8 + xi
                    d = D0[f, x, rows, :]
                    full = mask
                    if f == KF and xi in (0, 7):
                        full = mask & (x > 0) & (x < 31)
                    for p in range(2):
                        main = d if p == 0 else pltpu.roll(d, 64, 1)
                        halo = pltpu.roll(c, (64 - 16 * xi - 8 * p) % 128, 1)
                        dst[x, p, j] = jnp.where(full, jnp.where(lane < 64, main, halo), 0.0)
            return 0
        lax.fori_loop(0, 4, body, 0)

    def coefs0():
        def body(q, carry):
            (ke, ko), lower = carry
            for u in range(UC0):
                x = 1 + UC0 * q + u
                ne, no = K0[x + 1, 0], K0[x + 1, 1]
                xe, xo = 0.5 * (ke + ne), 0.5 * (ko + no)
                ye, yo = 0.5 * (ke + up(ke)), 0.5 * (ko + up(ko))
                me, mo = 0.5 * (ke[:1] + roll(ke[-1:], 1, -2)), 0.5 * (ko[:1] + roll(ko[-1:], 1, -2))
                ze, zo = 0.5 * (ke + ko), 0.5 * (ko + roll(ke, -1, -1))
                zm = 0.5 * (ke + roll(ko, 1, -1))
                de = xe + lower[0] + ye + jnp.concatenate([me, ye[:-1]], axis=0) + ze + zm
                do = xo + lower[1] + yo + jnp.concatenate([mo, yo[:-1]], axis=0) + zo + ze
                CX0[x, 0], CX0[x, 1] = xe, xo
                CY0[x, 0], CY0[x, 1] = ye, yo
                CYM0[x, 0], CYM0[x, 1] = me[0], mo[0]
                CZ0[x, 0], CZ0[x, 1] = ze, zo
                CZM0[x] = zm
                S0[x, 0] = jnp.where(ke > 0, DAMPING / de, 0.0)
                S0[x, 1] = jnp.where(ko > 0, DAMPING / do, 0.0)
                ke, ko, lower = ne, no, (xe, xo)
            return (ke, ko), lower
        first = (K0[1, 0], K0[1, 1])
        lax.fori_loop(0, 30 // UC0, body, (first, (0.5 * first[0], 0.5 * first[1])))

    def flow0(x, c, n, low):
        ce, co = c
        fe, fo = CX0[x, 0] * (n[0] - ce), CX0[x, 1] * (n[1] - co)
        ye, yo = CY0[x, 0] * (up(ce) - ce), CY0[x, 1] * (up(co) - co)
        me = CYM0[x, 0][None] * (ce[:1] - roll(ce[-1:], 1, -2))
        mo = CYM0[x, 1][None] * (co[:1] - roll(co[-1:], 1, -2))
        ze = CZ0[x, 0] * (co - ce)
        zo, zm = CZ0[x, 1] * (roll(ce, -1, -1) - co), CZM0[x] * (ce - roll(co, 1, -1))
        re = B0[x, 0] + ((fe - low[0]) + (ye - jnp.concatenate([me, ye[:-1]], axis=0)) + (ze - zm))
        ro = B0[x, 1] + ((fo - low[1]) + (yo - jnp.concatenate([mo, yo[:-1]], axis=0)) + (zo - ze))
        return (re, ro), (fe, fo)

    def pair0(x):
        return V0[x, 0], V0[x, 1]

    def first0(x):
        c, n = pair0(x - 1), pair0(x)
        return CX0[x - 1, 0] * (n[0] - c[0]), CX0[x - 1, 1] * (n[1] - c[1])

    def sweeps0(count):
        def sweep(i, _):
            lo = 3 + i
            def body(q, carry):
                c, low = carry
                for u in range(U0):
                    x = lo + U0 * q + u
                    n = pair0(x + 1)
                    r, low = flow0(x, c, n, low)
                    V0[x, 0] = c[0] + S0[x, 0] * r[0]
                    V0[x, 1] = c[1] + S0[x, 1] * r[1]
                    c = n
                return c, low
            lax.fori_loop(0, lax.div(26 - 2 * i + (U0 - 1), U0), body, (pair0(lo), first0(lo)))
            return 0
        lax.fori_loop(0, count, sweep, 0)

    def restrict_k1():
        def body(i, _):
            for t in range(2):
                parts = []
                for base in (8, 16):
                    x = base + 2 * i
                    a = None
                    for u in range(2):
                        for o in range(2):
                            d = D0[KF, x + u, pl.ds(8 + 16 * t + o, 8, stride=2), :]
                            a = d if a is None else a + d
                    parts.append((a + pltpu.roll(a, 64, 1)) * 0.125)
                D1[KF, 1, i, 16 + 8 * t:24 + 8 * t, :] = jnp.where(lane < 64, parts[0], parts[1])
            return 0
        lax.fori_loop(0, 4, body, 0)

    def restrict_b1():
        def coarse(x):
            total = None
            low = first0(x)
            c = pair0(x)
            for u in range(2):
                n = pair0(x + u + 1)
                r, low = flow0(x + u, c, n, low)
                c = n
                part = r[0] + r[1]
                total = part if total is None else total + part
            return [(total[2 * m] + total[2 * m + 1]) * 0.125 for m in range(3)]
        def body(i, _):
            a, b = coarse(8 + 2 * i), coarse(16 + 2 * i)
            for m in range(3):
                T1[i, pl.ds(4 + m, 8, stride=3), :] = jnp.where(lane < 64, a[m], pltpu.roll(b[m], 64, 1))
            return 0
        lax.fori_loop(0, 4, body, 0)
        D1[BF, 1, :, 16:32, :] = T1[:, 8:24, :]

    low_strip = (lane16 < 16) | ((lane16 >= 48) & (lane16 < 64))
    high_strip = ((lane16 >= 64) & (lane16 < 80)) | (lane16 >= 112)

    def pack1(f):
        for h, strip in ((0, low_strip), (1, high_strip)):
            total = None
            for u in range(4):
                d = D1[f, 1, u, 16:32, :]
                part = pltpu.roll(jnp.where(strip, d, 0.0), (64 * h + 32 * u) % 128, 1)
                total = part if total is None else total + part
            Z1s[f, h] = total

    ring1 = (lane < 64) | ((lane < 80) & (iz < 3)) | ((lane >= 112) & (iz > 0))
    even16 = lax.rem(lax.div(lane, 16), 2) == 0

    def assemble1(f, dst):
        def body(g, _):
            for j in range(5):
                rows = pl.ds(4 + j, 8, stride=5)
                c = [jnp.where(even16, Z1r[f, 0, g, h, rows, :], Z1r[f, 1, g, h, rows, :]) for h in range(2)]
                mask = ring1
                if f == KF:
                    y = row * 5 + j + (iy * 16 - 12)
                    xb = ix + g - 1
                    mask = mask & (y >= 0) & (y < 64) & (xb >= 0) & (xb < 8)
                for xl in range(8):
                    d = D1[f, g, xl % 4, rows, :]
                    main = d if xl < 4 else pltpu.roll(d, 64, 1)
                    halo = pltpu.roll(c[xl // 4], (64 - 32 * (xl % 4)) % 128, 1)
                    dst[1 + g * 8 + xl, j] = jnp.where(mask, jnp.where(lane < 64, main, halo), 0.0)
            return 0
        lax.fori_loop(0, 3, body, 0)

    HW1 = 0.5 * 0.25

    def coefs1():
        def body(q, lower):
            for u in range(UC1):
                x = 1 + UC1 * q + u
                k, n = K1[x], K1[x + 1]
                cx, cy, cz = HW1 * (k + n), HW1 * (k + up(k)), HW1 * (k + roll(k, -1, -1))
                ym, zm = HW1 * (k[:1] + roll(k[-1:], 1, -2)), HW1 * (k + roll(k, 1, -1))
                d = cx + lower + cy + jnp.concatenate([ym, cy[:-1]], axis=0) + cz + zm
                CX1[x], CY1[x], CYM1[x], CZ1[x], CZM1[x] = cx, cy, ym[0], cz, zm
                S1[x] = jnp.where(k > 0, DAMPING / d, 0.0)
                lower = cx
            return lower
        c0 = HW1 * (K1[0] + K1[1])
        CX1[0] = c0
        lax.fori_loop(0, 24 // UC1, body, c0)

    def flow1(x, c, n, low):
        f = CX1[x] * (n - c)
        y = CY1[x] * (up(c) - c)
        ym = CYM1[x][None] * (c[:1] - roll(c[-1:], 1, -2))
        z, zm = CZ1[x] * (roll(c, -1, -1) - c), CZM1[x] * (c - roll(c, 1, -1))
        return B1[x] + ((f - low) + (y - jnp.concatenate([ym, y[:-1]], axis=0)) + (z - zm)), f

    def sweeps1(lo, planes, count):
        def sweep(i, _):
            c = V1[lo]
            low = CX1[lo - 1] * (c - V1[lo - 1])
            for x in range(lo, lo + planes):
                n = V1[x + 1]
                r, low = flow1(x, c, n, low)
                V1[x] = c + S1[x] * r
                c = n
            return 0
        lax.fori_loop(0, count, sweep, 0)

    def pick(xl):
        q = lax.rem(ll, 32)
        z = lax.rem(q, 8) * 4 + lax.div(q, 8)
        return ((lax.div(ll, 32) == xl) & (lax.div(cc, 2) == z)).astype(F32)

    picks = [pick(xl) for xl in range(4)]

    def pack_k2():
        total = None
        for h in range(2):
            a = None
            for u in range(2):
                for o in range(2):
                    d = D1[KF, 1, 2 * h + u, pl.ds(16 + o, 8, stride=2), :]
                    a = d if a is None else a + d
            a = a * 0.125
            part = dot(a, picks[h]) + dot(pltpu.roll(a, 64, 1), picks[2 + h])
            total = part if total is None else total + part
        P2s[KF] = total
        R2[KF, here] = total

    def pack_b2():
        for xl in range(4):
            x = 9 + 2 * xl
            total = None
            c = V1[x]
            low = CX1[x - 1] * (c - V1[x - 1])
            for u in range(2):
                n = V1[x + u + 1]
                r, low = flow1(x + u, c, n, low)
                c = n
                total = r if total is None else total + r
            for j in range(5):
                T2[xl, pl.ds(j, 8, stride=5), :] = total[j]
        total = None
        for xl in range(4):
            a = (T2[xl, pl.ds(12, 8, stride=2), :] + T2[xl, pl.ds(13, 8, stride=2), :]) * 0.125
            part = dot(a, picks[xl])
            total = part if total is None else total + part
        P2s[BF] = total
        R2[BF, here] = total

    def spread(f):
        v = [R2[f, g] for g in range(16)]
        for bit in (1, 2, 4, 8):
            clear = lax.rem(lax.div(lane, 8 * bit), 2) == 0
            for r in range(16):
                if r & bit:
                    continue
                a, d = v[r], v[r | bit]
                v[r] = jnp.where(clear, a, pltpu.roll(d, 8 * bit, 1))
                v[r | bit] = jnp.where(clear, pltpu.roll(a, 128 - 8 * bit, 1), d)
        for q in range(16):
            G2[f, pl.ds(pl.multiple_of(ix * 128 + q * 8, 8), 8), :] = v[q]

    def gathered(f, yl):
        rows = []
        for xl in range(4):
            rows.append(jnp.stack([G2[f, pl.ds((xl * 4 + zl) * 8 + yl, 8, stride=128), :] for zl in range(4)], 0))
        return jnp.stack(rows, 0)

    def edges(ref, ny):
        ref[0] = jnp.where(lane >= 32, roll(ref[ny], 32, -1), 0.0)
        ref[ny + 1] = jnp.where(lane < 96, roll(ref[1], -32, -1), 0.0)

    def around(v):
        xp = shifted(v, 0, 1, roll(v[:1], -1, -2))
        xm = shifted(v, 0, -1, roll(v[-1:], 1, -2))
        zp = shifted(v, 1, 1, roll(v[:, :1], -1, -1))
        zm = shifted(v, 1, -1, roll(v[:, -1:], 1, -1))
        return xp, xm, zp, zm

    z_top, z_end = lax.rem(lane, 32) == 31, lax.rem(lane, 32) == 0

    def inside(k):
        xp = shifted(k, 0, 1, jnp.where(row == 7, 0.0, roll(k[:1], -1, -2)))
        xm = shifted(k, 0, -1, jnp.where(row == 0, 0.0, roll(k[-1:], 1, -2)))
        zp = shifted(k, 1, 1, jnp.where(z_top, 0.0, roll(k[:, :1], -1, -1)))
        zm = shifted(k, 1, -1, jnp.where(z_end, 0.0, roll(k[:, -1:], 1, -1)))
        return xp, xm, zp, zm

    def coefs_low(level, K, A, S, I, ny):
        hw = 0.5 * 0.25 ** level
        edges(K, ny)
        def body(y, _):
            k = K[y + 1]
            near = inside(k) + (K[y + 2], K[y])
            c = [hw * (k + n) for n in near]
            d = ((c[0] + c[1]) + (c[2] + c[3])) + (c[4] + c[5])
            s = DAMPING / d
            S[y] = s
            if I is not None:
                I[y] = d * (1.0 / DAMPING)
            for m in range(6):
                A[m, y] = jnp.where(near[m] > 0, s * c[m], 0.0)
            return 0
        lax.fori_loop(0, ny // 2, times(2, body), 0)

    def fold(blocks):
        t = blocks[0] + blocks[1]
        t = t.reshape((t.shape[0] // 2, 2) + t.shape[1:])
        t = t[:, 0] + t[:, 1]
        t = t.reshape((t.shape[0], t.shape[1] // 2, 2) + t.shape[2:])
        return (t[:, :, 0] + t[:, :, 1]) * 0.125

    def load_k2():
        def body(y, _):
            K2[y + 1] = gathered(KF, y)
            return 0
        lax.fori_loop(0, 2, times(4, body), 0)
        coefs_low(2, K2, A2, S2, I2, 8)
        def body3(y, _):
            K3[y + 1] = fold([K2[2 * y + 1], K2[2 * y + 2]])
            return 0
        lax.fori_loop(0, 1, times(4, body3), 0)
        coefs_low(3, K3, A3, S3, I3, 4)
        for y in range(2):
            K4[y + 1] = fold([K3[2 * y + 1], K3[2 * y + 2]])
        coefs_low(4, K4, A4, S4, None, 2)

    def next2(y, cur, before, after):
        xp, xm, zp, zm = around(cur)
        t = 0.2 * cur + Q2[y]
        t = t + A2[0, y] * xp + A2[1, y] * xm
        t = t + A2[2, y] * zp + A2[3, y] * zm
        return t + (A2[4, y] * after + A2[5, y] * before)

    def sweeps2(count):
        def sweep(i, _):
            edges(V2, 8)
            before = V2[0]
            for y in range(8):
                cur = V2[y + 1]
                V2[y + 1] = next2(y, cur, before, V2[y + 2])
                before = cur
            return 0
        lax.fori_loop(0, count, sweep, 0)

    def next_whole(v, a, g, ny):
        first = roll(v[ny - 1], 32, -1)
        last = roll(v[0], -32, -1)
        out = []
        for y in range(ny):
            xp, xm, zp, zm = around(v[y])
            yp = v[y + 1] if y + 1 < ny else last
            ym = v[y - 1] if y else first
            t = (0.2 * v[y] + g(y)) + (a(0, y) * xp + a(1, y) * xm)
            out.append(t + ((a(2, y) * zp + a(3, y) * zm) + (a(4, y) * yp + a(5, y) * ym)))
        return out

    def a3(m, y):
        return A3[m, y]

    def g3(y):
        return Q3[y]

    def sweeps3(v, count):
        return lax.fori_loop(0, count, lambda i, w: tuple(next_whole(list(w), a3, g3, 4)), tuple(v))

    def lower_levels():
        v = sweeps3([Q3[y] for y in range(4)], 5)
        w = next_whole(list(v), a3, g3, 4)
        r = [(w[y] - v[y]) * I3[y] for y in range(4)]
        g4 = [fold(r[2 * y:2 * y + 2]) * S4[y] for y in range(2)]
        a4 = [[A4[m, y] for y in range(2)] for m in range(6)]
        c = lax.fori_loop(
            0, 15, lambda i, w: tuple(next_whole(list(w), lambda m, y: a4[m][y], lambda y: g4[y], 2)), tuple(g4))
        v = [v[y] + c[y // 2] for y in range(4)]
        return sweeps3(v, 6)

    loads[0].wait()
    permute_in(KF)
    pack0(KF)
    pl.semaphore_wait(barrier, len(PEERS))
    k0 = copies0(KF)
    start(k0)
    loads[1].wait()
    permute_in(BF)
    pack0(BF)
    b0 = copies0(BF)
    start(b0)

    restrict_k1()
    pack1(KF)
    k1 = copies1(KF)
    start(k1)
    pack_k2()
    k2 = copies_plane(KF)
    start(k2)

    wait_recv(k0)
    assemble0(KF, K0)
    coefs0()
    wait_recv(b0)
    assemble0(BF, B0)

    def first_sweep0(x, _):
        V0[2 + x] = S0[2 + x] * B0[2 + x]
        return 0
    lax.fori_loop(0, 7, times(4, first_sweep0), 0)
    wait_recv(k2)
    spread(KF)
    k2l = copies_line(KF)
    start(k2l)
    sweeps0(5)
    restrict_b1()
    pack1(BF)
    b1 = copies1(BF)
    start(b1)

    wait_recv(k1)
    assemble1(KF, K1)
    k1f = copies_far(K1, 0)
    start(k1f)
    k2o = copies_on(KF)
    pass_on(k2l, k2o)
    k2l[3].wait_recv()
    wait_recv(k2o)
    load_k2()
    wait_recv(k1f)
    coefs1()

    wait_recv(b1)
    assemble1(BF, B1)

    def first_sweep1(x, _):
        V1[3 + x] = S1[3 + x] * B1[3 + x]
        return 0
    lax.fori_loop(0, 2, times(10, first_sweep1), 0)
    sweeps1(4, 18, 2)
    sweeps1(6, 14, 3)
    pack_b2()
    b2 = copies_plane(BF)
    start(b2)

    def stage1(i, _):
        for j in range(5):
            T2[i, pl.ds(j, 8, stride=5), :] = jnp.where(
                lane < 64, V1[9 + i, j], pltpu.roll(V1[13 + i, j], 64, 1))
        for t in range(2):
            D1[VF, 1, i, 16 + 8 * t:24 + 8 * t, :] = T2[i, pl.ds(12 + 8 * t, 8, stride=1), :]
        return 0
    lax.fori_loop(0, 1, times(4, stage1), 0)
    pack1(VF)
    def stage0(x, _):
        for j in range(6):
            T0[x, pl.ds(j, 8, stride=6), :] = jnp.where(
                lane < 64, V0[8 + x, 0, j], pltpu.roll(V0[8 + x, 1, j], 64, 1))
        D0[VF, 8 + x, 8:40, :] = T0[x, 8:40, :]
        return 0
    lax.fori_loop(0, 4, times(4, stage0), 0)
    pack0(VF)
    wait_recv(b2)
    spread(BF)
    b2l = copies_line(BF)
    start(b2l)

    v1 = copies1(VF)
    start(v1)
    v0 = copies0(VF)
    start(v0)
    b2o = copies_on(BF)
    pass_on(b2l, b2o)
    for made in (k0, b0, k1, b1, k1f, k2, b2, k2l, k2o):
        wait_send(made)
    b2l[3].wait_recv()
    wait_recv(b2o)

    def load_b2(y, _):
        q = S2[y] * gathered(BF, y)
        Q2[y] = q
        V2[y + 1] = q
        return 0
    lax.fori_loop(0, 2, times(4, load_b2), 0)
    sweeps2(5)
    wait_recv(v1)
    assemble1(VF, W1)
    v1f = copies_far(W1, 1)
    start(v1f)

    edges(V2, 8)

    def restrict2(y, _):
        r = []
        for u in range(2):
            z = 2 * y + u
            cur = V2[z + 1]
            r.append((next2(z, cur, V2[z], V2[z + 2]) - cur) * I2[z])
        Q3[y] = fold(r) * S3[y]
        return 0
    lax.fori_loop(0, 2, times(2, restrict2), 0)
    v3 = lower_levels()
    for y in range(4):
        V3[y] = v3[y]

    def prolong2(y, _):
        for xl in range(4):
            for zl in range(4):
                V2[y + 1, xl, zl] = V2[y + 1, xl, zl] + V3[lax.div(y, 2), xl // 2, zl // 2]
        return 0
    lax.fori_loop(0, 2, times(4, prolong2), 0)
    sweeps2(6)

    def lay2(y, _):
        for xl in range(4):
            for zl in range(4):
                H2[pl.ds((xl * 4 + zl) * 8 + y, 8, stride=128), :] = V2[y + 1, xl, zl]
        return 0
    lax.fori_loop(0, 2, times(4, lay2), 0)
    planes = [(-2, 3)] + [(o, xl) for o in (-1, 0, 1) for xl in range(4)] + [(2, 0)]
    acc = None
    zf = jnp.where(ll < 96, ll, ll - 128)
    zc = lax.div(zf + 128, 2) - 64 + iz * 32
    for zl in range(4):
        left = []
        for o, xl in planes:
            at_x = jnp.clip(ix + o, 0, 7)
            left.append(H2[pl.ds(pl.multiple_of(at_x * 128 + (xl * 4 + zl) * 8, 8), 8), :])
        left = jnp.concatenate(left, axis=0)
        ok = (zc >= 0) & (zc < 128) & (lax.rem(zc + 128, 4) == zl)
        right = jnp.concatenate(
            [(ok & (cc == (iy + dy) * 32 + lax.div(zc, 4))).astype(F32) for dy in (-1, 0, 1)], axis=1)
        part = dot(left, right)
        acc = part if acc is None else acc + part
    for m in range(14):
        for d in range(3):
            v = acc[8 * m:8 * m + 8, 128 * d:128 * d + 128]
            F1[m, pl.ds(16 * d, 8, stride=2), :] = v
            F1[m, pl.ds(16 * d + 1, 8, stride=2), :] = v
    wait_recv(v1f)

    def start1(x, _):
        m = lax.div(x + 1, 2)
        for j in range(5):
            V1[x, j] = jnp.where(K1[x, j] > 0, W1[x, j] + F1[m, pl.ds(4 + j, 8, stride=5), :], 0.0)
        return 0
    lax.fori_loop(0, 2, times(13, start1), 0)
    sweeps1(1, 24, 3)
    sweeps1(4, 18, 3)

    wait_recv(v0)
    assemble0(VF, W0)
    def lay1(i, _):
        for j in range(5):
            F0[i, pl.ds(j, 8, stride=5), :] = V1[6 + i, j]
        return 0
    lax.fori_loop(0, 2, times(7, lay1), 0)

    def start0(i, _):
        for m in range(3):
            add = F0[i, pl.ds(8 + m, 8, stride=3), :]
            for u in range(2):
                x = 2 + 2 * i + u
                for p in range(2):
                    for o in range(2):
                        j = 2 * m + o
                        V0[x, p, j] = jnp.where(S0[x, p, j] > 0, W0[x, p, j] + add, 0.0)
        return 0
    lax.fori_loop(0, 7, times(2, start0), 0)
    sweeps0(6)

    join = (ll == jnp.where(cc < 64, 2 * cc, 2 * (cc - 64) + 1)).astype(F32)

    def finish(x, _):
        for j in range(6):
            T0[x, pl.ds(j, 8, stride=6), :] = jnp.where(
                lane < 64, V0[8 + x, 0, j], pltpu.roll(V0[8 + x, 1, j], 64, 1))
        return 0
    lax.fori_loop(0, 4, times(4, finish), 0)

    for i in range(4):
        d = T0[4 * i:4 * i + 4, 8:40, :].reshape(128, 128)
        out_ref[4 * i:4 * i + 4] = dot(d, join).reshape(4, 32, 128)
    for made in (v0, v1, v1f, b2l, b2o):
        wait_send(made)


def shards(source, conductivity):
    def vm(*shape):
        return pltpu.VMEM(shape, F32)

    def dma(n):
        return pltpu.SemaphoreType.DMA((n,))

    fine = (32, 2, 6, 8, 128)
    mid = (26, 5, 8, 128)
    low2, low3, low4 = (4, 4, 8, 128), (2, 2, 8, 128), (1, 1, 8, 128)
    scratch = [
        vm(2, 16, 32, 128), vm(3, 32, 48, 128), vm(3, 2, 32, 128), vm(3, 2, 4, 48, 128),
        vm(*fine), vm(*fine), vm(*fine), vm(32, 2, 8, 128), vm(*fine), vm(32, 6, 8, 128),
        vm(*fine), vm(*fine), vm(*fine), vm(*fine), vm(16, 48, 128),
        vm(3, 3, 4, 48, 128), vm(3, 2, 16, 128), vm(3, 2, 3, 2, 48, 128),
        vm(*mid), vm(*mid), vm(*mid), vm(26, 8, 128), vm(*mid), vm(*mid), vm(*mid), vm(*mid), vm(*mid), vm(*mid),
        vm(4, 32, 128), vm(4, 40, 128), vm(14, 40, 128), vm(14, 48, 128),
        vm(2, 8, 128), vm(2, 16, 8, 128), vm(2, 1024, 128), vm(1024, 128),
        vm(10, *low2), vm(10, *low2), vm(6, 8, *low2), vm(8, *low2), vm(8, *low2), vm(8, *low2),
        vm(6, *low3), vm(4, *low3), vm(6, 4, *low3), vm(4, *low3), vm(4, *low3), vm(4, *low3),
        vm(4, *low4), vm(6, 2, *low4), vm(2, *low4), vm(2, *low4),
        dma(2), dma(78), dma(78), dma(78), dma(78), dma(4), dma(4), dma(30), dma(30), dma(14), dma(14),
    ]
    return pl.pallas_call(
        kernel,
        out_shape=jax.ShapeDtypeStruct((16, 32, 128), F32),
        in_specs=[pl.BlockSpec(memory_space=pl.ANY)] * 2,
        out_specs=pl.BlockSpec(memory_space=pltpu.VMEM),
        scratch_shapes=scratch,
        compiler_params=pltpu.CompilerParams(
            collective_id=0, has_side_effects=True, vmem_limit_bytes=62 * 1024 * 1024),
    )(source, conductivity)


def solution(mesh):
    spec = P("gx", "gy", "gz")
    return jax.shard_map(shards, mesh=mesh, in_specs=(spec, spec), out_specs=spec, check_vma=False)
```

```python
import jax
import jax.numpy as jnp
from jax import lax
from jax.experimental import pallas as pl
from jax.experimental.pallas import tpu as pltpu
from jax.sharding import PartitionSpec as P

MESH = pl.DeviceIdType.MESH
F32 = jnp.float32
HI = lax.Precision.HIGHEST
DAMPING = 0.8

U0 = 4
UC0 = 3
UC1 = 6

KF, BF, VF = 0, 1, 2
NEAR = [(a, b, c) for a in (-1, 0, 1) for b in (-1, 0, 1) for c in (-1, 0, 1) if (a, b, c) != (0, 0, 0)]
PLANE = [(0, b, c) for b in range(4) for c in range(4) if (b, c) != (0, 0)]
LINE = [(a, 0, 0) for a in range(1, 8)]
PEERS = sorted({(a % 8, b % 4, c % 4) for a, b, c in NEAR + PLANE + LINE})


def iota(shape, dim):
    return lax.broadcasted_iota(jnp.int32, shape, dim)


def roll(v, amount, axis):
    shape = v.shape
    if axis == -1:
        return pltpu.roll(v.reshape(-1, 128), amount % 128, 1).reshape(shape)
    return pltpu.roll(v.reshape(-1, 8, 128), amount % 8, 1).reshape(shape)


def shifted(v, axis, step, edge):
    n = v.shape[axis]
    if n == 1:
        return edge
    if step > 0:
        return jnp.concatenate([lax.slice_in_dim(v, 1, n, axis=axis), edge], axis=axis)
    return jnp.concatenate([edge, lax.slice_in_dim(v, 0, n - 1, axis=axis)], axis=axis)


def up(v):
    return jnp.concatenate([v[1:], roll(v[:1], -1, -2)], axis=0)


def down(v):
    return jnp.concatenate([roll(v[-1:], 1, -2), v[:-1]], axis=0)


def dot3(a, b):
    hi = a.astype(jnp.bfloat16)
    rest = a - hi.astype(F32)
    mid = rest.astype(jnp.bfloat16)
    low = (rest - mid.astype(F32)).astype(jnp.bfloat16)
    return sum(jnp.dot(p, b, preferred_element_type=F32) for p in (low, mid, hi))


def times(count, step):
    def body(i, carry):
        for u in range(count):
            step(i * count + u, 0)
        return carry
    return body


def dot(a, b):
    return jnp.dot(a, b, precision=HI, preferred_element_type=F32)


def kernel(
    src_hbm, cond_hbm, out_ref,
    raw, D0, Z0s, Z0r, K0, CX0, CY0, CYM0, CZ0, CZM0, S0, B0, V0, W0, T0,
    D1, Z1s, Z1r, K1, CX1, CY1, CYM1, CZ1, CZM1, S1, B1, V1, W1, T1, T2, F0, F1,
    P2s, R2, G2, H2, K2, V2, A2, S2, I2, Q2, K3, V3, A3, S3, I3, Q3, K4, A4, S4, Q4,
    raw_sem, s0s, s0r, s1s, s1r, xs, xr, g1s, g1r, g2s, g2r,
):
    ix, iy, iz = lax.axis_index("gx"), lax.axis_index("gy"), lax.axis_index("gz")
    lane = iota((8, 128), 1)
    row = iota((8, 128), 0)

    steps = {}

    def moved(axis, place, step, size):
        if not isinstance(step, int):
            return place + step
        key = (axis, step % size)
        if key not in steps:
            steps[key] = lax.rem(place + step % size, size) if step % size else place
        return steps[key]

    def at(offset):
        a, b, c = offset
        return (moved(0, ix, a, 8), moved(1, iy, b, 4), moved(2, iz, c, 4))

    def remote(src, dst, send, recv, offset):
        return pltpu.make_async_remote_copy(
            src_ref=src, dst_ref=dst, send_sem=send, recv_sem=recv, device_id=at(offset), device_id_type=MESH)

    loads = [pltpu.make_async_copy(cond_hbm, raw.at[0], raw_sem.at[0]),
             pltpu.make_async_copy(src_hbm, raw.at[1], raw_sem.at[1])]
    for c in loads:
        c.start()
    barrier = pltpu.get_barrier_semaphore()
    for offset in PEERS:
        pl.semaphore_signal(barrier, inc=1, device_id=at(offset), device_id_type=MESH)

    def copies0(f):
        reach = 7 if f == KF else 6
        made = []
        for n, (dx, dy, dz) in enumerate(NEAR):
            n_x = reach - (dy != 0) - (dz != 0)
            n_y = reach - (dx != 0) - (dz != 0)
            sx, tx, cx = {0: (8, 8, 16), -1: (8, 24, n_x), 1: (24 - n_x, 8 - n_x, n_x)}[dx]
            sr, tr, cr = {0: (8, 8, 32), -1: (8, 40, n_y), 1: (40 - n_y, 8 - n_y, n_y)}[dy]
            if dz == 0:
                src = D0.at[f, pl.ds(sx, cx), pl.ds(sr, cr)]
                dst = D0.at[f, pl.ds(tx, cx), pl.ds(tr, cr)]
            else:
                side = 0 if dz == -1 else 1
                sh, th, ch = {0: (0, 1, 2), -1: (0, 3, 1), 1: (1, 0, 1)}[dx]
                src = Z0s.at[f, pl.ds(sh, ch), pl.ds(sr - 8, cr)]
                dst = Z0r.at[f, side, pl.ds(th, ch), pl.ds(tr, cr)]
            made.append(remote(src, dst, s0s.at[f * 26 + n], s0r.at[f * 26 + n], (dx, dy, dz)))
        return made

    def copies1(f):
        made = []
        for n, (dx, dy, dz) in enumerate(NEAR):
            n_y = 8 if f == BF else 9
            sr, tr, cr = {0: (16, 16, 16), -1: (16, 32, n_y), 1: (32 - n_y, 16 - n_y, n_y)}[dy]
            if dz == 0:
                src = D1.at[f, 1, :, pl.ds(sr, cr)]
                dst = D1.at[f, 1 - dx, :, pl.ds(tr, cr)]
            else:
                side = 0 if dz == -1 else 1
                src = Z1s.at[f, :, pl.ds(sr - 16, cr)]
                dst = Z1r.at[f, side, 1 - dx, :, pl.ds(tr, cr)]
            made.append(remote(src, dst, s1s.at[f * 26 + n], s1r.at[f * 26 + n], (dx, dy, dz)))
        return made

    def copies_far(ref, f):
        return [remote(ref.at[8], ref.at[0], xs.at[2 * f], xr.at[2 * f], (1, 0, 0)),
                remote(ref.at[17], ref.at[25], xs.at[2 * f + 1], xr.at[2 * f + 1], (-1, 0, 0))]

    here = iy * 4 + iz

    def copies_plane(f):
        return [remote(P2s.at[f], R2.at[f, here], g1s.at[f * 15 + n], g1r.at[f * 15 + n], o)
                for n, o in enumerate(PLANE)]

    slab = pl.ds(pl.multiple_of(ix * 128, 128), 128)

    other = 1 - 2 * lax.rem(ix, 2)

    def copies_line(f):
        return [remote(G2.at[f, slab], G2.at[f, slab], g2s.at[f * 7 + n], g2r.at[f * 7 + n], (o, 0, 0))
                for n, o in enumerate((2, 6, 4, other))]

    def copies_on(f):
        made = []
        for n, o in enumerate((2, 6, 4)):
            rows = pl.ds(pl.multiple_of(lax.rem(ix + 8 - o, 8) * 128, 128), 128)
            made.append(remote(G2.at[f, rows], G2.at[f, rows], g2s.at[f * 7 + 4 + n], g2r.at[f * 7 + 4 + n], (other, 0, 0)))
        return made

    def pass_on(made, onward):
        for c, d in zip(made, onward):
            c.wait_recv()
            d.start()

    def start(made):
        for c in made:
            c.start()

    def wait_recv(made):
        for c in made:
            c.wait_recv()

    def wait_send(made):
        for c in made:
            c.wait_send()

    cc, ll = iota((128, 128), 0), iota((128, 128), 1)
    split = (cc == jnp.where(ll < 64, 2 * ll, 2 * (ll - 64) + 1)).astype(F32)
    lane32 = iota((32, 128), 1)
    lane16 = iota((16, 128), 1)

    def permute_in(f):
        for i in range(4):
            x = raw[f, 4 * i:4 * i + 4].reshape(128, 128)
            D0[f, 8 + 4 * i:12 + 4 * i, 8:40, :] = dot(x, split).reshape(4, 32, 128)

    even_strip = (lane32 < 4) | ((lane32 >= 60) & (lane32 < 64))
    odd_strip = ((lane32 >= 64) & (lane32 < 68)) | (lane32 >= 124)

    def pack0(f):
        for h in range(2):
            total = None
            for xi in range(8):
                d = D0[f, 8 + 8 * h + xi, 8:40, :]
                part = (pltpu.roll(jnp.where(even_strip, d, 0.0), (16 * xi) % 128, 1)
                        + pltpu.roll(jnp.where(odd_strip, d, 0.0), (16 * xi + 72) % 128, 1))
                total = part if total is None else total + part
            Z0s[f, h] = total

    ring0 = (lane < 64) | ((lane < 68) & (iz < 3)) | ((lane >= 124) & (iz > 0))
    even4 = lax.rem(lax.div(lane, 4), 2) == 0

    def assemble0(f, dst):
        def body(xh, _):
            for j in range(6):
                rows = pl.ds(j, 8, stride=6)
                c = jnp.where(even4, Z0r[f, 0, xh, rows, :], Z0r[f, 1, xh, rows, :])
                mask = ring0
                if f == KF:
                    y = row * 6 + j + (iy * 32 - 8)
                    xb = ix * 2 + xh - 1
                    mask = mask & (y >= 0) & (y < 128) & (xb >= 0) & (xb < 16)
                for xi in range(8):
                    x = xh * 8 + xi
                    d = D0[f, x, rows, :]
                    full = mask
                    if f == KF and xi in (0, 7):
                        full = mask & (x > 0) & (x < 31)
                    for p in range(2):
                        main = d if p == 0 else pltpu.roll(d, 64, 1)
                        halo = pltpu.roll(c, (64 - 16 * xi - 8 * p) % 128, 1)
                        dst[x, p, j] = jnp.where(full, jnp.where(lane < 64, main, halo), 0.0)
            return 0
        lax.fori_loop(0, 4, body, 0)

    def coefs0():
        def body(q, carry):
            (ke, ko), lower = carry
            for u in range(UC0):
                x = 1 + UC0 * q + u
                ne, no = K0[x + 1, 0], K0[x + 1, 1]
                xe, xo = 0.5 * (ke + ne), 0.5 * (ko + no)
                ye, yo = 0.5 * (ke + up(ke)), 0.5 * (ko + up(ko))
                me, mo = 0.5 * (ke[:1] + roll(ke[-1:], 1, -2)), 0.5 * (ko[:1] + roll(ko[-1:], 1, -2))
                ze, zo = 0.5 * (ke + ko), 0.5 * (ko + roll(ke, -1, -1))
                zm = 0.5 * (ke + roll(ko, 1, -1))
                de = xe + lower[0] + ye + jnp.concatenate([me, ye[:-1]], axis=0) + ze + zm
                do = xo + lower[1] + yo + jnp.concatenate([mo, yo[:-1]], axis=0) + zo + ze
                CX0[x, 0], CX0[x, 1] = xe, xo
                CY0[x, 0], CY0[x, 1] = ye, yo
                CYM0[x, 0], CYM0[x, 1] = me[0], mo[0]
                CZ0[x, 0], CZ0[x, 1] = ze, zo
                CZM0[x] = zm
                S0[x, 0] = jnp.where(ke > 0, DAMPING / de, 0.0)
                S0[x, 1] = jnp.where(ko > 0, DAMPING / do, 0.0)
                ke, ko, lower = ne, no, (xe, xo)
            return (ke, ko), lower
        first = (K0[1, 0], K0[1, 1])
        lax.fori_loop(0, 30 // UC0, body, (first, (0.5 * first[0], 0.5 * first[1])))

    def flow0(x, c, n, low):
        ce, co = c
        fe, fo = CX0[x, 0] * (n[0] - ce), CX0[x, 1] * (n[1] - co)
        ye, yo = CY0[x, 0] * (up(ce) - ce), CY0[x, 1] * (up(co) - co)
        me = CYM0[x, 0][None] * (ce[:1] - roll(ce[-1:], 1, -2))
        mo = CYM0[x, 1][None] * (co[:1] - roll(co[-1:], 1, -2))
        ze = CZ0[x, 0] * (co - ce)
        zo, zm = CZ0[x, 1] * (roll(ce, -1, -1) - co), CZM0[x] * (ce - roll(co, 1, -1))
        re = B0[x, 0] + ((fe - low[0]) + (ye - jnp.concatenate([me, ye[:-1]], axis=0)) + (ze - zm))
        ro = B0[x, 1] + ((fo - low[1]) + (yo - jnp.concatenate([mo, yo[:-1]], axis=0)) + (zo - ze))
        return (re, ro), (fe, fo)

    def pair0(x):
        return V0[x, 0], V0[x, 1]

    def first0(x):
        c, n = pair0(x - 1), pair0(x)
        return CX0[x - 1, 0] * (n[0] - c[0]), CX0[x - 1, 1] * (n[1] - c[1])

    def sweeps0(start, count):
        def sweep(i, _):
            lo = start + i
            def body(q, carry):
                c, low = carry
                ahead = [pair0(lo + U0 * q + u + 1) for u in range(U0)]
                for u in range(U0):
                    x = lo + U0 * q + u
                    n = ahead[u]
                    r, low = flow0(x, c, n, low)
                    V0[x, 0] = c[0] + S0[x, 0] * r[0]
                    V0[x, 1] = c[1] + S0[x, 1] * r[1]
                    c = n
                return c, low
            lax.fori_loop(0, lax.div(32 - 2 * lo + (U0 - 1), U0), body, (pair0(lo), first0(lo)))
            return 0
        lax.fori_loop(0, count, sweep, 0)

    def restrict_k1():
        def body(i, _):
            for t in range(2):
                parts = []
                for base in (8, 16):
                    x = base + 2 * i
                    a = None
                    for u in range(2):
                        for o in range(2):
                            d = D0[KF, x + u, pl.ds(8 + 16 * t + o, 8, stride=2), :]
                            a = d if a is None else a + d
                    parts.append((a + pltpu.roll(a, 64, 1)) * 0.125)
                D1[KF, 1, i, 16 + 8 * t:24 + 8 * t, :] = jnp.where(lane < 64, parts[0], parts[1])
            return 0
        lax.fori_loop(0, 4, body, 0)

    def restrict_b1():
        def coarse(x):
            total = None
            low = first0(x)
            c = pair0(x)
            for u in range(2):
                n = pair0(x + u + 1)
                r, low = flow0(x + u, c, n, low)
                c = n
                part = r[0] + r[1]
                total = part if total is None else total + part
            return [(total[2 * m] + total[2 * m + 1]) * 0.125 for m in range(3)]
        def body(i, _):
            a, b = coarse(8 + 2 * i), coarse(16 + 2 * i)
            for m in range(3):
                T1[i, pl.ds(4 + m, 8, stride=3), :] = jnp.where(lane < 64, a[m], pltpu.roll(b[m], 64, 1))
            return 0
        lax.fori_loop(0, 4, body, 0)
        D1[BF, 1, :, 16:32, :] = T1[:, 8:24, :]

    low_strip = (lane16 < 16) | ((lane16 >= 48) & (lane16 < 64))
    high_strip = ((lane16 >= 64) & (lane16 < 80)) | (lane16 >= 112)

    def pack1(f):
        for h, strip in ((0, low_strip), (1, high_strip)):
            total = None
            for u in range(4):
                d = D1[f, 1, u, 16:32, :]
                part = pltpu.roll(jnp.where(strip, d, 0.0), (64 * h + 32 * u) % 128, 1)
                total = part if total is None else total + part
            Z1s[f, h] = total

    ring1 = (lane < 64) | ((lane < 80) & (iz < 3)) | ((lane >= 112) & (iz > 0))
    even16 = lax.rem(lax.div(lane, 16), 2) == 0

    def assemble1(f, dst):
        def body(g, _):
            for j in range(5):
                rows = pl.ds(4 + j, 8, stride=5)
                c = [jnp.where(even16, Z1r[f, 0, g, h, rows, :], Z1r[f, 1, g, h, rows, :]) for h in range(2)]
                mask = ring1
                if f == KF:
                    y = row * 5 + j + (iy * 16 - 12)
                    xb = ix + g - 1
                    mask = mask & (y >= 0) & (y < 64) & (xb >= 0) & (xb < 8)
                for xl in range(8):
                    d = D1[f, g, xl % 4, rows, :]
                    main = d if xl < 4 else pltpu.roll(d, 64, 1)
                    halo = pltpu.roll(c[xl // 4], (64 - 32 * (xl % 4)) % 128, 1)
                    dst[1 + g * 8 + xl, j] = jnp.where(mask, jnp.where(lane < 64, main, halo), 0.0)
            return 0
        lax.fori_loop(0, 3, body, 0)

    HW1 = 0.5 * 0.25

    def coefs1():
        def body(q, lower):
            for u in range(UC1):
                x = 1 + UC1 * q + u
                k, n = K1[x], K1[x + 1]
                cx, cy, cz = HW1 * (k + n), HW1 * (k + up(k)), HW1 * (k + roll(k, -1, -1))
                ym, zm = HW1 * (k[:1] + roll(k[-1:], 1, -2)), HW1 * (k + roll(k, 1, -1))
                d = cx + lower + cy + jnp.concatenate([ym, cy[:-1]], axis=0) + cz + zm
                CX1[x], CY1[x], CYM1[x], CZ1[x], CZM1[x] = cx, cy, ym[0], cz, zm
                S1[x] = jnp.where(k > 0, DAMPING / d, 0.0)
                lower = cx
            return lower
        c0 = HW1 * (K1[0] + K1[1])
        CX1[0] = c0
        lax.fori_loop(0, 24 // UC1, body, c0)

    def flow1(x, c, n, low):
        f = CX1[x] * (n - c)
        y = CY1[x] * (up(c) - c)
        ym = CYM1[x][None] * (c[:1] - roll(c[-1:], 1, -2))
        z, zm = CZ1[x] * (roll(c, -1, -1) - c), CZM1[x] * (c - roll(c, 1, -1))
        return B1[x] + ((f - low) + (y - jnp.concatenate([ym, y[:-1]], axis=0)) + (z - zm)), f

    def sweeps1(lo, planes, count):
        def sweep(i, _):
            c = V1[lo]
            low = CX1[lo - 1] * (c - V1[lo - 1])
            for x in range(lo, lo + planes):
                n = V1[x + 1]
                r, low = flow1(x, c, n, low)
                V1[x] = c + S1[x] * r
                c = n
            return 0
        lax.fori_loop(0, count, sweep, 0)

    def pick(xl):
        q = lax.rem(ll, 32)
        z = lax.rem(q, 8) * 4 + lax.div(q, 8)
        return ((lax.div(ll, 32) == xl) & (lax.div(cc, 2) == z)).astype(F32)

    picks = [pick(xl) for xl in range(4)]

    def pack_k2():
        total = None
        for h in range(2):
            a = None
            for u in range(2):
                for o in range(2):
                    d = D1[KF, 1, 2 * h + u, pl.ds(16 + o, 8, stride=2), :]
                    a = d if a is None else a + d
            a = a * 0.125
            part = dot(a, picks[h]) + dot(pltpu.roll(a, 64, 1), picks[2 + h])
            total = part if total is None else total + part
        P2s[KF] = total
        R2[KF, here] = total

    def pack_b2():
        for xl in range(4):
            x = 9 + 2 * xl
            total = None
            c = V1[x]
            low = CX1[x - 1] * (c - V1[x - 1])
            for u in range(2):
                n = V1[x + u + 1]
                r, low = flow1(x + u, c, n, low)
                c = n
                total = r if total is None else total + r
            for j in range(5):
                T2[xl, pl.ds(j, 8, stride=5), :] = total[j]
        total = None
        for xl in range(4):
            a = (T2[xl, pl.ds(12, 8, stride=2), :] + T2[xl, pl.ds(13, 8, stride=2), :]) * 0.125
            part = dot(a, picks[xl])
            total = part if total is None else total + part
        P2s[BF] = total
        R2[BF, here] = total

    def spread(f):
        v = [R2[f, g] for g in range(16)]
        for bit in (1, 2, 4, 8):
            clear = lax.rem(lax.div(lane, 8 * bit), 2) == 0
            for r in range(16):
                if r & bit:
                    continue
                a, d = v[r], v[r | bit]
                v[r] = jnp.where(clear, a, pltpu.roll(d, 8 * bit, 1))
                v[r | bit] = jnp.where(clear, pltpu.roll(a, 128 - 8 * bit, 1), d)
        for q in range(16):
            G2[f, pl.ds(pl.multiple_of(ix * 128 + q * 8, 8), 8), :] = v[q]

    def gathered(f, yl):
        rows = []
        for xl in range(4):
            rows.append(jnp.stack([G2[f, pl.ds((xl * 4 + zl) * 8 + yl, 8, stride=128), :] for zl in range(4)], 0))
        return jnp.stack(rows, 0)

    def edges(ref, ny):
        ref[0] = jnp.where(lane >= 32, roll(ref[ny], 32, -1), 0.0)
        ref[ny + 1] = jnp.where(lane < 96, roll(ref[1], -32, -1), 0.0)

    def around(v):
        xp = shifted(v, 0, 1, roll(v[:1], -1, -2))
        xm = shifted(v, 0, -1, roll(v[-1:], 1, -2))
        zp = shifted(v, 1, 1, roll(v[:, :1], -1, -1))
        zm = shifted(v, 1, -1, roll(v[:, -1:], 1, -1))
        return xp, xm, zp, zm

    z_top, z_end = lax.rem(lane, 32) == 31, lax.rem(lane, 32) == 0

    def inside(k):
        xp = shifted(k, 0, 1, jnp.where(row == 7, 0.0, roll(k[:1], -1, -2)))
        xm = shifted(k, 0, -1, jnp.where(row == 0, 0.0, roll(k[-1:], 1, -2)))
        zp = shifted(k, 1, 1, jnp.where(z_top, 0.0, roll(k[:, :1], -1, -1)))
        zm = shifted(k, 1, -1, jnp.where(z_end, 0.0, roll(k[:, -1:], 1, -1)))
        return xp, xm, zp, zm

    def coefs_low(level, K, A, S, I, ny):
        hw = 0.5 * 0.25 ** level
        edges(K, ny)
        def body(y, _):
            k = K[y + 1]
            near = inside(k) + (K[y + 2], K[y])
            c = [hw * (k + n) for n in near]
            d = ((c[0] + c[1]) + (c[2] + c[3])) + (c[4] + c[5])
            s = DAMPING / d
            S[y] = s
            if I is not None:
                I[y] = d * (1.0 / DAMPING)
            for m in range(6):
                A[m, y] = jnp.where(near[m] > 0, s * c[m], 0.0)
            return 0
        lax.fori_loop(0, ny // 2, times(2, body), 0)

    def fold(blocks):
        t = blocks[0] + blocks[1]
        t = t.reshape((t.shape[0] // 2, 2) + t.shape[1:])
        t = t[:, 0] + t[:, 1]
        t = t.reshape((t.shape[0], t.shape[1] // 2, 2) + t.shape[2:])
        return (t[:, :, 0] + t[:, :, 1]) * 0.125

    def load_k2():
        def body(y, _):
            K2[y + 1] = gathered(KF, y)
            return 0
        lax.fori_loop(0, 2, times(4, body), 0)
        coefs_low(2, K2, A2, S2, I2, 8)
        def body3(y, _):
            K3[y + 1] = fold([K2[2 * y + 1], K2[2 * y + 2]])
            return 0
        lax.fori_loop(0, 1, times(4, body3), 0)
        coefs_low(3, K3, A3, S3, I3, 4)
        for y in range(2):
            K4[y + 1] = fold([K3[2 * y + 1], K3[2 * y + 2]])
        coefs_low(4, K4, A4, S4, None, 2)

    def next2(y, cur, before, after):
        xp, xm, zp, zm = around(cur)
        t = 0.2 * cur + Q2[y]
        t = t + A2[0, y] * xp + A2[1, y] * xm
        t = t + A2[2, y] * zp + A2[3, y] * zm
        return t + (A2[4, y] * after + A2[5, y] * before)

    def sweeps2(count):
        def sweep(i, _):
            edges(V2, 8)
            before = V2[0]
            for y in range(8):
                cur = V2[y + 1]
                V2[y + 1] = next2(y, cur, before, V2[y + 2])
                before = cur
            return 0
        lax.fori_loop(0, count, sweep, 0)

    def next_whole(v, a, g, ny):
        first = roll(v[ny - 1], 32, -1)
        last = roll(v[0], -32, -1)
        out = []
        for y in range(ny):
            xp, xm, zp, zm = around(v[y])
            yp = v[y + 1] if y + 1 < ny else last
            ym = v[y - 1] if y else first
            t = (0.2 * v[y] + g(y)) + (a(0, y) * xp + a(1, y) * xm)
            out.append(t + ((a(2, y) * zp + a(3, y) * zm) + (a(4, y) * yp + a(5, y) * ym)))
        return out

    def a3(m, y):
        return A3[m, y]

    def g3(y):
        return Q3[y]

    def sweeps3(v, count):
        return lax.fori_loop(0, count, lambda i, w: tuple(next_whole(list(w), a3, g3, 4)), tuple(v))

    def lower_levels():
        v = sweeps3([Q3[y] for y in range(4)], 5)
        w = next_whole(list(v), a3, g3, 4)
        r = [(w[y] - v[y]) * I3[y] for y in range(4)]
        g4 = [fold(r[2 * y:2 * y + 2]) * S4[y] for y in range(2)]
        a4 = [[A4[m, y] for y in range(2)] for m in range(6)]
        c = lax.fori_loop(
            0, 15, lambda i, w: tuple(next_whole(list(w), lambda m, y: a4[m][y], lambda y: g4[y], 2)), tuple(g4))
        v = [v[y] + c[y // 2] for y in range(4)]
        return sweeps3(v, 6)

    loads[0].wait()
    permute_in(KF)
    pack0(KF)
    loads[1].wait()
    permute_in(BF)
    pack0(BF)
    pl.semaphore_wait(barrier, len(PEERS))
    k0 = copies0(KF)
    start(k0)
    b0 = copies0(BF)
    start(b0)

    restrict_k1()
    pack1(KF)
    k1 = copies1(KF)
    start(k1)
    pack_k2()
    k2 = copies_plane(KF)
    start(k2)

    wait_recv(k0)
    assemble0(KF, K0)
    coefs0()
    wait_recv(b0)
    assemble0(BF, B0)

    def first_sweep0(x, _):
        V0[2 + x] = S0[2 + x] * B0[2 + x]
        return 0
    lax.fori_loop(0, 7, times(4, first_sweep0), 0)
    sweeps0(3, 5)
    restrict_b1()
    pack1(BF)
    b1 = copies1(BF)
    start(b1)

    wait_recv(k1)
    assemble1(KF, K1)
    k1f = copies_far(K1, 0)
    start(k1f)
    wait_recv(k2)
    spread(KF)
    k2l = copies_line(KF)
    start(k2l)
    def stage0(x, _):
        for j in range(6):
            T0[x, pl.ds(j, 8, stride=6), :] = jnp.where(
                lane < 64, V0[8 + x, 0, j], pltpu.roll(V0[8 + x, 1, j], 64, 1))
        D0[VF, 8 + x, 8:40, :] = T0[x, 8:40, :]
        return 0
    lax.fori_loop(0, 4, times(4, stage0), 0)
    pack0(VF)
    v0 = copies0(VF)
    start(v0)
    wait_recv(k1f)
    coefs1()

    wait_recv(b1)
    assemble1(BF, B1)

    def first_sweep1(x, _):
        V1[3 + x] = S1[3 + x] * B1[3 + x]
        return 0
    lax.fori_loop(0, 2, times(10, first_sweep1), 0)
    sweeps1(4, 18, 2)
    sweeps1(6, 14, 3)
    pack_b2()
    b2 = copies_plane(BF)
    start(b2)

    def stage1(i, _):
        for j in range(5):
            T2[i, pl.ds(j, 8, stride=5), :] = jnp.where(
                lane < 64, V1[9 + i, j], pltpu.roll(V1[13 + i, j], 64, 1))
        for t in range(2):
            D1[VF, 1, i, 16 + 8 * t:24 + 8 * t, :] = T2[i, pl.ds(12 + 8 * t, 8, stride=1), :]
        return 0
    lax.fori_loop(0, 1, times(4, stage1), 0)
    pack1(VF)
    k2o = copies_on(KF)
    pass_on(k2l, k2o)
    wait_recv(b2)
    spread(BF)
    b2l = copies_line(BF)
    start(b2l)

    v1 = copies1(VF)
    start(v1)
    k2l[3].wait_recv()
    wait_recv(k2o)
    load_k2()
    for made in (k0, b0, k1, b1, k1f, k2, b2, k2l, k2o):
        wait_send(made)
    wait_recv(v0)
    b2o = copies_on(BF)
    pass_on(b2l, b2o)
    assemble0(VF, W0)
    wait_send(v0)
    b2l[3].wait_recv()
    wait_recv(b2o)

    def load_b2(y, _):
        q = S2[y] * gathered(BF, y)
        Q2[y] = q
        V2[y + 1] = q
        return 0
    lax.fori_loop(0, 2, times(4, load_b2), 0)
    sweeps2(5)
    wait_recv(v1)
    assemble1(VF, W1)
    v1f = copies_far(W1, 1)
    start(v1f)

    edges(V2, 8)

    def restrict2(y, _):
        r = []
        for u in range(2):
            z = 2 * y + u
            cur = V2[z + 1]
            r.append((next2(z, cur, V2[z], V2[z + 2]) - cur) * I2[z])
        Q3[y] = fold(r) * S3[y]
        return 0
    lax.fori_loop(0, 2, times(2, restrict2), 0)
    v3 = lower_levels()
    for y in range(4):
        V3[y] = v3[y]

    def prolong2(y, _):
        for xl in range(4):
            for zl in range(4):
                V2[y + 1, xl, zl] = V2[y + 1, xl, zl] + V3[lax.div(y, 2), xl // 2, zl // 2]
        return 0
    lax.fori_loop(0, 2, times(4, prolong2), 0)
    sweeps2(6)

    def lay2(y, _):
        for xl in range(4):
            for zl in range(4):
                H2[pl.ds((xl * 4 + zl) * 8 + y, 8, stride=128), :] = V2[y + 1, xl, zl]
        return 0
    lax.fori_loop(0, 2, times(4, lay2), 0)
    planes = [(-2, 3)] + [(o, xl) for o in (-1, 0, 1) for xl in range(4)] + [(2, 0)]
    acc = None
    zf = jnp.where(ll < 96, ll, ll - 128)
    zc = lax.div(zf + 128, 2) - 64 + iz * 32
    for zl in range(4):
        left = []
        for o, xl in planes:
            at_x = jnp.clip(ix + o, 0, 7)
            left.append(H2[pl.ds(pl.multiple_of(at_x * 128 + (xl * 4 + zl) * 8, 8), 8), :])
        left = jnp.concatenate(left, axis=0)
        ok = (zc >= 0) & (zc < 128) & (lax.rem(zc + 128, 4) == zl)
        right = jnp.concatenate(
            [(ok & (cc == (iy + dy) * 32 + lax.div(zc, 4))).astype(F32) for dy in (-1, 0, 1)], axis=1)
        part = dot3(left, right.astype(jnp.bfloat16))
        acc = part if acc is None else acc + part
    for m in range(14):
        for d in range(3):
            v = acc[8 * m:8 * m + 8, 128 * d:128 * d + 128]
            F1[m, pl.ds(16 * d, 8, stride=2), :] = v
            F1[m, pl.ds(16 * d + 1, 8, stride=2), :] = v
    wait_recv(v1f)

    def start1(x, _):
        m = lax.div(x + 1, 2)
        for j in range(5):
            V1[x, j] = jnp.where(K1[x, j] > 0, W1[x, j] + F1[m, pl.ds(4 + j, 8, stride=5), :], 0.0)
        return 0
    lax.fori_loop(0, 2, times(13, start1), 0)
    sweeps1(1, 24, 3)
    sweeps1(4, 18, 3)

    def lay1(i, _):
        for j in range(5):
            F0[i, pl.ds(j, 8, stride=5), :] = V1[6 + i, j]
        return 0
    lax.fori_loop(0, 2, times(7, lay1), 0)

    def start0(i, _):
        for m in range(3):
            add = F0[i, pl.ds(8 + m, 8, stride=3), :]
            for u in range(2):
                x = 2 + 2 * i + u
                for p in range(2):
                    for o in range(2):
                        j = 2 * m + o
                        V0[x, p, j] = jnp.where(S0[x, p, j] > 0, W0[x, p, j] + add, 0.0)
        return 0
    lax.fori_loop(0, 7, times(2, start0), 0)
    sweeps0(3, 6)

    join = (ll == jnp.where(cc < 64, 2 * cc, 2 * (cc - 64) + 1)).astype(F32).astype(jnp.bfloat16)

    def finish(x, _):
        for j in range(6):
            T0[x, pl.ds(j, 8, stride=6), :] = jnp.where(
                lane < 64, V0[8 + x, 0, j], pltpu.roll(V0[8 + x, 1, j], 64, 1))
        return 0
    lax.fori_loop(0, 4, times(4, finish), 0)

    for i in range(4):
        d = T0[4 * i:4 * i + 4, 8:40, :].reshape(128, 128)
        out_ref[4 * i:4 * i + 4] = dot3(d, join).reshape(4, 32, 128)
    for made in (v1, v1f, b2l, b2o):
        wait_send(made)


def shards(source, conductivity):
    def vm(*shape):
        return pltpu.VMEM(shape, F32)

    def dma(n):
        return pltpu.SemaphoreType.DMA((n,))

    fine = (32, 2, 6, 8, 128)
    mid = (26, 5, 8, 128)
    low2, low3, low4 = (4, 4, 8, 128), (2, 2, 8, 128), (1, 1, 8, 128)
    scratch = [
        vm(2, 16, 32, 128), vm(3, 32, 48, 128), vm(3, 2, 32, 128), vm(3, 2, 4, 48, 128),
        vm(*fine), vm(*fine), vm(*fine), vm(32, 2, 8, 128), vm(*fine), vm(32, 6, 8, 128),
        vm(*fine), vm(*fine), vm(*fine), vm(*fine), vm(16, 48, 128),
        vm(3, 3, 4, 48, 128), vm(3, 2, 16, 128), vm(3, 2, 3, 2, 48, 128),
        vm(*mid), vm(*mid), vm(*mid), vm(26, 8, 128), vm(*mid), vm(*mid), vm(*mid), vm(*mid), vm(*mid), vm(*mid),
        vm(4, 32, 128), vm(4, 40, 128), vm(14, 40, 128), vm(14, 48, 128),
        vm(2, 8, 128), vm(2, 16, 8, 128), vm(2, 1024, 128), vm(1024, 128),
        vm(10, *low2), vm(10, *low2), vm(6, 8, *low2), vm(8, *low2), vm(8, *low2), vm(8, *low2),
        vm(6, *low3), vm(4, *low3), vm(6, 4, *low3), vm(4, *low3), vm(4, *low3), vm(4, *low3),
        vm(4, *low4), vm(6, 2, *low4), vm(2, *low4), vm(2, *low4),
        dma(2), dma(78), dma(78), dma(78), dma(78), dma(4), dma(4), dma(30), dma(30), dma(14), dma(14),
    ]
    return pl.pallas_call(
        kernel,
        out_shape=jax.ShapeDtypeStruct((16, 32, 128), F32),
        in_specs=[pl.BlockSpec(memory_space=pltpu.HBM)] * 2,
        out_specs=pl.BlockSpec(memory_space=pltpu.VMEM),
        scratch_shapes=scratch,
        compiler_params=pltpu.CompilerParams(
            collective_id=0, has_side_effects=True, vmem_limit_bytes=62 * 1024 * 1024),
    )(source, conductivity)


def solution(mesh):
    spec = P("gx", "gy", "gz")
    return jax.shard_map(shards, mesh=mesh, in_specs=(spec, spec), out_specs=spec, check_vma=False)
```

```python
import jax
import jax.numpy as jnp
from jax import lax
from jax.experimental import pallas as pl
from jax.experimental.pallas import tpu as pltpu
from jax.sharding import PartitionSpec as P

MESH = pl.DeviceIdType.MESH
F32 = jnp.float32
HI = lax.Precision.HIGHEST
DAMPING = 0.8

U0 = 6
UC0 = 3
UC1 = 6

KF, BF, VF = 0, 1, 2
NEAR = [(a, b, c) for a in (-1, 0, 1) for b in (-1, 0, 1) for c in (-1, 0, 1) if (a, b, c) != (0, 0, 0)]
PLANE = [(0, b, c) for b in range(4) for c in range(4) if (b, c) != (0, 0)]
LINE = [(a, 0, 0) for a in range(1, 8)]
PEERS = sorted({(a % 8, b % 4, c % 4) for a, b, c in NEAR + PLANE + LINE})


def iota(shape, dim):
    return lax.broadcasted_iota(jnp.int32, shape, dim)


def roll(v, amount, axis):
    shape = v.shape
    if axis == -1:
        return pltpu.roll(v.reshape(-1, 128), amount % 128, 1).reshape(shape)
    return pltpu.roll(v.reshape(-1, 8, 128), amount % 8, 1).reshape(shape)


def shifted(v, axis, step, edge):
    n = v.shape[axis]
    if n == 1:
        return edge
    if step > 0:
        return jnp.concatenate([lax.slice_in_dim(v, 1, n, axis=axis), edge], axis=axis)
    return jnp.concatenate([edge, lax.slice_in_dim(v, 0, n - 1, axis=axis)], axis=axis)


def up(v):
    return jnp.concatenate([v[1:], roll(v[:1], -1, -2)], axis=0)


def down(v):
    return jnp.concatenate([roll(v[-1:], 1, -2), v[:-1]], axis=0)


def dot3(a, b):
    hi = a.astype(jnp.bfloat16)
    rest = a - hi.astype(F32)
    mid = rest.astype(jnp.bfloat16)
    low = (rest - mid.astype(F32)).astype(jnp.bfloat16)
    return sum(jnp.dot(p, b, preferred_element_type=F32) for p in (low, mid, hi))


def times(count, step):
    def body(i, carry):
        for u in range(count):
            step(i * count + u, 0)
        return carry
    return body


def dot(a, b):
    return jnp.dot(a, b, precision=HI, preferred_element_type=F32)


def kernel(
    src_hbm, cond_hbm, out_ref,
    raw, D0, Z0s, Z0r, K0, CX0, CY0, CYM0, CZ0, CZM0, S0, B0, V0, W0, T0,
    D1, Z1s, Z1r, K1, CX1, CY1, CYM1, CZ1, CZM1, S1, B1, V1, W1, T1, T2, F0, F1,
    P2s, R2, G2, H2, K2, V2, A2, S2, I2, Q2, K3, V3, A3, S3, I3, Q3, K4, A4, S4, Q4,
    raw_sem, s0s, s0r, s1s, s1r, xs, xr, g1s, g1r, g2s, g2r,
):
    ix, iy, iz = lax.axis_index("gx"), lax.axis_index("gy"), lax.axis_index("gz")
    lane = iota((8, 128), 1)
    row = iota((8, 128), 0)

    steps = {}

    def moved(axis, place, step, size):
        if not isinstance(step, int):
            return place + step
        key = (axis, step % size)
        if key not in steps:
            steps[key] = lax.rem(place + step % size, size) if step % size else place
        return steps[key]

    def at(offset):
        a, b, c = offset
        return (moved(0, ix, a, 8), moved(1, iy, b, 4), moved(2, iz, c, 4))

    def remote(src, dst, send, recv, offset):
        return pltpu.make_async_remote_copy(
            src_ref=src, dst_ref=dst, send_sem=send, recv_sem=recv, device_id=at(offset), device_id_type=MESH)

    loads = [pltpu.make_async_copy(cond_hbm, raw.at[0], raw_sem.at[0]),
             pltpu.make_async_copy(src_hbm, raw.at[1], raw_sem.at[1])]
    for c in loads:
        c.start()
    barrier = pltpu.get_barrier_semaphore()
    for offset in PEERS:
        pl.semaphore_signal(barrier, inc=1, device_id=at(offset), device_id_type=MESH)

    def copies0(f):
        reach = 7 if f == KF else 6
        made = []
        for n, (dx, dy, dz) in enumerate(NEAR):
            n_x = reach - (dy != 0) - (dz != 0)
            n_y = reach - (dx != 0) - (dz != 0)
            sx, tx, cx = {0: (8, 8, 16), -1: (8, 24, n_x), 1: (24 - n_x, 8 - n_x, n_x)}[dx]
            sr, tr, cr = {0: (8, 8, 32), -1: (8, 40, n_y), 1: (40 - n_y, 8 - n_y, n_y)}[dy]
            if dz == 0:
                src = D0.at[f, pl.ds(sx, cx), pl.ds(sr, cr)]
                dst = D0.at[f, pl.ds(tx, cx), pl.ds(tr, cr)]
            else:
                side = 0 if dz == -1 else 1
                sh, th, ch = {0: (0, 1, 2), -1: (0, 3, 1), 1: (1, 0, 1)}[dx]
                src = Z0s.at[f, pl.ds(sh, ch), pl.ds(sr - 8, cr)]
                dst = Z0r.at[f, side, pl.ds(th, ch), pl.ds(tr, cr)]
            made.append(remote(src, dst, s0s.at[f * 26 + n], s0r.at[f * 26 + n], (dx, dy, dz)))
        return made

    def copies1(f):
        made = []
        for n, (dx, dy, dz) in enumerate(NEAR):
            n_y = 8 if f == BF else 9
            sr, tr, cr = {0: (16, 16, 16), -1: (16, 32, n_y), 1: (32 - n_y, 16 - n_y, n_y)}[dy]
            if dz == 0:
                src = D1.at[f, 1, :, pl.ds(sr, cr)]
                dst = D1.at[f, 1 - dx, :, pl.ds(tr, cr)]
            else:
                side = 0 if dz == -1 else 1
                src = Z1s.at[f, :, pl.ds(sr - 16, cr)]
                dst = Z1r.at[f, side, 1 - dx, :, pl.ds(tr, cr)]
            made.append(remote(src, dst, s1s.at[f * 26 + n], s1r.at[f * 26 + n], (dx, dy, dz)))
        return made

    def copies_far(ref, f):
        return [remote(ref.at[8], ref.at[0], xs.at[2 * f], xr.at[2 * f], (1, 0, 0)),
                remote(ref.at[17], ref.at[25], xs.at[2 * f + 1], xr.at[2 * f + 1], (-1, 0, 0))]

    here = iy * 4 + iz

    def copies_plane(f):
        return [remote(P2s.at[f], R2.at[f, here], g1s.at[f * 15 + n], g1r.at[f * 15 + n], o)
                for n, o in enumerate(PLANE)]

    slab = pl.ds(pl.multiple_of(ix * 128, 128), 128)

    other = 1 - 2 * lax.rem(ix, 2)

    def copies_line(f):
        return [remote(G2.at[f, slab], G2.at[f, slab], g2s.at[f * 7 + n], g2r.at[f * 7 + n], (o, 0, 0))
                for n, o in enumerate((2, 6, 4, other))]

    def copies_on(f):
        made = []
        for n, o in enumerate((2, 6, 4)):
            rows = pl.ds(pl.multiple_of(lax.rem(ix + 8 - o, 8) * 128, 128), 128)
            made.append(remote(G2.at[f, rows], G2.at[f, rows], g2s.at[f * 7 + 4 + n], g2r.at[f * 7 + 4 + n], (other, 0, 0)))
        return made

    def pass_on(made, onward):
        for c, d in zip(made, onward):
            c.wait_recv()
            d.start()

    def start(made):
        for c in made:
            c.start()

    def wait_recv(made):
        for c in made:
            c.wait_recv()

    def wait_send(made):
        for c in made:
            c.wait_send()

    cc, ll = iota((128, 128), 0), iota((128, 128), 1)
    split = (cc == jnp.where(ll < 64, 2 * ll, 2 * (ll - 64) + 1)).astype(F32)
    lane32 = iota((32, 128), 1)
    lane16 = iota((16, 128), 1)

    def permute_in(f):
        for i in range(4):
            x = raw[f, 4 * i:4 * i + 4].reshape(128, 128)
            D0[f, 8 + 4 * i:12 + 4 * i, 8:40, :] = dot(x, split).reshape(4, 32, 128)

    even_strip = (lane32 < 4) | ((lane32 >= 60) & (lane32 < 64))
    odd_strip = ((lane32 >= 64) & (lane32 < 68)) | (lane32 >= 124)

    def pack0(f):
        for h in range(2):
            total = None
            for xi in range(8):
                d = D0[f, 8 + 8 * h + xi, 8:40, :]
                part = (pltpu.roll(jnp.where(even_strip, d, 0.0), (16 * xi) % 128, 1)
                        + pltpu.roll(jnp.where(odd_strip, d, 0.0), (16 * xi + 72) % 128, 1))
                total = part if total is None else total + part
            Z0s[f, h] = total

    ring0 = (lane < 64) | ((lane < 68) & (iz < 3)) | ((lane >= 124) & (iz > 0))
    even4 = lax.rem(lax.div(lane, 4), 2) == 0

    def assemble0(f, dst):
        def body(xh, _):
            for j in range(6):
                rows = pl.ds(j, 8, stride=6)
                c = jnp.where(even4, Z0r[f, 0, xh, rows, :], Z0r[f, 1, xh, rows, :])
                mask = ring0
                if f == KF:
                    y = row * 6 + j + (iy * 32 - 8)
                    xb = ix * 2 + xh - 1
                    mask = mask & (y >= 0) & (y < 128) & (xb >= 0) & (xb < 16)
                for xi in range(8):
                    x = xh * 8 + xi
                    d = D0[f, x, rows, :]
                    full = mask
                    if f == KF and xi in (0, 7):
                        full = mask & (x > 0) & (x < 31)
                    for p in range(2):
                        main = d if p == 0 else pltpu.roll(d, 64, 1)
                        halo = pltpu.roll(c, (64 - 16 * xi - 8 * p) % 128, 1)
                        value = jnp.where(full, jnp.where(lane < 64, main, halo), 0.0)
                        dst[x, p, j] = value
                        if f == BF:
                            V0[x, p, j] = S0[x, p, j] * value
            return 0
        lax.fori_loop(0, 4, body, 0)

    def coefs0():
        def body(q, carry):
            (ke, ko), lower = carry
            for u in range(UC0):
                x = 1 + UC0 * q + u
                ne, no = K0[x + 1, 0], K0[x + 1, 1]
                xe, xo = 0.5 * (ke + ne), 0.5 * (ko + no)
                ye, yo = 0.5 * (ke + up(ke)), 0.5 * (ko + up(ko))
                me, mo = 0.5 * (ke[:1] + roll(ke[-1:], 1, -2)), 0.5 * (ko[:1] + roll(ko[-1:], 1, -2))
                ze, zo = 0.5 * (ke + ko), 0.5 * (ko + roll(ke, -1, -1))
                zm = 0.5 * (ke + roll(ko, 1, -1))
                de = xe + lower[0] + ye + jnp.concatenate([me, ye[:-1]], axis=0) + ze + zm
                do = xo + lower[1] + yo + jnp.concatenate([mo, yo[:-1]], axis=0) + zo + ze
                CX0[x, 0], CX0[x, 1] = xe, xo
                CY0[x, 0], CY0[x, 1] = ye, yo
                CYM0[x, 0], CYM0[x, 1] = me[0], mo[0]
                CZ0[x, 0], CZ0[x, 1] = ze, zo
                CZM0[x] = zm
                S0[x, 0] = jnp.where(ke > 0, DAMPING / de, 0.0)
                S0[x, 1] = jnp.where(ko > 0, DAMPING / do, 0.0)
                ke, ko, lower = ne, no, (xe, xo)
            return (ke, ko), lower
        first = (K0[1, 0], K0[1, 1])
        lax.fori_loop(0, 30 // UC0, body, (first, (0.5 * first[0], 0.5 * first[1])))

    def flow0(x, c, n, low):
        ce, co = c
        fe, fo = CX0[x, 0] * (n[0] - ce), CX0[x, 1] * (n[1] - co)
        ye, yo = CY0[x, 0] * (up(ce) - ce), CY0[x, 1] * (up(co) - co)
        me = CYM0[x, 0][None] * (ce[:1] - roll(ce[-1:], 1, -2))
        mo = CYM0[x, 1][None] * (co[:1] - roll(co[-1:], 1, -2))
        ze = CZ0[x, 0] * (co - ce)
        zo, zm = CZ0[x, 1] * (roll(ce, -1, -1) - co), CZM0[x] * (ce - roll(co, 1, -1))
        re = B0[x, 0] + ((fe - low[0]) + (ye - jnp.concatenate([me, ye[:-1]], axis=0)) + (ze - zm))
        ro = B0[x, 1] + ((fo - low[1]) + (yo - jnp.concatenate([mo, yo[:-1]], axis=0)) + (zo - ze))
        return (re, ro), (fe, fo)

    def pair0(x):
        return V0[x, 0], V0[x, 1]

    def first0(x):
        c, n = pair0(x - 1), pair0(x)
        return CX0[x - 1, 0] * (n[0] - c[0]), CX0[x - 1, 1] * (n[1] - c[1])

    def sweeps0(start, count):
        def sweep(i, _):
            lo = start + i
            def body(q, carry):
                c, low = carry
                ahead = [pair0(lo + U0 * q + u + 1) for u in range(U0)]
                for u in range(U0):
                    x = lo + U0 * q + u
                    n = ahead[u]
                    r, low = flow0(x, c, n, low)
                    V0[x, 0] = c[0] + S0[x, 0] * r[0]
                    V0[x, 1] = c[1] + S0[x, 1] * r[1]
                    c = n
                return c, low
            lax.fori_loop(0, lax.div(32 - 2 * lo + (U0 - 1), U0), body, (pair0(lo), first0(lo)))
            return 0
        lax.fori_loop(0, count, sweep, 0)

    def restrict_k1():
        def body(i, _):
            for t in range(2):
                parts = []
                for base in (8, 16):
                    x = base + 2 * i
                    a = None
                    for u in range(2):
                        for o in range(2):
                            d = D0[KF, x + u, pl.ds(8 + 16 * t + o, 8, stride=2), :]
                            a = d if a is None else a + d
                    parts.append((a + pltpu.roll(a, 64, 1)) * 0.125)
                D1[KF, 1, i, 16 + 8 * t:24 + 8 * t, :] = jnp.where(lane < 64, parts[0], parts[1])
            return 0
        lax.fori_loop(0, 4, body, 0)

    def restrict_b1():
        def coarse(x):
            total = None
            low = first0(x)
            c = pair0(x)
            for u in range(2):
                n = pair0(x + u + 1)
                r, low = flow0(x + u, c, n, low)
                c = n
                part = r[0] + r[1]
                total = part if total is None else total + part
            return [(total[2 * m] + total[2 * m + 1]) * 0.125 for m in range(3)]
        def body(i, _):
            a, b = coarse(8 + 2 * i), coarse(16 + 2 * i)
            for m in range(3):
                T1[i, pl.ds(4 + m, 8, stride=3), :] = jnp.where(lane < 64, a[m], pltpu.roll(b[m], 64, 1))
            return 0
        lax.fori_loop(0, 4, body, 0)
        D1[BF, 1, :, 16:32, :] = T1[:, 8:24, :]

    low_strip = (lane16 < 16) | ((lane16 >= 48) & (lane16 < 64))
    high_strip = ((lane16 >= 64) & (lane16 < 80)) | (lane16 >= 112)

    def pack1(f):
        for h, strip in ((0, low_strip), (1, high_strip)):
            total = None
            for u in range(4):
                d = D1[f, 1, u, 16:32, :]
                part = pltpu.roll(jnp.where(strip, d, 0.0), (64 * h + 32 * u) % 128, 1)
                total = part if total is None else total + part
            Z1s[f, h] = total

    ring1 = (lane < 64) | ((lane < 80) & (iz < 3)) | ((lane >= 112) & (iz > 0))
    even16 = lax.rem(lax.div(lane, 16), 2) == 0

    def assemble1(f, dst):
        def body(g, _):
            for j in range(5):
                rows = pl.ds(4 + j, 8, stride=5)
                c = [jnp.where(even16, Z1r[f, 0, g, h, rows, :], Z1r[f, 1, g, h, rows, :]) for h in range(2)]
                mask = ring1
                if f == KF:
                    y = row * 5 + j + (iy * 16 - 12)
                    xb = ix + g - 1
                    mask = mask & (y >= 0) & (y < 64) & (xb >= 0) & (xb < 8)
                for xl in range(8):
                    d = D1[f, g, xl % 4, rows, :]
                    main = d if xl < 4 else pltpu.roll(d, 64, 1)
                    halo = pltpu.roll(c[xl // 4], (64 - 32 * (xl % 4)) % 128, 1)
                    dst[1 + g * 8 + xl, j] = jnp.where(mask, jnp.where(lane < 64, main, halo), 0.0)
            return 0
        lax.fori_loop(0, 3, body, 0)

    HW1 = 0.5 * 0.25

    def coefs1():
        def body(q, lower):
            for u in range(UC1):
                x = 1 + UC1 * q + u
                k, n = K1[x], K1[x + 1]
                cx, cy, cz = HW1 * (k + n), HW1 * (k + up(k)), HW1 * (k + roll(k, -1, -1))
                ym, zm = HW1 * (k[:1] + roll(k[-1:], 1, -2)), HW1 * (k + roll(k, 1, -1))
                d = cx + lower + cy + jnp.concatenate([ym, cy[:-1]], axis=0) + cz + zm
                CX1[x], CY1[x], CYM1[x], CZ1[x], CZM1[x] = cx, cy, ym[0], cz, zm
                S1[x] = jnp.where(k > 0, DAMPING / d, 0.0)
                lower = cx
            return lower
        c0 = HW1 * (K1[0] + K1[1])
        CX1[0] = c0
        lax.fori_loop(0, 24 // UC1, body, c0)

    def flow1(x, c, n, low):
        f = CX1[x] * (n - c)
        y = CY1[x] * (up(c) - c)
        ym = CYM1[x][None] * (c[:1] - roll(c[-1:], 1, -2))
        z, zm = CZ1[x] * (roll(c, -1, -1) - c), CZM1[x] * (c - roll(c, 1, -1))
        return B1[x] + ((f - low) + (y - jnp.concatenate([ym, y[:-1]], axis=0)) + (z - zm)), f

    def sweeps1(lo, planes, count):
        def sweep(i, _):
            c = V1[lo]
            low = CX1[lo - 1] * (c - V1[lo - 1])
            for x in range(lo, lo + planes):
                n = V1[x + 1]
                r, low = flow1(x, c, n, low)
                V1[x] = c + S1[x] * r
                c = n
            return 0
        lax.fori_loop(0, count, sweep, 0)

    def pick(xl):
        q = lax.rem(ll, 32)
        z = lax.rem(q, 8) * 4 + lax.div(q, 8)
        return ((lax.div(ll, 32) == xl) & (lax.div(cc, 2) == z)).astype(F32)

    picks = [pick(xl) for xl in range(4)]

    def pack_k2():
        total = None
        for h in range(2):
            a = None
            for u in range(2):
                for o in range(2):
                    d = D1[KF, 1, 2 * h + u, pl.ds(16 + o, 8, stride=2), :]
                    a = d if a is None else a + d
            a = a * 0.125
            part = dot(a, picks[h]) + dot(pltpu.roll(a, 64, 1), picks[2 + h])
            total = part if total is None else total + part
        P2s[KF] = total
        R2[KF, here] = total

    def pack_b2():
        for xl in range(4):
            x = 9 + 2 * xl
            total = None
            c = V1[x]
            low = CX1[x - 1] * (c - V1[x - 1])
            for u in range(2):
                n = V1[x + u + 1]
                r, low = flow1(x + u, c, n, low)
                c = n
                total = r if total is None else total + r
            for j in range(5):
                T2[xl, pl.ds(j, 8, stride=5), :] = total[j]
        total = None
        for xl in range(4):
            a = (T2[xl, pl.ds(12, 8, stride=2), :] + T2[xl, pl.ds(13, 8, stride=2), :]) * 0.125
            part = dot(a, picks[xl])
            total = part if total is None else total + part
        P2s[BF] = total
        R2[BF, here] = total

    def spread(f):
        v = [R2[f, g] for g in range(16)]
        for bit in (1, 2, 4, 8):
            clear = lax.rem(lax.div(lane, 8 * bit), 2) == 0
            for r in range(16):
                if r & bit:
                    continue
                a, d = v[r], v[r | bit]
                v[r] = jnp.where(clear, a, pltpu.roll(d, 8 * bit, 1))
                v[r | bit] = jnp.where(clear, pltpu.roll(a, 128 - 8 * bit, 1), d)
        for q in range(16):
            G2[f, pl.ds(pl.multiple_of(ix * 128 + q * 8, 8), 8), :] = v[q]

    def gathered(f, yl):
        rows = []
        for xl in range(4):
            rows.append(jnp.stack([G2[f, pl.ds((xl * 4 + zl) * 8 + yl, 8, stride=128), :] for zl in range(4)], 0))
        return jnp.stack(rows, 0)

    def edges(ref, ny):
        ref[0] = jnp.where(lane >= 32, roll(ref[ny], 32, -1), 0.0)
        ref[ny + 1] = jnp.where(lane < 96, roll(ref[1], -32, -1), 0.0)

    def around(v):
        xp = shifted(v, 0, 1, roll(v[:1], -1, -2))
        xm = shifted(v, 0, -1, roll(v[-1:], 1, -2))
        zp = shifted(v, 1, 1, roll(v[:, :1], -1, -1))
        zm = shifted(v, 1, -1, roll(v[:, -1:], 1, -1))
        return xp, xm, zp, zm

    z_top, z_end = lax.rem(lane, 32) == 31, lax.rem(lane, 32) == 0

    def inside(k):
        xp = shifted(k, 0, 1, jnp.where(row == 7, 0.0, roll(k[:1], -1, -2)))
        xm = shifted(k, 0, -1, jnp.where(row == 0, 0.0, roll(k[-1:], 1, -2)))
        zp = shifted(k, 1, 1, jnp.where(z_top, 0.0, roll(k[:, :1], -1, -1)))
        zm = shifted(k, 1, -1, jnp.where(z_end, 0.0, roll(k[:, -1:], 1, -1)))
        return xp, xm, zp, zm

    def coefs_low(level, K, A, S, I, ny):
        hw = 0.5 * 0.25 ** level
        edges(K, ny)
        def body(y, _):
            k = K[y + 1]
            near = inside(k) + (K[y + 2], K[y])
            c = [hw * (k + n) for n in near]
            d = ((c[0] + c[1]) + (c[2] + c[3])) + (c[4] + c[5])
            s = DAMPING / d
            S[y] = s
            if I is not None:
                I[y] = d * (1.0 / DAMPING)
            for m in range(6):
                A[m, y] = jnp.where(near[m] > 0, s * c[m], 0.0)
            return 0
        lax.fori_loop(0, ny // 2, times(2, body), 0)

    def fold(blocks):
        t = blocks[0] + blocks[1]
        t = t.reshape((t.shape[0] // 2, 2) + t.shape[1:])
        t = t[:, 0] + t[:, 1]
        t = t.reshape((t.shape[0], t.shape[1] // 2, 2) + t.shape[2:])
        return (t[:, :, 0] + t[:, :, 1]) * 0.125

    def load_k2():
        def body(y, _):
            K2[y + 1] = gathered(KF, y)
            return 0
        lax.fori_loop(0, 2, times(4, body), 0)
        coefs_low(2, K2, A2, S2, I2, 8)
        def body3(y, _):
            K3[y + 1] = fold([K2[2 * y + 1], K2[2 * y + 2]])
            return 0
        lax.fori_loop(0, 1, times(4, body3), 0)
        coefs_low(3, K3, A3, S3, I3, 4)
        for y in range(2):
            K4[y + 1] = fold([K3[2 * y + 1], K3[2 * y + 2]])
        coefs_low(4, K4, A4, S4, None, 2)

    def next2(y, cur, before, after):
        xp, xm, zp, zm = around(cur)
        t = 0.2 * cur + Q2[y]
        t = t + A2[0, y] * xp + A2[1, y] * xm
        t = t + A2[2, y] * zp + A2[3, y] * zm
        return t + (A2[4, y] * after + A2[5, y] * before)

    def sweeps2(count):
        def sweep(i, _):
            edges(V2, 8)
            before = V2[0]
            for y in range(8):
                cur = V2[y + 1]
                V2[y + 1] = next2(y, cur, before, V2[y + 2])
                before = cur
            return 0
        lax.fori_loop(0, count, sweep, 0)

    def next_whole(v, a, g, ny):
        first = roll(v[ny - 1], 32, -1)
        last = roll(v[0], -32, -1)
        out = []
        for y in range(ny):
            xp, xm, zp, zm = around(v[y])
            yp = v[y + 1] if y + 1 < ny else last
            ym = v[y - 1] if y else first
            t = (0.2 * v[y] + g(y)) + (a(0, y) * xp + a(1, y) * xm)
            out.append(t + ((a(2, y) * zp + a(3, y) * zm) + (a(4, y) * yp + a(5, y) * ym)))
        return out

    def a3(m, y):
        return A3[m, y]

    def g3(y):
        return Q3[y]

    def sweeps3(v, count):
        return lax.fori_loop(0, count, lambda i, w: tuple(next_whole(list(w), a3, g3, 4)), tuple(v))

    def lower_levels():
        v = sweeps3([Q3[y] for y in range(4)], 5)
        w = next_whole(list(v), a3, g3, 4)
        r = [(w[y] - v[y]) * I3[y] for y in range(4)]
        g4 = [fold(r[2 * y:2 * y + 2]) * S4[y] for y in range(2)]
        a4 = [[A4[m, y] for y in range(2)] for m in range(6)]
        c = lax.fori_loop(
            0, 15, lambda i, w: tuple(next_whole(list(w), lambda m, y: a4[m][y], lambda y: g4[y], 2)), tuple(g4))
        v = [v[y] + c[y // 2] for y in range(4)]
        return sweeps3(v, 6)

    loads[0].wait()
    permute_in(KF)
    pack0(KF)
    loads[1].wait()
    permute_in(BF)
    pack0(BF)
    pl.semaphore_wait(barrier, len(PEERS))
    k0 = copies0(KF)
    start(k0)
    b0 = copies0(BF)
    start(b0)

    restrict_k1()
    pack1(KF)
    pack_k2()
    k2 = copies_plane(KF)
    start(k2)

    wait_recv(k0)
    assemble0(KF, K0)
    coefs0()
    wait_recv(b0)
    k1 = copies1(KF)
    start(k1)
    assemble0(BF, B0)

    sweeps0(3, 5)
    restrict_b1()
    pack1(BF)
    b1 = copies1(BF)
    start(b1)

    wait_recv(k1)
    assemble1(KF, K1)
    k1f = copies_far(K1, 0)
    start(k1f)
    wait_recv(k2)
    spread(KF)
    k2l = copies_line(KF)
    start(k2l)
    def stage0(x, _):
        for j in range(6):
            T0[x, pl.ds(j, 8, stride=6), :] = jnp.where(
                lane < 64, V0[8 + x, 0, j], pltpu.roll(V0[8 + x, 1, j], 64, 1))
        D0[VF, 8 + x, 8:40, :] = T0[x, 8:40, :]
        return 0
    lax.fori_loop(0, 4, times(4, stage0), 0)
    pack0(VF)
    v0 = copies0(VF)
    start(v0)
    wait_recv(k1f)
    coefs1()

    wait_recv(b1)
    assemble1(BF, B1)

    def first_sweep1(x, _):
        V1[3 + x] = S1[3 + x] * B1[3 + x]
        return 0
    lax.fori_loop(0, 2, times(10, first_sweep1), 0)
    sweeps1(4, 18, 2)
    sweeps1(6, 14, 3)
    pack_b2()
    b2 = copies_plane(BF)
    start(b2)

    def stage1(i, _):
        for j in range(5):
            T2[i, pl.ds(j, 8, stride=5), :] = jnp.where(
                lane < 64, V1[9 + i, j], pltpu.roll(V1[13 + i, j], 64, 1))
        for t in range(2):
            D1[VF, 1, i, 16 + 8 * t:24 + 8 * t, :] = T2[i, pl.ds(12 + 8 * t, 8, stride=1), :]
        return 0
    lax.fori_loop(0, 1, times(4, stage1), 0)
    pack1(VF)
    k2o = copies_on(KF)
    pass_on(k2l, k2o)
    wait_recv(b2)
    spread(BF)
    b2l = copies_line(BF)
    start(b2l)

    v1 = copies1(VF)
    start(v1)
    k2l[3].wait_recv()
    wait_recv(k2o)
    load_k2()
    for made in (k0, b0, k1, b1, k1f, k2, b2, k2l, k2o):
        wait_send(made)
    wait_recv(v0)
    b2o = copies_on(BF)
    pass_on(b2l, b2o)
    assemble0(VF, W0)
    wait_send(v0)
    b2l[3].wait_recv()
    wait_recv(b2o)

    def load_b2(y, _):
        q = S2[y] * gathered(BF, y)
        Q2[y] = q
        V2[y + 1] = q
        return 0
    lax.fori_loop(0, 2, times(4, load_b2), 0)
    sweeps2(5)
    wait_recv(v1)
    assemble1(VF, W1)
    v1f = copies_far(W1, 1)
    start(v1f)

    edges(V2, 8)

    def restrict2(y, _):
        r = []
        for u in range(2):
            z = 2 * y + u
            cur = V2[z + 1]
            r.append((next2(z, cur, V2[z], V2[z + 2]) - cur) * I2[z])
        Q3[y] = fold(r) * S3[y]
        return 0
    lax.fori_loop(0, 2, times(2, restrict2), 0)
    v3 = lower_levels()
    for y in range(4):
        V3[y] = v3[y]

    def prolong2(y, _):
        for xl in range(4):
            for zl in range(4):
                V2[y + 1, xl, zl] = V2[y + 1, xl, zl] + V3[lax.div(y, 2), xl // 2, zl // 2]
        return 0
    lax.fori_loop(0, 2, times(4, prolong2), 0)
    sweeps2(6)

    def lay2(y, _):
        for xl in range(4):
            for zl in range(4):
                H2[pl.ds((xl * 4 + zl) * 8 + y, 8, stride=128), :] = V2[y + 1, xl, zl]
        return 0
    lax.fori_loop(0, 2, times(4, lay2), 0)
    planes = [(-2, 3)] + [(o, xl) for o in (-1, 0, 1) for xl in range(4)] + [(2, 0)]
    acc = None
    zf = jnp.where(ll < 96, ll, ll - 128)
    zc = lax.div(zf + 128, 2) - 64 + iz * 32
    for zl in range(4):
        left = []
        for o, xl in planes:
            at_x = jnp.clip(ix + o, 0, 7)
            left.append(H2[pl.ds(pl.multiple_of(at_x * 128 + (xl * 4 + zl) * 8, 8), 8), :])
        left = jnp.concatenate(left, axis=0)
        ok = (zc >= 0) & (zc < 128) & (lax.rem(zc + 128, 4) == zl)
        right = jnp.concatenate(
            [(ok & (cc == (iy + dy) * 32 + lax.div(zc, 4))).astype(F32) for dy in (-1, 0, 1)], axis=1)
        part = dot3(left, right.astype(jnp.bfloat16))
        acc = part if acc is None else acc + part
    for m in range(14):
        for d in range(3):
            v = acc[8 * m:8 * m + 8, 128 * d:128 * d + 128]
            F1[m, pl.ds(16 * d, 8, stride=2), :] = v
            F1[m, pl.ds(16 * d + 1, 8, stride=2), :] = v
    wait_recv(v1f)

    def start1(x, _):
        m = lax.div(x + 1, 2)
        for j in range(5):
            V1[x, j] = jnp.where(K1[x, j] > 0, W1[x, j] + F1[m, pl.ds(4 + j, 8, stride=5), :], 0.0)
        return 0
    lax.fori_loop(0, 2, times(13, start1), 0)
    sweeps1(1, 24, 3)
    sweeps1(4, 18, 3)

    def lay1(i, _):
        for j in range(5):
            F0[i, pl.ds(j, 8, stride=5), :] = V1[6 + i, j]
        return 0
    lax.fori_loop(0, 2, times(7, lay1), 0)

    def start0(i, _):
        for m in range(3):
            add = F0[i, pl.ds(8 + m, 8, stride=3), :]
            for u in range(2):
                x = 2 + 2 * i + u
                for p in range(2):
                    for o in range(2):
                        j = 2 * m + o
                        V0[x, p, j] = jnp.where(S0[x, p, j] > 0, W0[x, p, j] + add, 0.0)
        return 0
    lax.fori_loop(0, 7, times(2, start0), 0)
    sweeps0(3, 6)

    join = (ll == jnp.where(cc < 64, 2 * cc, 2 * (cc - 64) + 1)).astype(F32).astype(jnp.bfloat16)

    def finish(x, _):
        for j in range(6):
            T0[x, pl.ds(j, 8, stride=6), :] = jnp.where(
                lane < 64, V0[8 + x, 0, j], pltpu.roll(V0[8 + x, 1, j], 64, 1))
        return 0
    lax.fori_loop(0, 4, times(4, finish), 0)

    for i in range(4):
        d = T0[4 * i:4 * i + 4, 8:40, :].reshape(128, 128)
        out_ref[4 * i:4 * i + 4] = dot3(d, join).reshape(4, 32, 128)
    for made in (v1, v1f, b2l, b2o):
        wait_send(made)


def shards(source, conductivity):
    def vm(*shape):
        return pltpu.VMEM(shape, F32)

    def dma(n):
        return pltpu.SemaphoreType.DMA((n,))

    fine = (36, 2, 6, 8, 128)
    mid = (26, 5, 8, 128)
    low2, low3, low4 = (4, 4, 8, 128), (2, 2, 8, 128), (1, 1, 8, 128)
    scratch = [
        vm(2, 16, 32, 128), vm(3, 32, 48, 128), vm(3, 2, 32, 128), vm(3, 2, 4, 48, 128),
        vm(*fine), vm(*fine), vm(*fine), vm(36, 2, 8, 128), vm(*fine), vm(36, 6, 8, 128),
        vm(*fine), vm(*fine), vm(*fine), vm(*fine), vm(16, 48, 128),
        vm(3, 3, 4, 48, 128), vm(3, 2, 16, 128), vm(3, 2, 3, 2, 48, 128),
        vm(*mid), vm(*mid), vm(*mid), vm(26, 8, 128), vm(*mid), vm(*mid), vm(*mid), vm(*mid), vm(*mid), vm(*mid),
        vm(4, 32, 128), vm(4, 40, 128), vm(14, 40, 128), vm(14, 48, 128),
        vm(2, 8, 128), vm(2, 16, 8, 128), vm(2, 1024, 128), vm(1024, 128),
        vm(10, *low2), vm(10, *low2), vm(6, 8, *low2), vm(8, *low2), vm(8, *low2), vm(8, *low2),
        vm(6, *low3), vm(4, *low3), vm(6, 4, *low3), vm(4, *low3), vm(4, *low3), vm(4, *low3),
        vm(4, *low4), vm(6, 2, *low4), vm(2, *low4), vm(2, *low4),
        dma(2), dma(78), dma(78), dma(78), dma(78), dma(4), dma(4), dma(30), dma(30), dma(14), dma(14),
    ]
    return pl.pallas_call(
        kernel,
        out_shape=jax.ShapeDtypeStruct((16, 32, 128), F32),
        in_specs=[pl.BlockSpec(memory_space=pltpu.HBM)] * 2,
        out_specs=pl.BlockSpec(memory_space=pltpu.VMEM),
        scratch_shapes=scratch,
        compiler_params=pltpu.CompilerParams(
            collective_id=0, has_side_effects=True, vmem_limit_bytes=62 * 1024 * 1024),
    )(source, conductivity)


def solution(mesh):
    spec = P("gx", "gy", "gz")
    return jax.shard_map(shards, mesh=mesh, in_specs=(spec, spec), out_specs=spec, check_vma=False)
```

```python
import jax
import jax.numpy as jnp
from jax import lax
from jax.experimental import pallas as pl
from jax.experimental.pallas import tpu as pltpu
from jax.sharding import PartitionSpec as P

MESH = pl.DeviceIdType.MESH
F32 = jnp.float32
HI = lax.Precision.HIGHEST
DAMPING = 0.8

U0 = 6
UC0 = 3
UC1 = 6

KF, BF, VF = 0, 1, 2
NEAR = [(a, b, c) for a in (-1, 0, 1) for b in (-1, 0, 1) for c in (-1, 0, 1) if (a, b, c) != (0, 0, 0)]
PLANE = [(0, b, c) for b in range(4) for c in range(4) if (b, c) != (0, 0)]
LINE = [(a, 0, 0) for a in range(1, 8)]
PEERS = sorted({(a % 8, b % 4, c % 4) for a, b, c in NEAR + PLANE + LINE})


def iota(shape, dim):
    return lax.broadcasted_iota(jnp.int32, shape, dim)


def roll(v, amount, axis):
    shape = v.shape
    if axis == -1:
        return pltpu.roll(v.reshape(-1, 128), amount % 128, 1).reshape(shape)
    return pltpu.roll(v.reshape(-1, 8, 128), amount % 8, 1).reshape(shape)


def shifted(v, axis, step, edge):
    n = v.shape[axis]
    if n == 1:
        return edge
    if step > 0:
        return jnp.concatenate([lax.slice_in_dim(v, 1, n, axis=axis), edge], axis=axis)
    return jnp.concatenate([edge, lax.slice_in_dim(v, 0, n - 1, axis=axis)], axis=axis)


def up(v):
    return jnp.concatenate([v[1:], roll(v[:1], -1, -2)], axis=0)


def down(v):
    return jnp.concatenate([roll(v[-1:], 1, -2), v[:-1]], axis=0)


def dot3(a, b):
    hi = a.astype(jnp.bfloat16)
    rest = a - hi.astype(F32)
    mid = rest.astype(jnp.bfloat16)
    low = (rest - mid.astype(F32)).astype(jnp.bfloat16)
    return sum(jnp.dot(p, b, preferred_element_type=F32) for p in (low, mid, hi))


def times(count, step):
    def body(i, carry):
        for u in range(count):
            step(i * count + u, 0)
        return carry
    return body


def dot(a, b):
    return jnp.dot(a, b, precision=HI, preferred_element_type=F32)


def kernel(
    src_hbm, cond_hbm, out_ref,
    raw, D0, Z0s, Z0r, K0, CX0, CY0, CYM0, CZ0, CZM0, S0, B0, V0, W0, T0,
    D1, Z1s, Z1r, K1, CX1, CY1, CYM1, CZ1, CZM1, S1, B1, V1, W1, T1, T2, F0, F1,
    P2s, R2, G2, H2, K2, V2, A2, S2, I2, Q2, K3, V3, A3, S3, I3, Q3, K4, A4, S4, Q4,
    raw_sem, s0s, s0r, s1s, s1r, xs, xr, g1s, g1r, g2s, g2r,
):
    ix, iy, iz = lax.axis_index("gx"), lax.axis_index("gy"), lax.axis_index("gz")
    lane = iota((8, 128), 1)
    row = iota((8, 128), 0)

    steps = {}

    def moved(axis, place, step, size):
        if not isinstance(step, int):
            return place + step
        key = (axis, step % size)
        if key not in steps:
            steps[key] = lax.rem(place + step % size, size) if step % size else place
        return steps[key]

    def at(offset):
        a, b, c = offset
        return (moved(0, ix, a, 8), moved(1, iy, b, 4), moved(2, iz, c, 4))

    def remote(src, dst, send, recv, offset):
        return pltpu.make_async_remote_copy(
            src_ref=src, dst_ref=dst, send_sem=send, recv_sem=recv, device_id=at(offset), device_id_type=MESH)

    loads = [pltpu.make_async_copy(cond_hbm, raw.at[0], raw_sem.at[0]),
             pltpu.make_async_copy(src_hbm, raw.at[1], raw_sem.at[1])]
    for c in loads:
        c.start()
    barrier = pltpu.get_barrier_semaphore()
    for offset in PEERS:
        pl.semaphore_signal(barrier, inc=1, device_id=at(offset), device_id_type=MESH)

    def copies0(f):
        reach = 7 if f == KF else 6
        made = []
        for n, (dx, dy, dz) in enumerate(NEAR):
            n_x = reach - (dy != 0) - (dz != 0)
            n_y = reach - (dx != 0) - (dz != 0)
            sx, tx, cx = {0: (8, 8, 16), -1: (8, 24, n_x), 1: (24 - n_x, 8 - n_x, n_x)}[dx]
            sr, tr, cr = {0: (8, 8, 32), -1: (8, 40, n_y), 1: (40 - n_y, 8 - n_y, n_y)}[dy]
            if dz == 0:
                src = D0.at[f, pl.ds(sx, cx), pl.ds(sr, cr)]
                dst = D0.at[f, pl.ds(tx, cx), pl.ds(tr, cr)]
            else:
                side = 0 if dz == -1 else 1
                sh, th, ch = {0: (0, 1, 2), -1: (0, 3, 1), 1: (1, 0, 1)}[dx]
                src = Z0s.at[f, pl.ds(sh, ch), pl.ds(sr - 8, cr)]
                dst = Z0r.at[f, side, pl.ds(th, ch), pl.ds(tr, cr)]
            made.append(remote(src, dst, s0s.at[f * 26 + n], s0r.at[f * 26 + n], (dx, dy, dz)))
        return made

    def copies1(f):
        made = []
        for n, (dx, dy, dz) in enumerate(NEAR):
            n_y = 8 if f == BF else 9
            sr, tr, cr = {0: (16, 16, 16), -1: (16, 32, n_y), 1: (32 - n_y, 16 - n_y, n_y)}[dy]
            if dz == 0:
                src = D1.at[f, 1, :, pl.ds(sr, cr)]
                dst = D1.at[f, 1 - dx, :, pl.ds(tr, cr)]
            else:
                side = 0 if dz == -1 else 1
                src = Z1s.at[f, :, pl.ds(sr - 16, cr)]
                dst = Z1r.at[f, side, 1 - dx, :, pl.ds(tr, cr)]
            made.append(remote(src, dst, s1s.at[f * 26 + n], s1r.at[f * 26 + n], (dx, dy, dz)))
        return made

    def copies_far(ref, f):
        return [remote(ref.at[8], ref.at[0], xs.at[2 * f], xr.at[2 * f], (1, 0, 0)),
                remote(ref.at[17], ref.at[25], xs.at[2 * f + 1], xr.at[2 * f + 1], (-1, 0, 0))]

    here = iy * 4 + iz

    def copies_plane(f):
        return [remote(P2s.at[f], R2.at[f, here], g1s.at[f * 15 + n], g1r.at[f * 15 + n], o)
                for n, o in enumerate(PLANE)]

    slab = pl.ds(pl.multiple_of(ix * 128, 128), 128)

    other = 1 - 2 * lax.rem(ix, 2)

    def copies_line(f):
        return [remote(G2.at[f, slab], G2.at[f, slab], g2s.at[f * 7 + n], g2r.at[f * 7 + n], (o, 0, 0))
                for n, o in enumerate((2, 6, 4, other))]

    def copies_on(f):
        made = []
        for n, o in enumerate((2, 6, 4)):
            rows = pl.ds(pl.multiple_of(lax.rem(ix + 8 - o, 8) * 128, 128), 128)
            made.append(remote(G2.at[f, rows], G2.at[f, rows], g2s.at[f * 7 + 4 + n], g2r.at[f * 7 + 4 + n], (other, 0, 0)))
        return made

    def pass_on(made, onward):
        for c, d in zip(made, onward):
            c.wait_recv()
            d.start()

    def start(made):
        for c in made:
            c.start()

    def wait_recv(made):
        for c in made:
            c.wait_recv()

    def wait_send(made):
        for c in made:
            c.wait_send()

    cc, ll = iota((128, 128), 0), iota((128, 128), 1)
    split = (cc == jnp.where(ll < 64, 2 * ll, 2 * (ll - 64) + 1)).astype(F32)
    lane32 = iota((32, 128), 1)
    lane16 = iota((16, 128), 1)

    def permute_in(f):
        for i in range(4):
            x = raw[f, 4 * i:4 * i + 4].reshape(128, 128)
            D0[f, 8 + 4 * i:12 + 4 * i, 8:40, :] = dot(x, split).reshape(4, 32, 128)

    even_strip = (lane32 < 4) | ((lane32 >= 60) & (lane32 < 64))
    odd_strip = ((lane32 >= 64) & (lane32 < 68)) | (lane32 >= 124)

    def pack0(f):
        for h in range(2):
            total = None
            for xi in range(8):
                d = D0[f, 8 + 8 * h + xi, 8:40, :]
                part = (pltpu.roll(jnp.where(even_strip, d, 0.0), (16 * xi) % 128, 1)
                        + pltpu.roll(jnp.where(odd_strip, d, 0.0), (16 * xi + 72) % 128, 1))
                total = part if total is None else total + part
            Z0s[f, h] = total

    ring0 = (lane < 64) | ((lane < 68) & (iz < 3)) | ((lane >= 124) & (iz > 0))
    even4 = lax.rem(lax.div(lane, 4), 2) == 0

    def assemble0(f, dst):
        def body(xh, _):
            for j in range(6):
                rows = pl.ds(j, 8, stride=6)
                c = jnp.where(even4, Z0r[f, 0, xh, rows, :], Z0r[f, 1, xh, rows, :])
                mask = ring0
                if f == KF:
                    y = row * 6 + j + (iy * 32 - 8)
                    xb = ix * 2 + xh - 1
                    mask = mask & (y >= 0) & (y < 128) & (xb >= 0) & (xb < 16)
                for xi in range(8):
                    x = xh * 8 + xi
                    d = D0[f, x, rows, :]
                    full = mask
                    if f == KF and xi in (0, 7):
                        full = mask & (x > 0) & (x < 31)
                    for p in range(2):
                        main = d if p == 0 else pltpu.roll(d, 64, 1)
                        halo = pltpu.roll(c, (64 - 16 * xi - 8 * p) % 128, 1)
                        value = jnp.where(full, jnp.where(lane < 64, main, halo), 0.0)
                        dst[x, p, j] = value
                        if f == BF:
                            V0[x, p, j] = S0[x, p, j] * value
            return 0
        lax.fori_loop(0, 4, body, 0)

    def coefs0():
        def body(q, carry):
            (ke, ko), lower = carry
            for u in range(UC0):
                x = 1 + UC0 * q + u
                ne, no = K0[x + 1, 0], K0[x + 1, 1]
                xe, xo = 0.5 * (ke + ne), 0.5 * (ko + no)
                ye, yo = 0.5 * (ke + up(ke)), 0.5 * (ko + up(ko))
                me, mo = 0.5 * (ke[:1] + roll(ke[-1:], 1, -2)), 0.5 * (ko[:1] + roll(ko[-1:], 1, -2))
                ze, zo = 0.5 * (ke + ko), 0.5 * (ko + roll(ke, -1, -1))
                zm = 0.5 * (ke + roll(ko, 1, -1))
                de = xe + lower[0] + ye + jnp.concatenate([me, ye[:-1]], axis=0) + ze + zm
                do = xo + lower[1] + yo + jnp.concatenate([mo, yo[:-1]], axis=0) + zo + ze
                CX0[x, 0], CX0[x, 1] = xe, xo
                CY0[x, 0], CY0[x, 1] = ye, yo
                CYM0[x, 0], CYM0[x, 1] = me[0], mo[0]
                CZ0[x, 0], CZ0[x, 1] = ze, zo
                CZM0[x] = zm
                S0[x, 0] = jnp.where(ke > 0, DAMPING / de, 0.0)
                S0[x, 1] = jnp.where(ko > 0, DAMPING / do, 0.0)
                ke, ko, lower = ne, no, (xe, xo)
            return (ke, ko), lower
        first = (K0[1, 0], K0[1, 1])
        lax.fori_loop(0, 30 // UC0, body, (first, (0.5 * first[0], 0.5 * first[1])))

    def flow0(x, c, n, low):
        ce, co = c
        fe, fo = CX0[x, 0] * (n[0] - ce), CX0[x, 1] * (n[1] - co)
        ye, yo = CY0[x, 0] * (up(ce) - ce), CY0[x, 1] * (up(co) - co)
        me = CYM0[x, 0][None] * (ce[:1] - roll(ce[-1:], 1, -2))
        mo = CYM0[x, 1][None] * (co[:1] - roll(co[-1:], 1, -2))
        ze = CZ0[x, 0] * (co - ce)
        zo, zm = CZ0[x, 1] * (roll(ce, -1, -1) - co), CZM0[x] * (ce - roll(co, 1, -1))
        re = B0[x, 0] + ((fe - low[0]) + (ye - jnp.concatenate([me, ye[:-1]], axis=0)) + (ze - zm))
        ro = B0[x, 1] + ((fo - low[1]) + (yo - jnp.concatenate([mo, yo[:-1]], axis=0)) + (zo - ze))
        return (re, ro), (fe, fo)

    def pair0(x):
        return V0[x, 0], V0[x, 1]

    def first0(x):
        c, n = pair0(x - 1), pair0(x)
        return CX0[x - 1, 0] * (n[0] - c[0]), CX0[x - 1, 1] * (n[1] - c[1])

    def sweeps0(start, count):
        def sweep(i, _):
            lo = start + i
            def body(q, carry):
                c, low = carry
                ahead = [pair0(lo + U0 * q + u + 1) for u in range(U0)]
                for u in range(U0):
                    x = lo + U0 * q + u
                    n = ahead[u]
                    r, low = flow0(x, c, n, low)
                    V0[x, 0] = c[0] + S0[x, 0] * r[0]
                    V0[x, 1] = c[1] + S0[x, 1] * r[1]
                    c = n
                return c, low
            lax.fori_loop(0, lax.div(32 - 2 * lo + (U0 - 1), U0), body, (pair0(lo), first0(lo)))
            return 0
        lax.fori_loop(0, count, sweep, 0)

    def restrict_k1():
        def body(i, _):
            for t in range(2):
                parts = []
                for base in (8, 16):
                    x = base + 2 * i
                    a = None
                    for u in range(2):
                        for o in range(2):
                            d = D0[KF, x + u, pl.ds(8 + 16 * t + o, 8, stride=2), :]
                            a = d if a is None else a + d
                    parts.append((a + pltpu.roll(a, 64, 1)) * 0.125)
                D1[KF, 1, i, 16 + 8 * t:24 + 8 * t, :] = jnp.where(lane < 64, parts[0], parts[1])
            return 0
        lax.fori_loop(0, 4, body, 0)

    def restrict_b1():
        def coarse(x):
            total = None
            low = first0(x)
            c = pair0(x)
            for u in range(2):
                n = pair0(x + u + 1)
                r, low = flow0(x + u, c, n, low)
                c = n
                part = r[0] + r[1]
                total = part if total is None else total + part
            return [(total[2 * m] + total[2 * m + 1]) * 0.125 for m in range(3)]
        def body(i, _):
            a, b = coarse(8 + 2 * i), coarse(16 + 2 * i)
            for m in range(3):
                T1[i, pl.ds(4 + m, 8, stride=3), :] = jnp.where(lane < 64, a[m], pltpu.roll(b[m], 64, 1))
            return 0
        lax.fori_loop(0, 1, times(4, body), 0)
        D1[BF, 1, :, 16:32, :] = T1[:, 8:24, :]

    low_strip = (lane16 < 16) | ((lane16 >= 48) & (lane16 < 64))
    high_strip = ((lane16 >= 64) & (lane16 < 80)) | (lane16 >= 112)

    def pack1(f):
        for h, strip in ((0, low_strip), (1, high_strip)):
            total = None
            for u in range(4):
                d = D1[f, 1, u, 16:32, :]
                part = pltpu.roll(jnp.where(strip, d, 0.0), (64 * h + 32 * u) % 128, 1)
                total = part if total is None else total + part
            Z1s[f, h] = total

    ring1 = (lane < 64) | ((lane < 80) & (iz < 3)) | ((lane >= 112) & (iz > 0))
    even16 = lax.rem(lax.div(lane, 16), 2) == 0

    def assemble1(f, dst):
        def body(g, _):
            for j in range(5):
                rows = pl.ds(4 + j, 8, stride=5)
                c = [jnp.where(even16, Z1r[f, 0, g, h, rows, :], Z1r[f, 1, g, h, rows, :]) for h in range(2)]
                mask = ring1
                if f == KF:
                    y = row * 5 + j + (iy * 16 - 12)
                    xb = ix + g - 1
                    mask = mask & (y >= 0) & (y < 64) & (xb >= 0) & (xb < 8)
                for xl in range(8):
                    d = D1[f, g, xl % 4, rows, :]
                    main = d if xl < 4 else pltpu.roll(d, 64, 1)
                    halo = pltpu.roll(c[xl // 4], (64 - 32 * (xl % 4)) % 128, 1)
                    dst[1 + g * 8 + xl, j] = jnp.where(mask, jnp.where(lane < 64, main, halo), 0.0)
            return 0
        lax.fori_loop(0, 3, body, 0)

    HW1 = 0.5 * 0.25

    def coefs1():
        def body(q, lower):
            for u in range(UC1):
                x = 1 + UC1 * q + u
                k, n = K1[x], K1[x + 1]
                cx, cy, cz = HW1 * (k + n), HW1 * (k + up(k)), HW1 * (k + roll(k, -1, -1))
                ym, zm = HW1 * (k[:1] + roll(k[-1:], 1, -2)), HW1 * (k + roll(k, 1, -1))
                d = cx + lower + cy + jnp.concatenate([ym, cy[:-1]], axis=0) + cz + zm
                CX1[x], CY1[x], CYM1[x], CZ1[x], CZM1[x] = cx, cy, ym[0], cz, zm
                S1[x] = jnp.where(k > 0, DAMPING / d, 0.0)
                lower = cx
            return lower
        c0 = HW1 * (K1[0] + K1[1])
        CX1[0] = c0
        lax.fori_loop(0, 24 // UC1, body, c0)

    def flow1(x, c, n, low):
        f = CX1[x] * (n - c)
        y = CY1[x] * (up(c) - c)
        ym = CYM1[x][None] * (c[:1] - roll(c[-1:], 1, -2))
        z, zm = CZ1[x] * (roll(c, -1, -1) - c), CZM1[x] * (c - roll(c, 1, -1))
        return B1[x] + ((f - low) + (y - jnp.concatenate([ym, y[:-1]], axis=0)) + (z - zm)), f

    def sweeps1(lo, planes, count):
        def sweep(i, _):
            c = V1[lo]
            low = CX1[lo - 1] * (c - V1[lo - 1])
            for x in range(lo, lo + planes):
                n = V1[x + 1]
                r, low = flow1(x, c, n, low)
                V1[x] = c + S1[x] * r
                c = n
            return 0
        lax.fori_loop(0, count, sweep, 0)

    def pick(xl):
        q = lax.rem(ll, 32)
        z = lax.rem(q, 8) * 4 + lax.div(q, 8)
        return ((lax.div(ll, 32) == xl) & (lax.div(cc, 2) == z)).astype(F32)

    picks = [pick(xl) for xl in range(4)]

    def pack_k2():
        total = None
        for h in range(2):
            a = None
            for u in range(2):
                for o in range(2):
                    d = D1[KF, 1, 2 * h + u, pl.ds(16 + o, 8, stride=2), :]
                    a = d if a is None else a + d
            a = a * 0.125
            part = dot(a, picks[h]) + dot(pltpu.roll(a, 64, 1), picks[2 + h])
            total = part if total is None else total + part
        P2s[KF] = total
        R2[KF, here] = total

    def pack_b2():
        for xl in range(4):
            x = 9 + 2 * xl
            total = None
            c = V1[x]
            low = CX1[x - 1] * (c - V1[x - 1])
            for u in range(2):
                n = V1[x + u + 1]
                r, low = flow1(x + u, c, n, low)
                c = n
                total = r if total is None else total + r
            for j in range(5):
                T2[xl, pl.ds(j, 8, stride=5), :] = total[j]
        total = None
        for xl in range(4):
            a = (T2[xl, pl.ds(12, 8, stride=2), :] + T2[xl, pl.ds(13, 8, stride=2), :]) * 0.125
            part = dot(a, picks[xl])
            total = part if total is None else total + part
        P2s[BF] = total
        R2[BF, here] = total

    def spread(f):
        v = [R2[f, g] for g in range(16)]
        for bit in (1, 2, 4, 8):
            clear = lax.rem(lax.div(lane, 8 * bit), 2) == 0
            for r in range(16):
                if r & bit:
                    continue
                a, d = v[r], v[r | bit]
                v[r] = jnp.where(clear, a, pltpu.roll(d, 8 * bit, 1))
                v[r | bit] = jnp.where(clear, pltpu.roll(a, 128 - 8 * bit, 1), d)
        for q in range(16):
            G2[f, pl.ds(pl.multiple_of(ix * 128 + q * 8, 8), 8), :] = v[q]

    def gathered(f, yl):
        rows = []
        for xl in range(4):
            rows.append(jnp.stack([G2[f, pl.ds((xl * 4 + zl) * 8 + yl, 8, stride=128), :] for zl in range(4)], 0))
        return jnp.stack(rows, 0)

    def edges(ref, ny):
        ref[0] = jnp.where(lane >= 32, roll(ref[ny], 32, -1), 0.0)
        ref[ny + 1] = jnp.where(lane < 96, roll(ref[1], -32, -1), 0.0)

    def around(v):
        xp = shifted(v, 0, 1, roll(v[:1], -1, -2))
        xm = shifted(v, 0, -1, roll(v[-1:], 1, -2))
        zp = shifted(v, 1, 1, roll(v[:, :1], -1, -1))
        zm = shifted(v, 1, -1, roll(v[:, -1:], 1, -1))
        return xp, xm, zp, zm

    z_top, z_end = lax.rem(lane, 32) == 31, lax.rem(lane, 32) == 0

    def inside(k):
        xp = shifted(k, 0, 1, jnp.where(row == 7, 0.0, roll(k[:1], -1, -2)))
        xm = shifted(k, 0, -1, jnp.where(row == 0, 0.0, roll(k[-1:], 1, -2)))
        zp = shifted(k, 1, 1, jnp.where(z_top, 0.0, roll(k[:, :1], -1, -1)))
        zm = shifted(k, 1, -1, jnp.where(z_end, 0.0, roll(k[:, -1:], 1, -1)))
        return xp, xm, zp, zm

    def coefs_low(level, K, A, S, I, ny):
        hw = 0.5 * 0.25 ** level
        edges(K, ny)
        def body(y, _):
            k = K[y + 1]
            near = inside(k) + (K[y + 2], K[y])
            c = [hw * (k + n) for n in near]
            d = ((c[0] + c[1]) + (c[2] + c[3])) + (c[4] + c[5])
            s = DAMPING / d
            S[y] = s
            if I is not None:
                I[y] = d * (1.0 / DAMPING)
            for m in range(6):
                A[m, y] = jnp.where(near[m] > 0, s * c[m], 0.0)
            return 0
        lax.fori_loop(0, ny // 2, times(2, body), 0)

    def fold(blocks):
        t = blocks[0] + blocks[1]
        t = t.reshape((t.shape[0] // 2, 2) + t.shape[1:])
        t = t[:, 0] + t[:, 1]
        t = t.reshape((t.shape[0], t.shape[1] // 2, 2) + t.shape[2:])
        return (t[:, :, 0] + t[:, :, 1]) * 0.125

    def load_k2():
        def body(y, _):
            K2[y + 1] = gathered(KF, y)
            return 0
        lax.fori_loop(0, 2, times(4, body), 0)
        coefs_low(2, K2, A2, S2, I2, 8)
        def body3(y, _):
            K3[y + 1] = fold([K2[2 * y + 1], K2[2 * y + 2]])
            return 0
        lax.fori_loop(0, 1, times(4, body3), 0)
        coefs_low(3, K3, A3, S3, I3, 4)
        for y in range(2):
            K4[y + 1] = fold([K3[2 * y + 1], K3[2 * y + 2]])
        coefs_low(4, K4, A4, S4, None, 2)

    def next2(y, cur, before, after):
        xp, xm, zp, zm = around(cur)
        t = 0.2 * cur + Q2[y]
        t = t + A2[0, y] * xp + A2[1, y] * xm
        t = t + A2[2, y] * zp + A2[3, y] * zm
        return t + (A2[4, y] * after + A2[5, y] * before)

    def sweeps2(count):
        def sweep(i, _):
            edges(V2, 8)
            before = V2[0]
            for y in range(8):
                cur = V2[y + 1]
                V2[y + 1] = next2(y, cur, before, V2[y + 2])
                before = cur
            return 0
        lax.fori_loop(0, count, sweep, 0)

    def next_whole(v, a, g, ny):
        first = roll(v[ny - 1], 32, -1)
        last = roll(v[0], -32, -1)
        out = []
        for y in range(ny):
            xp, xm, zp, zm = around(v[y])
            yp = v[y + 1] if y + 1 < ny else last
            ym = v[y - 1] if y else first
            t = (0.2 * v[y] + g(y)) + (a(0, y) * xp + a(1, y) * xm)
            out.append(t + ((a(2, y) * zp + a(3, y) * zm) + (a(4, y) * yp + a(5, y) * ym)))
        return out

    def a3(m, y):
        return A3[m, y]

    def g3(y):
        return Q3[y]

    def sweeps3(v, count):
        return lax.fori_loop(0, count, lambda i, w: tuple(next_whole(list(w), a3, g3, 4)), tuple(v))

    def lower_levels():
        v = sweeps3([Q3[y] for y in range(4)], 5)
        w = next_whole(list(v), a3, g3, 4)
        r = [(w[y] - v[y]) * I3[y] for y in range(4)]
        g4 = [fold(r[2 * y:2 * y + 2]) * S4[y] for y in range(2)]
        a4 = [[A4[m, y] for y in range(2)] for m in range(6)]
        c = lax.fori_loop(
            0, 15, lambda i, w: tuple(next_whole(list(w), lambda m, y: a4[m][y], lambda y: g4[y], 2)), tuple(g4))
        v = [v[y] + c[y // 2] for y in range(4)]
        return sweeps3(v, 6)

    loads[0].wait()
    permute_in(KF)
    pack0(KF)
    loads[1].wait()
    permute_in(BF)
    pack0(BF)
    pl.semaphore_wait(barrier, len(PEERS))
    k0 = copies0(KF)
    start(k0)
    b0 = copies0(BF)
    start(b0)

    restrict_k1()
    pack1(KF)
    pack_k2()
    k2 = copies_plane(KF)
    start(k2)

    wait_recv(k0)
    assemble0(KF, K0)
    coefs0()
    wait_recv(b0)
    k1 = copies1(KF)
    start(k1)
    assemble0(BF, B0)

    sweeps0(3, 5)
    restrict_b1()
    pack1(BF)
    b1 = copies1(BF)
    start(b1)

    wait_recv(k1)
    assemble1(KF, K1)
    k1f = copies_far(K1, 0)
    start(k1f)
    wait_recv(k2)
    spread(KF)
    k2l = copies_line(KF)
    start(k2l)
    def stage0(x, _):
        for j in range(6):
            T0[x, pl.ds(j, 8, stride=6), :] = jnp.where(
                lane < 64, V0[8 + x, 0, j], pltpu.roll(V0[8 + x, 1, j], 64, 1))
        D0[VF, 8 + x, 8:40, :] = T0[x, 8:40, :]
        return 0
    lax.fori_loop(0, 4, times(4, stage0), 0)
    pack0(VF)
    v0 = copies0(VF)
    start(v0)
    wait_recv(k1f)
    coefs1()

    wait_recv(b1)
    assemble1(BF, B1)

    def first_sweep1(x, _):
        V1[3 + x] = S1[3 + x] * B1[3 + x]
        return 0
    lax.fori_loop(0, 2, times(10, first_sweep1), 0)
    sweeps1(4, 18, 2)
    sweeps1(6, 14, 3)
    pack_b2()
    b2 = copies_plane(BF)
    start(b2)

    def stage1(i, _):
        for j in range(5):
            T2[i, pl.ds(j, 8, stride=5), :] = jnp.where(
                lane < 64, V1[9 + i, j], pltpu.roll(V1[13 + i, j], 64, 1))
        for t in range(2):
            D1[VF, 1, i, 16 + 8 * t:24 + 8 * t, :] = T2[i, pl.ds(12 + 8 * t, 8, stride=1), :]
        return 0
    lax.fori_loop(0, 1, times(4, stage1), 0)
    pack1(VF)
    k2o = copies_on(KF)
    pass_on(k2l, k2o)
    wait_recv(b2)
    spread(BF)
    b2l = copies_line(BF)
    start(b2l)

    v1 = copies1(VF)
    start(v1)
    k2l[3].wait_recv()
    wait_recv(k2o)
    load_k2()
    for made in (k0, b0, k1, b1, k1f, k2, b2, k2l, k2o):
        wait_send(made)
    wait_recv(v0)
    b2o = copies_on(BF)
    pass_on(b2l, b2o)
    assemble0(VF, W0)
    wait_send(v0)
    b2l[3].wait_recv()
    wait_recv(b2o)

    def load_b2(y, _):
        q = S2[y] * gathered(BF, y)
        Q2[y] = q
        V2[y + 1] = q
        return 0
    lax.fori_loop(0, 2, times(4, load_b2), 0)
    sweeps2(5)
    wait_recv(v1)
    assemble1(VF, W1)
    v1f = copies_far(W1, 1)
    start(v1f)

    edges(V2, 8)

    def restrict2(y, _):
        r = []
        for u in range(2):
            z = 2 * y + u
            cur = V2[z + 1]
            r.append((next2(z, cur, V2[z], V2[z + 2]) - cur) * I2[z])
        Q3[y] = fold(r) * S3[y]
        return 0
    lax.fori_loop(0, 2, times(2, restrict2), 0)
    v3 = lower_levels()
    for y in range(4):
        V3[y] = v3[y]

    def prolong2(y, _):
        for xl in range(4):
            for zl in range(4):
                V2[y + 1, xl, zl] = V2[y + 1, xl, zl] + V3[lax.div(y, 2), xl // 2, zl // 2]
        return 0
    lax.fori_loop(0, 2, times(4, prolong2), 0)
    sweeps2(6)

    def lay2(y, _):
        for xl in range(4):
            for zl in range(4):
                H2[pl.ds((xl * 4 + zl) * 8 + y, 8, stride=128), :] = V2[y + 1, xl, zl]
        return 0
    lax.fori_loop(0, 2, times(4, lay2), 0)
    planes = [(-2, 3)] + [(o, xl) for o in (-1, 0, 1) for xl in range(4)] + [(2, 0)]
    acc = None
    zf = jnp.where(ll < 96, ll, ll - 128)
    zc = lax.div(zf + 128, 2) - 64 + iz * 32
    for zl in range(4):
        left = []
        for o, xl in planes:
            at_x = jnp.clip(ix + o, 0, 7)
            left.append(H2[pl.ds(pl.multiple_of(at_x * 128 + (xl * 4 + zl) * 8, 8), 8), :])
        left = jnp.concatenate(left, axis=0)
        ok = (zc >= 0) & (zc < 128) & (lax.rem(zc + 128, 4) == zl)
        right = jnp.concatenate(
            [(ok & (cc == (iy + dy) * 32 + lax.div(zc, 4))).astype(F32) for dy in (-1, 0, 1)], axis=1)
        part = dot3(left, right.astype(jnp.bfloat16))
        acc = part if acc is None else acc + part
    for m in range(14):
        for d in range(3):
            v = acc[8 * m:8 * m + 8, 128 * d:128 * d + 128]
            F1[m, pl.ds(16 * d, 8, stride=2), :] = v
            F1[m, pl.ds(16 * d + 1, 8, stride=2), :] = v
    wait_recv(v1f)

    def start1(x, _):
        m = lax.div(x + 1, 2)
        for j in range(5):
            V1[x, j] = jnp.where(K1[x, j] > 0, W1[x, j] + F1[m, pl.ds(4 + j, 8, stride=5), :], 0.0)
        return 0
    lax.fori_loop(0, 2, times(13, start1), 0)
    sweeps1(1, 24, 3)
    sweeps1(4, 18, 3)

    def lay1(i, _):
        for j in range(5):
            F0[i, pl.ds(j, 8, stride=5), :] = V1[6 + i, j]
        return 0
    lax.fori_loop(0, 2, times(7, lay1), 0)

    def start0(i, _):
        for m in range(3):
            add = F0[i, pl.ds(8 + m, 8, stride=3), :]
            for u in range(2):
                x = 2 + 2 * i + u
                for p in range(2):
                    for o in range(2):
                        j = 2 * m + o
                        V0[x, p, j] = jnp.where(S0[x, p, j] > 0, W0[x, p, j] + add, 0.0)
        return 0
    lax.fori_loop(0, 2, times(7, start0), 0)
    sweeps0(3, 6)

    join = (ll == jnp.where(cc < 64, 2 * cc, 2 * (cc - 64) + 1)).astype(F32).astype(jnp.bfloat16)

    def finish(x, _):
        for j in range(6):
            T0[x, pl.ds(j, 8, stride=6), :] = jnp.where(
                lane < 64, V0[8 + x, 0, j], pltpu.roll(V0[8 + x, 1, j], 64, 1))
        return 0
    lax.fori_loop(0, 4, times(4, finish), 0)

    for i in range(4):
        d = T0[4 * i:4 * i + 4, 8:40, :].reshape(128, 128)
        out_ref[4 * i:4 * i + 4] = dot3(d, join).reshape(4, 32, 128)
    for made in (v1, v1f, b2l, b2o):
        wait_send(made)


def shards(source, conductivity):
    def vm(*shape):
        return pltpu.VMEM(shape, F32)

    def dma(n):
        return pltpu.SemaphoreType.DMA((n,))

    fine = (36, 2, 6, 8, 128)
    mid = (26, 5, 8, 128)
    low2, low3, low4 = (4, 4, 8, 128), (2, 2, 8, 128), (1, 1, 8, 128)
    scratch = [
        vm(2, 16, 32, 128), vm(3, 32, 48, 128), vm(3, 2, 32, 128), vm(3, 2, 4, 48, 128),
        vm(*fine), vm(*fine), vm(*fine), vm(36, 2, 8, 128), vm(*fine), vm(36, 6, 8, 128),
        vm(*fine), vm(*fine), vm(*fine), vm(*fine), vm(16, 48, 128),
        vm(3, 3, 4, 48, 128), vm(3, 2, 16, 128), vm(3, 2, 3, 2, 48, 128),
        vm(*mid), vm(*mid), vm(*mid), vm(26, 8, 128), vm(*mid), vm(*mid), vm(*mid), vm(*mid), vm(*mid), vm(*mid),
        vm(4, 32, 128), vm(4, 40, 128), vm(14, 40, 128), vm(14, 48, 128),
        vm(2, 8, 128), vm(2, 16, 8, 128), vm(2, 1024, 128), vm(1024, 128),
        vm(10, *low2), vm(10, *low2), vm(6, 8, *low2), vm(8, *low2), vm(8, *low2), vm(8, *low2),
        vm(6, *low3), vm(4, *low3), vm(6, 4, *low3), vm(4, *low3), vm(4, *low3), vm(4, *low3),
        vm(4, *low4), vm(6, 2, *low4), vm(2, *low4), vm(2, *low4),
        dma(2), dma(78), dma(78), dma(78), dma(78), dma(4), dma(4), dma(30), dma(30), dma(14), dma(14),
    ]
    return pl.pallas_call(
        kernel,
        out_shape=jax.ShapeDtypeStruct((16, 32, 128), F32),
        in_specs=[pl.BlockSpec(memory_space=pltpu.HBM)] * 2,
        out_specs=pl.BlockSpec(memory_space=pltpu.VMEM),
        scratch_shapes=scratch,
        compiler_params=pltpu.CompilerParams(
            collective_id=0, has_side_effects=True, vmem_limit_bytes=62 * 1024 * 1024),
    )(source, conductivity)


def solution(mesh):
    spec = P("gx", "gy", "gz")
    return jax.shard_map(shards, mesh=mesh, in_specs=(spec, spec), out_specs=spec, check_vma=False)
```
